32 devices in a mesh: section: 4 (over y, x), dp: 8 (over z, core).
Axes of the slice: x: 2, y: 2, z: 4, core: 2. Of those that a mesh axis runs over, the one named last changes fastest.
Arguments:
- aspp_input: bfloat16 [32, 24, 24, 2048], P('dp'), may hold values from -6 to 6
- low_input: bfloat16 [32, 96, 96, 256], P('dp', 'section'), may hold values from -6 to 6
- aspp_ids: int32 [32, 24, 24], P('dp'), may hold values from 0 to 1, as said below
- low_ids: int32 [32, 96, 96], P('dp'), may hold values from 0 to 1, as said below
- aspp_weight: bfloat16 [2048, 28, 256], P(None, None, 'section'), may hold values from -0.046875 to 0.046875
- pool_weight: bfloat16 [2048, 256], P(None, 'section'), may hold values from -0.125 to 0.125
- bn_gain: float32 [5, 256], P(None, 'section'), may hold values from 0.1 to 1.9
- bn_shift: float32 [5, 256], P(None, 'section'), may hold values from -3 to 3
- projection_matrix: bfloat16 [5, 256, 256], P(None, 'section'), may hold values from -0.15625 to 0.15625
- reduce_weight: bfloat16 [256, 48], replicated, may hold values from -0.375 to 0.375
- merge1_weight: bfloat16 [9, 304, 256], replicated, may hold values from -0.109375 to 0.109375
- merge2_weight: bfloat16 [9, 256, 256], replicated, may hold values from -0.125 to 0.125
- class_weight: bfloat16 [256, 21], replicated, may hold values from -0.375 to 0.375
- logit_grad: bfloat16 [32, 96, 96, 21], P('dp', 'section'), may hold values from -6 to 6
Outputs:
- logits: float32 [32, 96, 96, 21], P('dp', 'section')
- aspp_input_grad: float32 [32, 24, 24, 2048], P('dp', None, None, 'section')
- low_input_grad: float32 [32, 96, 96, 256], P('dp', 'section')
- aspp_weight_grad: float32 [2048, 28, 256], P(None, None, 'section')
- pool_weight_grad: float32 [2048, 256], P(None, 'section')
- bn_gain_grad: float32 [5, 256], P(None, 'section')
- bn_shift_grad: float32 [5, 256], P(None, 'section')
- proj_weight_grad: float32 [5, 256, 256], P(None, 'section')
- reduction_weight_gradient: float32 [256, 48], replicated
- merge1_weight_grad: float32 [9, 304, 256], replicated
- merge2_weight_grad: float32 [9, 256, 256], replicated
- class_weight_grad: float32 [256, 21], replicated
The draws below stay inside these ranges and needn't reach their ends.
Inputs may be any that keep to these rules, and one draw needn't show every extreme that they name: `aspp_ids`: each canvas holds one image (all 0) or two stacked bands of rows: 0 above a row between 6 and 17, 1 from that row down; some canvas holds one image and some two. low_ids at (row, column) equals aspp_ids at (row // 4, column // 4) of the same canvas.
All inputs are finite; a program needn't handle non-finite values.
Results may differ from the reference program's by a relative error of at most 0.02.
Values may be sent and summed in bfloat16 or wider, within the bound.
No kernel may reach another device: no remote copies, remote signals or barrier semaphores. Data moves between devices by JAX's collectives and lax.ppermute only.
A program may use at most 192 MiB of HBM per device.

```python
import jax
import jax.numpy as jnp
from jax import lax

IN_CH = 2048
ASPP_CH = 256
LOW_CH = 256
RED_CH = 48
MERGE_CH = 256
CLASSES = 21
TAPS = 28
IMAGES = 2
HA = 24
WA = 24
CAN_DEV = 4
HL = 96
WL = 96
CANVASES = 32
N_DP = 8


def band_layout(key):
    count_key, cut_key, pick_key = jax.random.split(key, 3)
    paired = jax.random.randint(count_key, (CANVASES,), 0, 2)
    single = jax.random.randint(pick_key, (), 0, CANVASES)
    canvas_index = jnp.arange(CANVASES, dtype=jnp.int32)
    paired = jnp.where(canvas_index == single, 0, paired)
    paired = jnp.where(canvas_index == (single + 1) % CANVASES, 1, paired)
    cut_row = jax.random.randint(cut_key, (CANVASES,), HA // 4, 3 * HA // 4)
    row_index = jnp.arange(HA, dtype=jnp.int32)
    return ((row_index[None, :] >= cut_row[:, None]) & (paired[:, None] == 1)).astype(jnp.int32)


def draw_aspp_ids(key, part):
    banding = band_layout(key)
    return jnp.broadcast_to(banding[:, :, None], (CANVASES, HA, WA)).astype(jnp.int32)


def draw_low_ids(key, part):
    banding = jnp.repeat(band_layout(key), 4, axis=1)
    return jnp.broadcast_to(banding[:, :, None], (CANVASES, HL, WL)).astype(jnp.int32)


def steps_of(rng, shape, pieces, least, largest):
    def one(position, shards_of):
        heights = jax.random.uniform(jax.random.fold_in(jax.random.fold_in(rng, 6), position), (shards_of,), jnp.float32, least / len(pieces), largest / len(pieces))
        return jnp.repeat(jnp.exp(heights), shape[position] // shards_of).reshape((-1,) + (1,) * (len(shape) - position - 1))

    level = one(*pieces[0])
    for cut in pieces[1:]:
        level = level * one(*cut)
    return level


def gaussian(key, shape, spread, reach, cuts=(), kind=jnp.bfloat16):
    values = spread * jax.random.normal(key, shape, jnp.float32)
    if cuts:
        values = values * steps_of(key, shape, cuts, -0.22, 0.18)
    return jnp.clip(values, -reach, reach).astype(kind)


def setup_inputs(seed: int = 0) -> dict:
    arg_keys = jax.random.split(jax.random.key(seed), 15)
    aspp_input = gaussian(arg_keys[0], (CANVASES, HA, WA, IN_CH), 1.0, 6.0, ((0, 8),))
    low_input = gaussian(arg_keys[1], (CANVASES, HL, WL, LOW_CH), 1.0, 6.0, ((0, 8), (1, 4)))
    aspp_ids = draw_aspp_ids(jax.random.fold_in(arg_keys[14], 71), 0)
    low_ids = draw_low_ids(jax.random.fold_in(arg_keys[14], 71), 0)
    aspp_weight = gaussian(arg_keys[4], (IN_CH, TAPS, ASPP_CH), (9 * IN_CH) ** -0.5, 0.046875, ((2, 4),))
    pool_weight = gaussian(arg_keys[5], (IN_CH, ASPP_CH), IN_CH ** -0.5, 0.125, ((1, 4),))
    bn_gain = jnp.clip(1.0 + 0.18 * jax.random.normal(arg_keys[6], (5, ASPP_CH), jnp.float32), 0.1, 1.9)
    bn_shift = gaussian(arg_keys[7], (5, ASPP_CH), 0.5, 3.0, ((1, 4),), jnp.float32)
    projection_matrix = gaussian(arg_keys[8], (5, ASPP_CH, ASPP_CH), (5 * ASPP_CH) ** -0.5, 0.15625, ((1, 4),))
    reduce_weight = gaussian(arg_keys[9], (LOW_CH, RED_CH), LOW_CH ** -0.5, 0.375)
    merge1_weight = gaussian(arg_keys[10], (9, ASPP_CH + RED_CH, MERGE_CH), (9 * (ASPP_CH + RED_CH)) ** -0.5, 0.109375)
    merge2_weight = gaussian(arg_keys[11], (9, MERGE_CH, MERGE_CH), (9 * MERGE_CH) ** -0.5, 0.125)
    class_weight = gaussian(arg_keys[12], (MERGE_CH, CLASSES), MERGE_CH ** -0.5, 0.375)
    logit_grad = gaussian(arg_keys[13], (CANVASES, HL, WL, CLASSES), 1.0, 6.0, ((0, 8), (1, 4)))
    return dict(aspp_input=aspp_input, low_input=low_input, aspp_ids=aspp_ids, low_ids=low_ids, aspp_weight=aspp_weight, pool_weight=pool_weight, bn_gain=bn_gain, bn_shift=bn_shift, projection_matrix=projection_matrix, reduce_weight=reduce_weight, merge1_weight=merge1_weight, merge2_weight=merge2_weight, class_weight=class_weight, logit_grad=logit_grad)


atrous_rates = (6, 12, 18)
highest_precision = lax.Precision.HIGHEST
epsilon = 1e-05

@jax.custom_vjp
def low(v):
    return lax.optimization_barrier(v.astype(jnp.bfloat16)).astype(jnp.float32)

@jax.custom_vjp
def low_level_gradient(v):
    return v

def low_keep(v):
    return (low(v), None)

def low_pass(kept, grad):
    return (grad,)

def back_keep(v):
    return (v, None)

def back_low(kept, grad):
    return (low(grad),)
low.defvjp(low_keep, low_pass)
low_level_gradient.defvjp(back_keep, back_low)

def tap_list():
    listed = [(0, 0, 0)]
    for branch_index, rate_value in enumerate(atrous_rates):
        for step_rows in (-1, 0, 1):
            for step_cols in (-1, 0, 1):
                listed.append((rate_value * step_rows, rate_value * step_cols, branch_index + 1))
    return listed

def moved(grid_values, step_rows, step_cols, fill_value):
    pad_rows = abs(step_rows)
    pad_cols = abs(step_cols)
    widths = ((pad_rows, pad_rows), (pad_cols, pad_cols)) + ((0, 0),) * (grid_values.ndim - 2)
    padded = jnp.pad(grid_values, widths, constant_values=fill_value)
    first_row = pad_rows + step_rows
    first_col = pad_cols + step_cols
    return padded[first_row:first_row + grid_values.shape[0], first_col:first_col + grid_values.shape[1]]

def upsample_matrix(coarse_count):
    fine_index = jnp.arange(4 * coarse_count, dtype=jnp.int32)
    coarse = fine_index // 4
    phase_index = fine_index % 4
    near_weight = jnp.where(phase_index < 2, 5.0 + 2.0 * phase_index, 11.0 - 2.0 * phase_index).astype(jnp.float32) / 8.0
    other_row = jnp.clip(jnp.where(phase_index < 2, coarse - 1, coarse + 1), 0, coarse_count - 1)
    columns = jnp.arange(coarse_count, dtype=jnp.int32)
    near_part = (columns[None, :] == coarse[:, None]).astype(jnp.float32) * near_weight[:, None]
    far_part = (columns[None, :] == other_row[:, None]).astype(jnp.float32) * (1.0 - near_weight)[:, None]
    return near_part + far_part

def aspp_canvas(image_grid, ident, aspp_weight):
    branch_sums = [jnp.zeros(image_grid.shape[:2] + (aspp_weight.shape[2],), jnp.float32) for branch in range(4)]
    for tap_index, (step_rows, step_cols, branch) in enumerate(tap_list()):
        same_image = (moved(ident, step_rows, step_cols, -1) == ident).astype(jnp.float32)
        product = jnp.einsum('hwc,cd->hwd', moved(image_grid, step_rows, step_cols, 0.0), aspp_weight[:, tap_index, :], precision=highest_precision)
        branch_sums[branch] = branch_sums[branch] + same_image[:, :, None] * low_level_gradient(product)
    return jnp.stack(branch_sums, axis=2)

def merging_conv(grid_values, ident, weights):
    result = jnp.zeros(grid_values.shape[:2] + (weights.shape[2],), jnp.float32)
    tap_index = 0
    for step_rows in (-1, 0, 1):
        for step_cols in (-1, 0, 1):
            same_image = (moved(ident, step_rows, step_cols, -1) == ident).astype(jnp.float32)
            product = jnp.einsum('hwc,cd->hwd', moved(grid_values, step_rows, step_cols, 0.0), weights[tap_index], precision=highest_precision)
            result = result + same_image[:, :, None] * product
            tap_index += 1
    return result

def decoder_canvas(upsampled, low_feat, ident, reduce_weight, merge1_weight, merge2_weight, class_weight):
    reduce_pre = jnp.einsum('hwc,cd->hwd', low_feat, reduce_weight, precision=highest_precision)
    reduced = low(jax.nn.silu(low_level_gradient(reduce_pre)))
    joined = jnp.concatenate([upsampled, reduced], axis=-1)
    first = low(jax.nn.silu(low_level_gradient(merging_conv(joined, ident, merge1_weight))))
    second = low(jax.nn.silu(low_level_gradient(merging_conv(first, ident, merge2_weight))))
    return jnp.einsum('hwc,cd->hwd', second, class_weight, precision=highest_precision)

def forward(aspp_input, low_input, aspp_ids, low_ids, aspp_weight, pool_weight, bn_gain, bn_shift, projection_matrix, reduce_weight, merge1_weight, merge2_weight, class_weight):
    conv_branches = lax.map(jax.checkpoint(lambda canvas_pair: aspp_canvas(canvas_pair[0], canvas_pair[1], aspp_weight)), (aspp_input, aspp_ids))
    onehot = (aspp_ids[..., None] == jnp.arange(IMAGES, dtype=jnp.int32)).astype(jnp.float32)
    counts = lax.optimization_barrier(jnp.sum(onehot, axis=(1, 2)))
    pooled_sum = jnp.einsum('nhwi,nhwc->nic', onehot, aspp_input, precision=highest_precision)
    pooled = low(pooled_sum / jnp.maximum(counts, 1.0)[:, :, None])
    pool_out = low_level_gradient(jnp.einsum('nic,cd->nid', pooled, pool_weight, precision=highest_precision))
    pool_branch = jnp.einsum('nhwi,nid->nhwd', onehot, pool_out, precision=highest_precision)
    branches = jnp.concatenate([conv_branches, pool_branch[:, :, :, None, :]], axis=3)
    grouped = branches.reshape((N_DP, CAN_DEV) + branches.shape[1:])
    mean_value = lax.optimization_barrier(jnp.mean(grouped, axis=(0, 2, 3), keepdims=True))
    square_mean = lax.optimization_barrier(jnp.mean(grouped * grouped, axis=(0, 2, 3), keepdims=True))
    scaled = (grouped - mean_value) * lax.rsqrt(square_mean - mean_value * mean_value + epsilon)
    active_mask_rows = low(jax.nn.silu(scaled * bn_gain + bn_shift)).reshape(branches.shape)
    projected_output = low_level_gradient(jnp.einsum('xfgcy,cys->xfgs', active_mask_rows, projection_matrix, precision=highest_precision))
    row_matrix = upsample_matrix(HA)
    col_matrix = upsample_matrix(WA)
    along_rows = jnp.einsum('ia,nabd->nibd', row_matrix, projected_output, precision=highest_precision)
    upsampled = low(jnp.einsum('jb,nibd->nijd', col_matrix, along_rows, precision=highest_precision))
    decoder = jax.checkpoint(lambda canvas_trio: decoder_canvas(canvas_trio[0], canvas_trio[1], canvas_trio[2], reduce_weight, merge1_weight, merge2_weight, class_weight))
    return lax.map(decoder, (upsampled, low_input, low_ids))

def reference(aspp_input, low_input, aspp_ids, low_ids, aspp_weight, pool_weight, bn_gain, bn_shift, projection_matrix, reduce_weight, merge1_weight, merge2_weight, class_weight, logit_grad):
    floats = tuple((item.astype(jnp.float32) for item in (aspp_input, low_input, aspp_weight, pool_weight, bn_gain, bn_shift, projection_matrix, reduce_weight, merge1_weight, merge2_weight, class_weight)))

    def wrapped(aspp_feat, low_feat, aspp_w, pool_w, gain_w, shift_w, proj_w, reduce_w, merge1_w, merge2_w, class_w):
        return forward(aspp_feat, low_feat, aspp_ids, low_ids, aspp_w, pool_w, gain_w, shift_w, proj_w, reduce_w, merge1_w, merge2_w, class_w)
    logits, pullback = jax.vjp(wrapped, *floats)
    grads = pullback(logit_grad.astype(jnp.float32))
    return (logits, grads[0], grads[1], grads[2], grads[3], grads[4], grads[5], grads[6], grads[7], grads[8], grads[9], grads[10])
```

```python
import jax
import jax.numpy as jnp
from jax import lax
from jax.experimental import pallas as pl
from jax.experimental.pallas import tpu as pltpu
from jax.sharding import PartitionSpec as P

IMAGES = 2
bf16 = jnp.bfloat16
f32 = jnp.float32
HALO = 4
LANE = 128


def upsample_matrix(coarse_count):
    fine_index = jnp.arange(4 * coarse_count, dtype=jnp.int32)
    coarse = fine_index // 4
    phase_index = fine_index % 4
    near_weight = (
        jnp.where(phase_index < 2, 5.0 + 2.0 * phase_index, 11.0 - 2.0 * phase_index).astype(f32)
        / 8.0
    )
    other_row = jnp.clip(jnp.where(phase_index < 2, coarse - 1, coarse + 1), 0, coarse_count - 1)
    columns = jnp.arange(coarse_count, dtype=jnp.int32)
    near_part = (columns[None, :] == coarse[:, None]).astype(f32) * near_weight[:, None]
    far_part = (columns[None, :] == other_row[:, None]).astype(f32) * (1.0 - near_weight)[:, None]
    return near_part + far_part


def split_rows(first, stop, target):
    count = stop - first
    pieces = -(-count // target)
    edges = [first + (count * k) // pieces for k in range(pieces + 1)]
    return [(edges[k], edges[k + 1] - edges[k]) for k in range(pieces)]


def silu_and_slope(v):
    s = 0.5 + 0.5 * jnp.tanh(0.5 * v)
    a = v * s
    return a, s * (1.0 + v - a)


def row_tables(ids_rows, section_index, own_rows, coarse_rows):
    fine_total = ids_rows.shape[1]
    window = own_rows + 2 * HALO
    slots = window + 1
    first = section_index * own_rows - HALO
    cut = jnp.sum((ids_rows == 0).astype(jnp.int32), axis=1)[:, None] - first
    gap = jnp.where((cut >= 1) & (cut < window), cut, window)
    slot = jnp.arange(slots, dtype=jnp.int32)[None, :]
    src = slot - (slot > gap).astype(jnp.int32)
    row = src + first
    valid = (slot != gap) & (row >= 0) & (row < fine_total)
    own = valid & (src >= HALO) & (src < own_rows + HALO)
    coarse = row // 4
    phase = row % 4
    near_weight = jnp.where(phase < 2, 5 + 2 * phase, 11 - 2 * phase).astype(f32) / 8.0
    far = jnp.clip(jnp.where(phase < 2, coarse - 1, coarse + 1), 0, coarse_rows - 1)
    base = section_index * (own_rows // 4) - 2
    held = own_rows // 4 + 4
    near_at = jnp.clip(coarse - base, 0, held - 1)
    far_at = jnp.clip(far - base, 0, held - 1)
    validf = valid.astype(f32)
    ownf = own.astype(f32)
    own_at = jnp.where(own, src - HALO, own_rows)
    slot_of = slot + (slot >= gap).astype(jnp.int32)
    inside = ((slot + first >= 0) & (slot + first < fine_total)).astype(f32)
    inside = jnp.broadcast_to(inside, validf.shape)
    ints = jnp.stack(
        [jnp.clip(src, 0, window - 1), near_at, far_at, own_at, slot_of, jnp.broadcast_to(gap, src.shape)], axis=1
    )
    floats = jnp.stack(
        [
            validf,
            ownf,
            near_weight * validf,
            (1.0 - near_weight) * validf,
            near_weight * ownf,
            (1.0 - near_weight) * ownf,
            inside,
        ],
        axis=1,
    )
    return ints.astype(jnp.int32), floats


def column_sides(v):
    n = v.shape[0]
    col = lax.broadcasted_iota(jnp.int32, v.shape, 0)
    left = jnp.where(col == 0, 0.0, pltpu.roll(v, 1, 0))
    right = jnp.where(col == n - 1, 0.0, pltpu.roll(v, n - 1, 0))
    return left, right


def three_columns(v):
    left, right = column_sides(v)
    return jnp.concatenate([left.astype(bf16), v.astype(bf16), right.astype(bf16)], axis=1)


def decode_kernel(own_rows, cols, chans, red, itab, ftab, low_top, low, low_end, proj, tgt, colm, colt, rw3, w1, w2, clsb, wb2, wb1u, wb1r,
                  up_o, red_o, fst_o, sec_o, g2_o, g1_o, rg_o, pg_o,
                  jc, fc, gc2, gc1, sl1, rs, tgg, lift, drop, a0, a1, b0, b1, sems):
    m = pl.program_id(0)
    window = own_rows + 2 * HALO
    slots = window + 1
    held = proj.shape[1]
    wide = 3 * chans
    redw = jc.shape[2] - wide

    def it(k, j):
        return itab[m, k * slots + j]

    def ft(k, j):
        return ftab[m, k * slots + j]

    accs = (a0, a1)
    bccs = (b0, b1)

    def staged(blocks, multiply, finish):
        for k, block in enumerate(blocks):
            multiply(*block, accs[k % 2], bccs[k % 2])
            if k:
                finish(*blocks[k - 1], accs[(k - 1) % 2], bccs[(k - 1) % 2])
        k = len(blocks) - 1
        finish(*blocks[k], accs[k % 2], bccs[k % 2])

    def rows_of(ref, lo, n):
        return ref[lo:lo + n].reshape(n * cols, ref.shape[2])

    def dot(a, b):
        return jnp.dot(a, b, preferred_element_type=f32)

    for j in range(2, slots - 2):
        tgg[j] = tgt[0, jnp.clip(it(0, j) - 2, 0, own_rows + 3)]

    lane = lax.broadcasted_iota(jnp.int32, (cols, redw), 1)

    def reduce_mul(ref, lo, n, place, acc, _):
        acc[0:n * cols] = dot(ref[0, lo:lo + n].reshape(n * cols, ref.shape[3]), rw3[...])

    def reduce_fin(ref, lo, n, place, acc, _):
        for r in range(n):
            a, slope = silu_and_slope(acc[r * cols:(r + 1) * cols])
            a = a * ft(6, place + r)
            left, right = column_sides(a)
            a = jnp.where(lane < red, left, jnp.where(lane < 2 * red, a, right))
            jc[it(4, place + r), :, wide:] = a.astype(bf16)
            if HALO <= place + r < own_rows + HALO:
                rs[place + r - HALO] = slope.astype(bf16)

    staged(
        [(low_top, 0, HALO, 0)]
        + [(low, lo, n, lo + HALO) for lo, n in split_rows(0, own_rows, 8)]
        + [(low_end, 0, HALO, own_rows + HALO)],
        reduce_mul, reduce_fin,
    )
    jc[it(5, 0), :, wide:] = jnp.zeros((cols, redw), bf16)

    for k in range(held):
        lift[k] = dot(colm[...], proj[0, k])
    for j in range(slots):
        v = (ft(2, j) * lift[it(1, j)] + ft(3, j) * lift[it(2, j)]).astype(bf16)
        for d in range(3):
            jc[j, :, d * chans:(d + 1) * chans] = v[d * cols:(d + 1) * cols]

    keep = own_rows + 3
    up_copy = pltpu.make_async_copy(jc.at[3:3 + keep, :, chans:2 * chans], up_o.at[m], sems.at[0])
    red_copy = pltpu.make_async_copy(jc.at[3:3 + keep, :, wide:], red_o.at[m], sems.at[1])
    up_copy.start()
    red_copy.start()

    def first_mul(lo, n, acc, _):
        acc[0:n * cols] = (
            dot(rows_of(jc, lo - 1, n), w1[0]) + dot(rows_of(jc, lo, n), w1[1]) + dot(rows_of(jc, lo + 1, n), w1[2])
        )

    def first_fin(lo, n, acc, _):
        for r in range(n):
            a, slope = silu_and_slope(acc[r * cols:(r + 1) * cols])
            keep_row = ft(0, lo + r)
            fc[lo + r] = three_columns(a * keep_row)
            sl1[lo + r] = (slope * keep_row).astype(bf16)

    staged(split_rows(1, slots - 1, 8), first_mul, first_fin)
    fst_copy = pltpu.make_async_copy(fc.at[3:3 + keep, :, chans:2 * chans], fst_o.at[m], sems.at[2])
    fst_copy.start()

    def second_mul(lo, n, acc, bcc):
        acc[0:n * cols] = (
            dot(rows_of(fc, lo - 1, n), w2[0]) + dot(rows_of(fc, lo, n), w2[1]) + dot(rows_of(fc, lo + 1, n), w2[2])
        )
        bcc[0:n * cols] = dot(rows_of(tgg, lo, n), clsb[...])

    def second_fin(lo, n, acc, bcc):
        for r in range(n):
            j = lo + r
            a, slope = silu_and_slope(acc[r * cols:(r + 1) * cols])
            sec_o[0, it(3, j)] = a.astype(bf16)
            g = bcc[r * cols:(r + 1) * cols] * slope * ft(0, j)
            gc2[j] = three_columns(g)
            if HALO <= j <= own_rows + HALO:
                g2_o[0, j - HALO] = (g * ft(1, j)).astype(bf16)

    staged(split_rows(2, slots - 2, 8), second_mul, second_fin)

    def back2_mul(lo, n, acc, _):
        acc[0:n * cols] = (
            dot(rows_of(gc2, lo - 1, n), wb2[0]) + dot(rows_of(gc2, lo, n), wb2[1]) + dot(rows_of(gc2, lo + 1, n), wb2[2])
        )

    def back2_fin(lo, n, acc, _):
        for r in range(n):
            j = lo + r
            g = acc[r * cols:(r + 1) * cols] * sl1[j].astype(f32)
            gc1[j] = three_columns(g)
            if HALO <= j <= own_rows + HALO:
                g1_o[0, j - HALO] = (g * ft(1, j)).astype(bf16)

    staged(split_rows(3, slots - 3, 8), back2_mul, back2_fin)

    drop[...] = jnp.zeros(drop.shape, f32)

    def back1_mul(lo, n, acc, bcc):
        acc[0:n * cols] = (
            dot(rows_of(gc1, lo - 1, n), wb1u[0]) + dot(rows_of(gc1, lo, n), wb1u[1]) + dot(rows_of(gc1, lo + 1, n), wb1u[2])
        )
        mid = slice(chans, 2 * chans)
        bcc[0:n * cols] = (
            dot(rows_of(gc1, lo - 1, n)[:, mid], wb1r[0]) + dot(rows_of(gc1, lo, n)[:, mid], wb1r[1])
            + dot(rows_of(gc1, lo + 1, n)[:, mid], wb1r[2])
        )

    def back1_fin(lo, n, acc, bcc):
        for r in range(n):
            j = lo + r
            up = acc[r * cols:(r + 1) * cols]
            near, far = it(1, j), it(2, j)
            drop[near] += ft(4, j) * up
            drop[far] += ft(5, j) * up
            t = bcc[r * cols:(r + 1) * cols]
            left, right = column_sides(t)
            t = jnp.where(lane < red, right, jnp.where(lane < 2 * red, t, left))
            rg_o[0, it(3, j)] = (t * rs[it(3, j)].astype(f32)).astype(bf16)

    staged(split_rows(HALO, slots - HALO, 8), back1_mul, back1_fin)

    for k in range(held):
        pg_o[0, k] = dot(colt[...], drop[k].astype(bf16)).astype(bf16)
    up_copy.wait()
    red_copy.wait()
    fst_copy.wait()


def grads_kernel(own_rows, cols, chans, red, up, red3, fst, sec, g2, g1, rg, low, tgt, clst, rb3,
                 o1, o2, oc, orr, lowgrad, logits, upc, fcc):
    m = pl.program_id(0)
    keep = own_rows + 3
    wide = 3 * chans
    span = own_rows + 1

    @pl.when(m == 0)
    def _():
        o1[...] = jnp.zeros(o1.shape, f32)
        o2[...] = jnp.zeros(o2.shape, f32)
        oc[...] = jnp.zeros(oc.shape, f32)
        orr[...] = jnp.zeros(orr.shape, f32)

    def tdot(a, b):
        return lax.dot_general(a, b, (((0,), (0,)), ((), ())), preferred_element_type=f32)

    for j in range(keep):
        upc[j] = three_columns(up[0, j].astype(f32))
    for j in range(keep):
        fcc[j] = three_columns(fst[0, j].astype(f32))

    def flat(v):
        return v.reshape(v.shape[0] * cols, v.shape[2])

    gg1 = flat(g1[0])
    for dy in range(3):
        o1[dy, 0:wide] += tdot(flat(upc[dy:dy + span]), gg1)
        o1[dy, wide:] += tdot(flat(red3[0, dy:dy + span]), gg1)
    gg2 = flat(g2[0])
    for dy in range(3):
        o2[dy] += tdot(flat(fcc[dy:dy + span]), gg2)
    second = flat(sec[0])
    oc[...] += tdot(second, flat(tgt[0, 2:2 + own_rows]))
    rgv = flat(rg[0])
    orr[...] += tdot(flat(low[0]), rgv)
    for r in range(own_rows):
        lowgrad[0, r] = jnp.dot(rg[0, r], rb3[...], preferred_element_type=f32)
        lt = lax.dot_general(clst[...], sec[0, r], (((1,), (1,)), ((), ())), preferred_element_type=f32)
        logits[0, :, r] = lt[0:logits.shape[1]]


def decode(ids_rows, section_index, low_top, low_input, low_end, proj_ext, tgt_ext, reduce_weight, merge1_weight, merge2_weight, class_weight, coarse_rows):
    batch, own_rows, cols, low_ch = low_input.shape
    window = own_rows + 2 * HALO
    slots = window + 1
    chans = merge2_weight.shape[1]
    red = reduce_weight.shape[1]
    held = proj_ext.shape[1]
    coarse_cols = proj_ext.shape[2]
    redw = -(-3 * red // LANE) * LANE
    wide = 3 * chans
    classes = class_weight.shape[1]
    ints, floats = row_tables(ids_rows, section_index, own_rows, coarse_rows)
    ints = ints.reshape(batch, -1)
    floats = floats.reshape(batch, -1)
    colm = upsample_matrix(coarse_cols)
    zero = jnp.zeros((1, coarse_cols), f32)
    colm3 = jnp.concatenate([zero, colm[:-1], colm, colm[1:], zero], axis=0).astype(bf16)
    colt = colm.T.astype(bf16)
    rw3 = jnp.pad(jnp.concatenate([reduce_weight] * 3, axis=1), ((0, 0), (0, redw - 3 * red)))
    rb3 = rw3.T
    m1 = merge1_weight.reshape(3, 3, chans + red, chans)
    w1 = jnp.concatenate(
        [m1[:, :, :chans].reshape(3, wide, chans), m1[:, :, chans:].reshape(3, 3 * red, chans),
         jnp.zeros((3, redw - 3 * red, chans), bf16)], axis=1)
    w2 = merge2_weight.reshape(3, wide, chans)
    clsb = jnp.pad(class_weight.T, ((0, LANE - classes), (0, 0)))
    wb2 = jnp.transpose(merge2_weight[::-1], (0, 2, 1)).reshape(3, wide, chans)
    m1t = jnp.transpose(merge1_weight, (0, 2, 1))
    wb1u = m1t[::-1, :, :chans].reshape(3, wide, chans)
    wb1r = jnp.transpose(m1t[:, :, chans:].reshape(3, 3, chans, red)[::-1], (0, 2, 1, 3)).reshape(3, chans, 3 * red)
    wb1r = jnp.pad(wb1r, ((0, 0), (0, 0), (0, redw - 3 * red)))
    keep = own_rows + 3

    def whole(a):
        return pl.BlockSpec(a.shape, lambda m: (0,) * a.ndim, pipeline_mode=pl.Buffered(1))

    def per(shape):
        return pl.BlockSpec((1,) + shape, lambda m: (m,) + (0,) * len(shape))

    smem = pl.BlockSpec(memory_space=pltpu.SMEM)
    hbm = pl.BlockSpec(memory_space=pl.ANY)
    most = max(n for lo, hi in ((0, slots), (1, slots - 1), (2, slots - 2), (3, slots - 3), (4, slots - 4)) for _, n in split_rows(lo, hi, 8))
    consts = (colm3, colt, rw3, w1, w2, clsb, wb2, wb1u, wb1r)
    shapes = [((keep, cols, chans), hbm), ((keep, cols, redw), hbm), ((keep, cols, chans), hbm),
              ((own_rows + 1, cols, chans), None), ((own_rows + 1, cols, chans), None), ((own_rows + 1, cols, chans), None),
              ((own_rows + 1, cols, redw), None), ((held, coarse_cols, chans), None)]
    saved = pl.pallas_call(
        lambda *refs: decode_kernel(own_rows, cols, chans, red, *refs),
        grid=(batch,),
        in_specs=[smem, smem] + [per(a.shape[1:]) for a in (low_top, low_input, low_end)] + [per((held, coarse_cols, chans)), per(tgt_ext.shape[1:])] + [whole(a) for a in consts],
        out_specs=[s or per(sh) for sh, s in shapes],
        out_shape=[jax.ShapeDtypeStruct((batch,) + sh, bf16) for sh, _ in shapes],
        scratch_shapes=[
            pltpu.VMEM((slots, cols, wide + redw), bf16), pltpu.VMEM((slots, cols, wide), bf16),
            pltpu.VMEM((slots, cols, wide), bf16), pltpu.VMEM((slots, cols, wide), bf16),
            pltpu.VMEM((slots, cols, chans), bf16), pltpu.VMEM((own_rows + 1, cols, redw), bf16),
            pltpu.VMEM((slots, cols, LANE), bf16),
            pltpu.VMEM((held, 3 * cols, chans), f32), pltpu.VMEM((held, cols, chans), f32),
            pltpu.VMEM((most * cols, chans), f32), pltpu.VMEM((most * cols, chans), f32),
            pltpu.VMEM((most * cols, chans), f32), pltpu.VMEM((most * cols, chans), f32),
            pltpu.SemaphoreType.DMA((3,)),
        ],
        compiler_params=pltpu.CompilerParams(vmem_limit_bytes=63 * 2 ** 20),
        name="decode",
    )(ints, floats, low_top, low_input, low_end, proj_ext, tgt_ext, *consts)
    up, red3, fst, sec, g2, g1, rg, pg = saved
    return pg, (up, red3, fst, sec, g2, g1, rg)


def decode_grads(saved, low_input, tgt_ext, reduce_weight, class_weight):
    up, red3, fst, sec, g2, g1, rg = saved
    batch, own_rows, cols, low_ch = low_input.shape
    chans = up.shape[3]
    redw = red3.shape[3]
    red = reduce_weight.shape[1]
    classes = class_weight.shape[1]
    wide = 3 * chans
    keep = own_rows + 3
    rb3 = jnp.pad(jnp.concatenate([reduce_weight] * 3, axis=1), ((0, 0), (0, redw - 3 * red))).T
    clst = jnp.pad(class_weight.T, ((0, 32 - classes), (0, 0)))

    def whole(a):
        return pl.BlockSpec(a.shape, lambda m: (0,) * a.ndim, pipeline_mode=pl.Buffered(1))

    def per(shape):
        return pl.BlockSpec((1,) + shape, lambda m: (m,) + (0,) * len(shape))

    def total(shape):
        return pl.BlockSpec(shape, lambda m: (0,) * len(shape))

    tots = [(3, wide + redw, chans), (3, wide, chans), (chans, LANE), (low_ch, redw)]
    pers = [(own_rows, cols, low_ch), (classes, own_rows, cols)]
    o1, o2, oc, orr, lowgrad, logits = pl.pallas_call(
        lambda *refs: grads_kernel(own_rows, cols, chans, red, *refs),
        grid=(batch,),
        in_specs=[per((keep, cols, chans)), per((keep, cols, redw)), per((keep, cols, chans)), per((own_rows, cols, chans)),
                  per((own_rows + 1, cols, chans)), per((own_rows + 1, cols, chans)), per((own_rows, cols, redw)),
                  per((own_rows, cols, low_ch)), per(tgt_ext.shape[1:]), whole(clst), whole(rb3)],
        out_specs=[total(s) for s in tots] + [per(s) for s in pers],
        out_shape=[jax.ShapeDtypeStruct(s, f32) for s in tots] + [jax.ShapeDtypeStruct((batch,) + s, f32) for s in pers],
        scratch_shapes=[pltpu.VMEM((keep, cols, wide), bf16), pltpu.VMEM((keep, cols, wide), bf16)],
        compiler_params=pltpu.CompilerParams(vmem_limit_bytes=63 * 2 ** 20),
        name="decode_grads",
    )(up, red3, fst, sec, g2, g1, rg, low_input, tgt_ext, clst, rb3)
    return o1, o2, oc[:, :classes], orr, lowgrad, jnp.transpose(logits, (0, 2, 3, 1))


def unpack_decoder(o1, o2, orr, chans, red):
    wide = 3 * chans
    m1 = jnp.concatenate([o1[:, :wide].reshape(9, chans, chans), o1[:, wide:wide + 3 * red].reshape(9, red, chans)], axis=1)
    m2 = o2.reshape(9, chans, chans)
    rw = orr[:, :red] + orr[:, red:2 * red] + orr[:, 2 * red:3 * red]
    return m1, m2, rw
atrous_rates = (6, 12, 18)
epsilon = 1e-05


def tap_list():
    listed = [(0, 0, 0)]
    for branch_index, rate_value in enumerate(atrous_rates):
        for step_rows in (-1, 0, 1):
            for step_cols in (-1, 0, 1):
                listed.append((rate_value * step_rows, rate_value * step_cols, branch_index + 1))
    return listed


def pixel_tables(cut, height, width):
    batch = cut.shape[0]
    pixel = jnp.arange(height * width, dtype=jnp.int32)
    row, col = (pixel // width)[None], (pixel % width)[None]
    band = row >= cut[:, None]
    taps = tap_list()
    dr = jnp.array([t[0] for t in taps], jnp.int32)[:, None, None]
    dc = jnp.array([t[1] for t in taps], jnp.int32)[:, None, None]
    to_row, to_col = row[None] + dr, col[None] + dc
    inside = (to_row >= 0) & (to_row < height) & (to_col >= 0) & (to_col < width)
    valid = inside & ((to_row >= cut[None, :, None]) == band[None])
    valid = valid.astype(f32).reshape(len(taps), batch * height * width)
    index = jnp.arange(IMAGES * batch, dtype=jnp.int32)[:, None, None]
    member = (index // IMAGES == jnp.arange(batch)[None, :, None]) & (index % IMAGES == band[None].astype(jnp.int32))
    return valid, member.astype(bf16).reshape(IMAGES * batch, batch * height * width), band.astype(f32)


def branch_kernel(shifts, batch, x, w, valid, member, cnt, pw, band, br_o, mom_o, pooled_o, y, pool):
    i = pl.program_id(0)
    block = x.shape[0]
    pixels = y.shape[1] // batch
    own = pw.shape[0]
    at = pl.multiple_of(i * block, block)

    @pl.when(i == 0)
    def _():
        pool[...] = jnp.zeros(pool.shape, f32)

    xv = x[...]
    y[:, pl.ds(at, block)] = lax.dot_general(w[...], xv, (((1,), (1,)), ((), ())), preferred_element_type=f32)
    pool[...] += jnp.dot(member[...], xv, preferred_element_type=f32)

    def keep(m, b, v):
        br_o[m, b * own:(b + 1) * own] = v
        mom_o[m, b * own:(b + 1) * own, 0:1] = jnp.sum(v, axis=1, keepdims=True)
        mom_o[m, b * own:(b + 1) * own, 1:2] = jnp.sum(v * v, axis=1, keepdims=True)

    @pl.when(i == pl.num_programs(0) - 1)
    def _():
        total = y.shape[1]
        for b in range(4):
            acc = None
            for t, (shift, branch) in enumerate(shifts):
                if branch != b:
                    continue
                v = y[t * own:(t + 1) * own]
                if shift:
                    v = pltpu.roll(v, (-shift) % total, 1) * valid[t:t + 1]
                acc = v if acc is None else acc + v
            for m in range(batch):
                keep(m, b, acc[:, m * pixels:(m + 1) * pixels])
        pooled = (pool[...] / cnt[...]).astype(bf16)
        pooled_o[...] = pooled
        po = lax.dot_general(pw[...], pooled, (((1,), (1,)), ((), ())), preferred_element_type=f32)
        for m in range(batch):
            v = jnp.where(band[m:m + 1] > 0.5, po[:, IMAGES * m + 1:IMAGES * m + 2], po[:, IMAGES * m:IMAGES * m + 1])
            keep(m, 4, v)


def aspp_forward(x, wt, pwt, valid, member, counts, band):
    total, in_chans = x.shape
    batch, pixels = band.shape
    own = pwt.shape[0]
    taps = tap_list()
    width = int(round(pixels ** 0.5))
    shifts = [(dr * width + dc, b) for dr, dc, b in taps]
    block = total // 3 if total % 3 == 0 and (total // 3) % LANE == 0 else total
    cnt = counts.reshape(-1, 1)

    def whole(a):
        return pl.BlockSpec(a.shape, lambda i: (0,) * a.ndim, pipeline_mode=pl.Buffered(1))

    def full(shape):
        return pl.BlockSpec(shape, lambda i: (0,) * len(shape))

    outs = [((batch, 5 * own, pixels), f32), ((batch, 5 * own, 2), f32), ((IMAGES * batch, in_chans), bf16)]
    return pl.pallas_call(
        lambda *refs: branch_kernel(shifts, batch, *refs),
        grid=(total // block,),
        in_specs=[pl.BlockSpec((block, in_chans), lambda i: (i, 0)), whole(wt), whole(valid),
                  pl.BlockSpec((IMAGES * batch, block), lambda i: (0, i)), whole(cnt), whole(pwt), whole(band)],
        out_specs=[full(s) for s, _ in outs],
        out_shape=[jax.ShapeDtypeStruct(s, d) for s, d in outs],
        scratch_shapes=[pltpu.VMEM((len(taps) * own, total), f32), pltpu.VMEM((IMAGES * batch, in_chans), f32)],
        compiler_params=pltpu.CompilerParams(vmem_limit_bytes=63 * 2 ** 20),
        name="aspp_forward",
    )(x, wt, valid, member, cnt, pwt, band)


def weight_grad_kernel(shifts, batch, x, bg, valid, pooled, pg, proj, wg_o, tg_o, both):
    i = pl.program_id(0)
    own = pg.shape[0]
    pixels = bg.shape[2]
    total = tg_o.shape[1]
    rows = tg_o.shape[0]

    @pl.when(i == 0)
    def _():
        for m in range(batch):
            both[:, m * pixels:(m + 1) * pixels] = bg[m]
        for t, (shift, b) in enumerate(shifts):
            v = both[b * own:(b + 1) * own]
            if shift:
                v = pltpu.roll(v * valid[t:t + 1], shift % total, 1)
            tg_o[t * own:(t + 1) * own] = v.astype(bf16)

    wg_o[0:rows] = jnp.dot(tg_o[...], x[...], preferred_element_type=f32).astype(bf16)
    wg_o[rows:rows + own] = jnp.dot(pg[...], pooled[...], preferred_element_type=f32).astype(bf16)
    wg_o[rows + own:] = proj[...].astype(bf16)


def aspp_weight_grads(x, bg, valid, pooled, pool_grad, proj_grad):
    total, in_chans = x.shape
    batch, four, pixels = bg.shape
    own = pool_grad.shape[0]
    taps = tap_list()
    width = int(round(pixels ** 0.5))
    shifts = [(dr * width + dc, b) for dr, dc, b in taps]
    block = 512 if in_chans % 512 == 0 else in_chans
    rows = len(taps) * own
    more = proj_grad.shape[0]

    def whole(a):
        return pl.BlockSpec(a.shape, lambda i: (0,) * a.ndim, pipeline_mode=pl.Buffered(1))

    def lanes(a):
        return pl.BlockSpec((a.shape[0], block), lambda i: (0, i))

    outs = [(rows + own + more, in_chans), (rows, total)]
    return pl.pallas_call(
        lambda *refs: weight_grad_kernel(shifts, batch, *refs),
        grid=(in_chans // block,),
        in_specs=[lanes(x), whole(bg), whole(valid), lanes(pooled), whole(pool_grad), lanes(proj_grad)],
        out_specs=[pl.BlockSpec((rows + own + more, block), lambda i: (0, i)), pl.BlockSpec((rows, total), lambda i: (0, 0))],
        out_shape=[jax.ShapeDtypeStruct(s, bf16) for s in outs],
        scratch_shapes=[pltpu.VMEM((four, total), f32)],
        compiler_params=pltpu.CompilerParams(vmem_limit_bytes=63 * 2 ** 20),
        name="aspp_weight_grads",
    )(x, bg, valid, pooled, pool_grad, proj_grad)


def input_grad_kernel(at, tg, w, low_image, high_image, band, o):
    v = lax.dot_general(tg[...], w[...], (((0,), (0,)), ((), ())), preferred_element_type=f32)
    b = band[...]
    o[...] = (v + jnp.where(b > 0.5, high_image[0], low_image[0])).astype(bf16)


def aspp_input_grad(place, tg, wt, image_grads, band_column, parts):
    rows, total = tg.shape
    in_chans = wt.shape[1]
    batch = image_grads.shape[0] // IMAGES
    pixels = total // batch
    block = in_chans // parts
    low_image = image_grads[0::IMAGES][:, None]
    high_image = image_grads[1::IMAGES][:, None]
    span = 2 if (2 * pixels) % LANE == 0 and batch % 2 == 0 else batch
    grid = batch // span

    def pad_rows(v):
        return jnp.repeat(v, 1, axis=0)

    def body(at, tg, w, lo, hi, band, o):
        v = lax.dot_general(tg[...], w[...], (((0,), (0,)), ((), ())), preferred_element_type=f32)
        for k in range(span):
            b = band[k * pixels:(k + 1) * pixels]
            o[k * pixels:(k + 1) * pixels] = (v[k * pixels:(k + 1) * pixels] + jnp.where(b > 0.5, hi[k], lo[k])).astype(bf16)

    return pl.pallas_call(
        body,
        grid_spec=pltpu.PrefetchScalarGridSpec(
            num_scalar_prefetch=1,
            grid=(grid,),
            in_specs=[
                pl.BlockSpec((rows, span * pixels), lambda i, at: (0, i)),
                pl.BlockSpec((rows, block), lambda i, at: (0, at[0])),
                pl.BlockSpec((span, 1, block), lambda i, at: (i, 0, at[0])),
                pl.BlockSpec((span, 1, block), lambda i, at: (i, 0, at[0])),
                pl.BlockSpec((span * pixels, 1), lambda i, at: (i, 0)),
            ],
            out_specs=pl.BlockSpec((span * pixels, block), lambda i, at: (i, 0)),
        ),
        out_shape=jax.ShapeDtypeStruct((total, block), bf16),
        compiler_params=pltpu.CompilerParams(vmem_limit_bytes=63 * 2 ** 20),
        name="aspp_input_grad",
    )(place, tg, wt, low_image, high_image, band_column)
def doubled_sum(value, axis):
    size = lax.axis_size(axis)
    if size & (size - 1):
        return lax.psum(value, axis)
    step = 1
    while step < size:
        value = value + lax.ppermute(value, axis, [(i, i ^ step) for i in range(size)])
        step *= 2
    return value


def exchanged(pieces, axis):
    size = lax.axis_size(axis)
    me = lax.axis_index(axis)
    got = [pieces(me)]
    for k in range(1, size):
        got.append(lax.ppermute(pieces(me ^ k), axis, [(i, i ^ k) for i in range(size)]))
    return got


def local(aspp_input, low_input, aspp_ids, low_ids, aspp_weight, pool_weight, bn_gain, bn_shift, projection_matrix,
          reduce_weight, merge1_weight, merge2_weight, class_weight, logit_grad):
    section = lax.axis_index("section")
    sections = lax.axis_size("section")
    batch, height, width, in_chans = aspp_input.shape
    taps, own = aspp_weight.shape[1], aspp_weight.shape[2]
    branches = bn_gain.shape[0]
    chans = projection_matrix.shape[2]
    red = reduce_weight.shape[1]
    classes = class_weight.shape[1]
    fine_rows, fine_cols = low_input.shape[1], low_input.shape[2]
    pixels = height * width
    count = pixels * lax.axis_size("dp")
    coarse_rows = fine_rows // 4
    held = coarse_rows + 4

    down = [(i, i + 1) for i in range(sections - 1)]
    up = [(i + 1, i) for i in range(sections - 1)]
    low_top = lax.ppermute(low_input[:, -HALO:], "section", down)
    low_end = lax.ppermute(low_input[:, :HALO], "section", up)
    target = jnp.pad(logit_grad, ((0, 0), (0, 0), (0, 0), (0, LANE - classes)))
    target_top = lax.ppermute(target[:, -2:], "section", down)
    target_end = lax.ppermute(target[:, :2], "section", up)
    target = jnp.concatenate([target_top, target, target_end], axis=1)

    x = aspp_input.reshape(batch * pixels, in_chans)
    wt = jnp.transpose(aspp_weight, (1, 2, 0)).reshape(taps * own, in_chans)
    pwt = pool_weight.T
    cut = jnp.sum((aspp_ids[:, :, 0] == 0).astype(jnp.int32), axis=1)
    valid, member, band = pixel_tables(cut, height, width)
    counts = jnp.maximum(jnp.stack([cut, height - cut], axis=1) * width, 1).astype(f32)
    br, moments, pooled = aspp_forward(x, wt, pwt, valid, member, counts, band)

    moments = doubled_sum(moments, "dp") / count
    mean = moments[:, :, 0:1]
    inv_std = lax.rsqrt(moments[:, :, 1:2] - mean * mean + epsilon)
    gain = bn_gain.reshape(1, branches * own, 1)
    shift = bn_shift.reshape(1, branches * own, 1)
    scaled = (br - mean) * inv_std
    before = scaled * gain + shift
    active, slope = silu_and_slope(before)
    active = active.astype(bf16)
    proj = projection_matrix.reshape(branches * own, chans)
    partial = jnp.einsum("mcp,cd->mpd", active, proj, preferred_element_type=f32).astype(bf16)
    partial = jnp.pad(partial.reshape(batch, height, width, chans), ((0, 0), (2, 2), (0, 0), (0, 0)))
    got = exchanged(lambda p: lax.dynamic_slice_in_dim(partial, p * coarse_rows, held, 1), "section")
    projected = sum(g.astype(f32) for g in got).astype(bf16)

    pgrad, saved = decode(low_ids[:, :, 0], section, low_top, low_input, low_end, projected, target,
                          reduce_weight, merge1_weight, merge2_weight, class_weight, height)

    got = jnp.stack(exchanged(lambda p: pgrad, "section"))
    projected_grad = jnp.zeros((batch, height + 4, width, chans), f32)
    for p in range(sections):
        piece = lax.dynamic_index_in_dim(got, section ^ p, 0, False).astype(f32)
        first = p * coarse_rows
        projected_grad = projected_grad + jnp.pad(piece, ((0, 0), (first, height + 4 - first - held), (0, 0), (0, 0)))
    projected_grad = projected_grad[:, 2:2 + height].reshape(batch, pixels, chans).astype(bf16)

    before_grad = jnp.einsum("cd,mpd->mcp", proj, projected_grad, preferred_element_type=f32) * slope
    sums = jnp.stack([jnp.sum(before_grad * scaled, axis=2), jnp.sum(before_grad, axis=2)], axis=2)
    sums = doubled_sum(sums, "dp")
    branch_grad = inv_std * gain * (before_grad - (sums[:, :, 1:2] + scaled * sums[:, :, 0:1]) / count)
    proj_grad = jnp.einsum("mcp,mpd->cd", active, projected_grad, preferred_element_type=f32)
    pool_part = branch_grad[:, 4 * own:]
    high = jnp.sum(pool_part * band[:, None], axis=2)
    everything = jnp.sum(pool_part, axis=2)
    low_high = jnp.stack([everything - high, high], axis=1).astype(bf16)
    pool_grad = low_high.reshape(batch * IMAGES, own)
    image_grads = jnp.dot(pool_grad, pwt, preferred_element_type=f32) / counts.reshape(-1, 1)

    proj_rows = proj_grad.reshape(-1, in_chans)
    grads, tg = aspp_weight_grads(x, branch_grad[:, :4 * own], valid, pooled, pool_grad.T, proj_rows)
    grads = lax.psum(grads, "dp")

    o1, o2, oc, orr, low_grad, logits = decode_grads(saved, low_input, target, reduce_weight, class_weight)
    small = lax.psum((o1.astype(bf16), o2.astype(bf16), oc.astype(bf16), orr.astype(bf16)), ("section", "dp"))
    merge1_grad, merge2_grad, reduce_grad = unpack_decoder(*(small[k].astype(f32) for k in (0, 1, 3)), chans, red)

    band_column = band.reshape(batch * pixels, 1)
    total = None
    for k in reversed(range(sections)):
        place = (section ^ k).reshape(1).astype(jnp.int32)
        piece = aspp_input_grad(place, tg, wt, image_grads, band_column, sections)
        if k:
            piece = lax.ppermute(piece, "section", [(i, i ^ k) for i in range(sections)])
        total = piece.astype(f32) if total is None else total + piece.astype(f32)
    input_grad = total.reshape(batch, height, width, in_chans // sections)

    rows = taps * own
    wide = grads[:rows].astype(f32).reshape(taps, own, in_chans)
    return (
        logits,
        input_grad,
        low_grad,
        jnp.transpose(wide, (2, 0, 1)),
        grads[rows:rows + own].astype(f32).T,
        jnp.sum(sums[:, :, 0], axis=0).reshape(branches, own),
        jnp.sum(sums[:, :, 1], axis=0).reshape(branches, own),
        grads[rows + own:].astype(f32).reshape(branches, own, chans),
        reduce_grad,
        merge1_grad,
        merge2_grad,
        small[2].astype(f32),
    )


def solution(mesh):
    return jax.shard_map(
        local,
        mesh=mesh,
        in_specs=(
            P("dp", None, None, None), P("dp", "section", None, None), P("dp", None, None), P("dp", None, None),
            P(None, None, "section"), P(None, "section"), P(None, "section"), P(None, "section"), P(None, "section", None),
            P(), P(), P(), P(), P("dp", "section", None, None),
        ),
        out_specs=(
            P("dp", "section", None, None), P("dp", None, None, "section"), P("dp", "section", None, None),
            P(None, None, "section"), P(None, "section"), P(None, "section"), P(None, "section"), P(None, "section", None),
            P(), P(), P(), P(),
        ),
        check_vma=False,
    )
```

```python
import jax
import jax.numpy as jnp
import numpy as np
from jax import lax
from jax.experimental import pallas as pl
from jax.experimental.pallas import tpu as pltpu
from jax.sharding import PartitionSpec as P

IMAGES = 2
bf16 = jnp.bfloat16
f32 = jnp.float32
HALO = 4
LANE = 128


def upsample_matrix(coarse_count):
    fine = np.arange(4 * coarse_count)
    coarse, phase = fine // 4, fine % 4
    near = np.where(phase < 2, 5 + 2 * phase, 11 - 2 * phase) / 8.0
    far = np.clip(np.where(phase < 2, coarse - 1, coarse + 1), 0, coarse_count - 1)
    matrix = np.zeros((4 * coarse_count, coarse_count), np.float32)
    np.add.at(matrix, (fine, coarse), near)
    np.add.at(matrix, (fine, far), 1.0 - near)
    return matrix


def split_rows(first, stop, target):
    count = stop - first
    pieces = -(-count // target)
    edges = [first + (count * k) // pieces for k in range(pieces + 1)]
    return [(edges[k], edges[k + 1] - edges[k]) for k in range(pieces)]


def silu_and_slope(v):
    s = 0.5 + 0.5 * jnp.tanh(0.5 * v)
    a = v * s
    return a, s * (1.0 + v - a)


def row_tables(ids_rows, section_index, own_rows, coarse_rows):
    fine_total = ids_rows.shape[1]
    window = own_rows + 2 * HALO
    slots = window + 1
    first = section_index * own_rows - HALO
    cut = jnp.sum((ids_rows == 0).astype(jnp.int32), axis=1)[:, None] - first
    gap = jnp.where((cut >= 1) & (cut < window), cut, window)
    slot = jnp.arange(slots, dtype=jnp.int32)[None, :]
    src = slot - (slot > gap).astype(jnp.int32)
    row = src + first
    valid = (slot != gap) & (row >= 0) & (row < fine_total)
    own = valid & (src >= HALO) & (src < own_rows + HALO)
    coarse = row // 4
    phase = row % 4
    near_weight = jnp.where(phase < 2, 5 + 2 * phase, 11 - 2 * phase).astype(f32) / 8.0
    far = jnp.clip(jnp.where(phase < 2, coarse - 1, coarse + 1), 0, coarse_rows - 1)
    base = section_index * (own_rows // 4) - 2
    held = own_rows // 4 + 4
    near_at = jnp.clip(coarse - base, 0, held - 1)
    far_at = jnp.clip(far - base, 0, held - 1)
    validf = valid.astype(f32)
    ownf = own.astype(f32)
    own_at = jnp.where(own, src - HALO, own_rows)
    slot_of = slot + (slot >= gap).astype(jnp.int32)
    inside = ((slot + first >= 0) & (slot + first < fine_total)).astype(f32)
    inside = jnp.broadcast_to(inside, validf.shape)
    ints = jnp.stack(
        [jnp.clip(src, 0, window - 1), near_at, far_at, own_at, slot_of, jnp.broadcast_to(gap, src.shape)], axis=1
    )
    floats = jnp.stack(
        [
            validf,
            ownf,
            near_weight * validf,
            (1.0 - near_weight) * validf,
            near_weight * ownf,
            (1.0 - near_weight) * ownf,
            inside,
        ],
        axis=1,
    )
    batch = ids_rows.shape[0]
    return ints.astype(jnp.int32).reshape(batch, -1), floats.reshape(batch, -1)


def column_sides(v):
    n = v.shape[0]
    col = lax.broadcasted_iota(jnp.int32, v.shape, 0)
    left = jnp.where(col == 0, 0.0, pltpu.roll(v, 1, 0))
    right = jnp.where(col == n - 1, 0.0, pltpu.roll(v, n - 1, 0))
    return left, right


def three_columns(v):
    left, right = column_sides(v)
    return jnp.concatenate([left.astype(bf16), v.astype(bf16), right.astype(bf16)], axis=1)


def decode_kernel(first, own_rows, cols, chans, red, parts, itab, ftab, low_top, low, low_end, tgt, colm, colt, rwt, m1, m2, clst, *refs):
    projs, refs = refs[:parts], refs[parts:]
    decode_body(first, own_rows, cols, chans, red, projs, itab, ftab, low_top, low, low_end, tgt, colm, colt, rwt, m1, m2, clst, *refs)


def decode_body(first, own_rows, cols, chans, red, projs, itab, ftab, low_top, low, low_end, tgt, colm, colt, rwt, m1, m2, clst,
                  up_o, red_o, fst_o, sec_o, g2_o, g1_o, rg_o, pg_o,
                  jc, fc, gc2, gc1, sl1, rs, tgg, lift, drop, a0, a1, b0, b1,
                w1, rw3, clsb, wb2, wb1u, wb1r, sems):
    m = pl.program_id(0)
    window = own_rows + 2 * HALO
    slots = window + 1
    held = projs[0].shape[1]
    wide = 3 * chans
    redw = jc.shape[2] - wide

    @pl.when(m == 0)
    def _():
        w1[:, wide + 3 * red:] = jnp.zeros((3, redw - 3 * red, chans), bf16)
        clsb[...] = jnp.zeros(clsb.shape, bf16)
        clsb[0:clst.shape[0]] = clst[...]
        spare = jnp.zeros((redw - 3 * red, chans), bf16)
        rw3[...] = jnp.concatenate([rwt[...]] * 3 + [spare], axis=0).T
        for r in range(3):
            for d in range(3):
                part = slice(d * chans, (d + 1) * chans)
                w1[r, part] = m1[3 * r + d, 0:chans]
                w1[r, wide + d * red:wide + (d + 1) * red] = m1[3 * r + d, chans:]
                tap = 3 * (2 - r) + 2 - d
                wb2[r, part] = m2[tap].T
                wb1u[r, part] = m1[tap, 0:chans].T
            tails = [m1[3 * (2 - r) + d, chans:] for d in range(3)]
            wb1r[r] = jnp.concatenate(tails + [spare], axis=0).T

    def w2(r):
        return m2[3 * r:3 * r + 3].reshape(wide, chans)

    def it(k, j):
        return itab[first + m, k * slots + j]

    def ft(k, j):
        return ftab[first + m, k * slots + j]

    accs = (a0, a1)
    bccs = (b0, b1)

    def staged(blocks, multiply, finish):
        for k, block in enumerate(blocks):
            multiply(*block, accs[k % 2], bccs[k % 2])
            if k:
                finish(*blocks[k - 1], accs[(k - 1) % 2], bccs[(k - 1) % 2])
        k = len(blocks) - 1
        finish(*blocks[k], accs[k % 2], bccs[k % 2])

    def rows_of(ref, lo, n):
        return ref[lo:lo + n].reshape(n * cols, ref.shape[2])

    def dot(a, b):
        return jnp.dot(a, b, preferred_element_type=f32)

    for j in range(2, slots - 2):
        tgg[j] = tgt[0, jnp.clip(it(0, j) - 2, 0, own_rows + 3)]

    lane = lax.broadcasted_iota(jnp.int32, (cols, redw), 1)

    def reduce_mul(ref, lo, n, place, acc, _):
        acc[0:n * cols] = dot(ref[0, lo:lo + n].reshape(n * cols, ref.shape[3]), rw3[...])

    def reduce_fin(ref, lo, n, place, acc, _):
        for r in range(n):
            a, slope = silu_and_slope(acc[r * cols:(r + 1) * cols])
            a = a * ft(6, place + r)
            left, right = column_sides(a)
            a = jnp.where(lane < red, left, jnp.where(lane < 2 * red, a, right))
            jc[it(4, place + r), :, wide:] = a.astype(bf16)
            if HALO <= place + r < own_rows + HALO:
                rs[place + r - HALO] = slope.astype(bf16)

    staged(
        [(low_top, 0, HALO, 0)]
        + [(low, lo, n, lo + HALO) for lo, n in split_rows(0, own_rows, 8)]
        + [(low_end, 0, HALO, own_rows + HALO)],
        reduce_mul, reduce_fin,
    )
    jc[it(5, 0), :, wide:] = jnp.zeros((cols, redw), bf16)

    for k in range(held):
        v = sum(p[0, k].astype(f32) for p in projs).astype(bf16)
        lift[k] = dot(colm[...], v)
    for j in range(slots):
        v = (ft(2, j) * lift[it(1, j)] + ft(3, j) * lift[it(2, j)]).astype(bf16)
        for d in range(3):
            jc[j, :, d * chans:(d + 1) * chans] = v[d * cols:(d + 1) * cols]

    keep = own_rows + 3
    up_copy = pltpu.make_async_copy(jc.at[3:3 + keep, :, chans:2 * chans], up_o.at[m], sems.at[0])
    red_copy = pltpu.make_async_copy(jc.at[3:3 + keep, :, wide:], red_o.at[m], sems.at[1])
    up_copy.start()
    red_copy.start()

    def first_mul(lo, n, acc, _):
        acc[0:n * cols] = (
            dot(rows_of(jc, lo - 1, n), w1[0]) + dot(rows_of(jc, lo, n), w1[1]) + dot(rows_of(jc, lo + 1, n), w1[2])
        )

    def first_fin(lo, n, acc, _):
        for r in range(n):
            a, slope = silu_and_slope(acc[r * cols:(r + 1) * cols])
            keep_row = ft(0, lo + r)
            fc[lo + r] = three_columns(a * keep_row)
            sl1[lo + r] = (slope * keep_row).astype(bf16)

    staged(split_rows(1, slots - 1, 8), first_mul, first_fin)
    fst_copy = pltpu.make_async_copy(fc.at[3:3 + keep, :, chans:2 * chans], fst_o.at[m], sems.at[2])
    fst_copy.start()

    def second_mul(lo, n, acc, bcc):
        acc[0:n * cols] = (
            dot(rows_of(fc, lo - 1, n), w2(0)) + dot(rows_of(fc, lo, n), w2(1)) + dot(rows_of(fc, lo + 1, n), w2(2))
        )
        bcc[0:n * cols] = dot(rows_of(tgg, lo, n), clsb[...])

    def second_fin(lo, n, acc, bcc):
        for r in range(n):
            j = lo + r
            a, slope = silu_and_slope(acc[r * cols:(r + 1) * cols])
            sec_o[0, it(3, j)] = a.astype(bf16)
            g = bcc[r * cols:(r + 1) * cols] * slope * ft(0, j)
            gc2[j] = three_columns(g)
            if HALO <= j <= own_rows + HALO:
                g2_o[0, j - HALO] = (g * ft(1, j)).astype(bf16)

    staged(split_rows(2, slots - 2, 8), second_mul, second_fin)

    def back2_mul(lo, n, acc, _):
        acc[0:n * cols] = (
            dot(rows_of(gc2, lo - 1, n), wb2[0]) + dot(rows_of(gc2, lo, n), wb2[1]) + dot(rows_of(gc2, lo + 1, n), wb2[2])
        )

    def back2_fin(lo, n, acc, _):
        for r in range(n):
            j = lo + r
            g = acc[r * cols:(r + 1) * cols] * sl1[j].astype(f32)
            gc1[j] = three_columns(g)
            if HALO <= j <= own_rows + HALO:
                g1_o[0, j - HALO] = (g * ft(1, j)).astype(bf16)

    staged(split_rows(3, slots - 3, 8), back2_mul, back2_fin)

    drop[...] = jnp.zeros(drop.shape, f32)

    def back1_mul(lo, n, acc, bcc):
        acc[0:n * cols] = (
            dot(rows_of(gc1, lo - 1, n), wb1u[0]) + dot(rows_of(gc1, lo, n), wb1u[1]) + dot(rows_of(gc1, lo + 1, n), wb1u[2])
        )
        mid = slice(chans, 2 * chans)
        bcc[0:n * cols] = (
            dot(rows_of(gc1, lo - 1, n)[:, mid], wb1r[0]) + dot(rows_of(gc1, lo, n)[:, mid], wb1r[1])
            + dot(rows_of(gc1, lo + 1, n)[:, mid], wb1r[2])
        )

    def back1_fin(lo, n, acc, bcc):
        for r in range(n):
            j = lo + r
            up = acc[r * cols:(r + 1) * cols]
            near, far = it(1, j), it(2, j)
            drop[near] += ft(4, j) * up
            drop[far] += ft(5, j) * up
            t = bcc[r * cols:(r + 1) * cols]
            left, right = column_sides(t)
            t = jnp.where(lane < red, right, jnp.where(lane < 2 * red, t, left))
            rg_o[0, it(3, j)] = (t * rs[it(3, j)].astype(f32)).astype(bf16)

    staged(split_rows(HALO, slots - HALO, 8), back1_mul, back1_fin)

    for k in range(held):
        pg_o[0, k] = dot(colt[...], drop[k].astype(bf16)).astype(bf16)
    up_copy.wait()
    red_copy.wait()
    fst_copy.wait()


def whole(a):
    return pl.BlockSpec(a.shape, lambda *at: (0,) * a.ndim, pipeline_mode=pl.Buffered(1))


def per(shape, first=0):
    return pl.BlockSpec((1,) + shape, lambda m: (m + first,) + (0,) * len(shape))


def total(shape):
    return pl.BlockSpec(shape, lambda *at: (0,) * len(shape))


def params():
    return pltpu.CompilerParams(vmem_limit_bytes=63 * 2 ** 20)


def decode(first, batch, tables, low_top, low_input, low_end, projs, target, reduce_t, merge1_weight, merge2_weight, class_t):
    ints, floats = tables
    _, own_rows, cols, low_ch = low_input.shape
    window = own_rows + 2 * HALO
    slots = window + 1
    chans = merge2_weight.shape[1]
    red = reduce_t.shape[0]
    held, coarse_cols = projs[0].shape[1], projs[0].shape[2]
    redw = -(-3 * red // LANE) * LANE
    wide = 3 * chans
    colm = upsample_matrix(coarse_cols)
    zero = np.zeros((1, coarse_cols), np.float32)
    colm3 = jnp.asarray(np.concatenate([zero, colm[:-1], colm, colm[1:], zero], axis=0), bf16)
    colt = jnp.asarray(colm.T, bf16)
    keep = own_rows + 3
    smem = pl.BlockSpec(memory_space=pltpu.SMEM)
    hbm = pl.BlockSpec(memory_space=pl.ANY)
    most = max(n for k in range(5) for _, n in split_rows(k, slots - k, 8))
    consts = (colm3, colt, reduce_t, merge1_weight, merge2_weight, class_t)
    shapes = [((keep, cols, chans), hbm), ((keep, cols, redw), hbm), ((keep, cols, chans), hbm),
              ((own_rows + 1, cols, chans), None), ((own_rows + 1, cols, chans), None), ((own_rows + 1, cols, chans), None),
              ((own_rows + 1, cols, redw), None), ((held, coarse_cols, chans), None)]
    saved = pl.pallas_call(
        lambda *refs: decode_kernel(first, own_rows, cols, chans, red, len(projs), *refs),
        grid=(batch,),
        in_specs=[smem, smem] + [per(a.shape[1:], first) for a in (low_top, low_input, low_end, target)]
        + [whole(a) for a in consts] + [per(p.shape[1:]) for p in projs],
        out_specs=[s or per(sh) for sh, s in shapes],
        out_shape=[jax.ShapeDtypeStruct((batch,) + sh, bf16) for sh, _ in shapes],
        scratch_shapes=[
            pltpu.VMEM((slots, cols, wide + redw), bf16), pltpu.VMEM((slots, cols, wide), bf16),
            pltpu.VMEM((slots, cols, wide), bf16), pltpu.VMEM((slots, cols, wide), bf16),
            pltpu.VMEM((slots, cols, chans), bf16), pltpu.VMEM((own_rows + 1, cols, redw), bf16),
            pltpu.VMEM((slots, cols, LANE), bf16),
            pltpu.VMEM((held, 3 * cols, chans), f32), pltpu.VMEM((held, cols, chans), f32),
            pltpu.VMEM((most * cols, chans), f32), pltpu.VMEM((most * cols, chans), f32),
            pltpu.VMEM((most * cols, chans), f32), pltpu.VMEM((most * cols, chans), f32),
            pltpu.VMEM((3, wide + redw, chans), bf16), pltpu.VMEM((low_ch, redw), bf16), pltpu.VMEM((LANE, chans), bf16),
            pltpu.VMEM((3, wide, chans), bf16), pltpu.VMEM((3, wide, chans), bf16), pltpu.VMEM((3, chans, redw), bf16),
            pltpu.SemaphoreType.DMA((3,)),
        ],
        compiler_params=params(),
        name="decode",
    )(ints, floats, low_top, low_input, low_end, target, *consts, *projs)
    return saved[7], tuple(saved[:7])


def grads_kernel(own_rows, cols, chans, red, before, up, red3, fst, sec, g2, g1, rg, low, tgt, clst, rwt, *refs):
    earlier = refs[:before]
    packed, lowgrad, logits, o1, o2, oc, orr, upc, fcc = refs[before:]
    m = pl.program_id(0)
    keep = own_rows + 3
    wide = 3 * chans
    span = own_rows + 1
    classes = clst.shape[0]

    @pl.when(m == 0)
    def _():
        o1[...] = jnp.zeros(o1.shape, f32)
        o2[...] = jnp.zeros(o2.shape, f32)
        oc[...] = jnp.zeros(oc.shape, f32)
        orr[...] = jnp.zeros(orr.shape, f32)

    def tdot(a, b):
        return lax.dot_general(a, b, (((0,), (0,)), ((), ())), preferred_element_type=f32)

    for j in range(keep):
        upc[j] = three_columns(up[0, j].astype(f32))
    for j in range(keep):
        fcc[j] = three_columns(fst[0, j].astype(f32))

    def flat(v):
        return v.reshape(v.shape[0] * cols, v.shape[2])

    gg1 = flat(g1[0])
    for dy in range(3):
        o1[dy, 0:wide] += tdot(flat(upc[dy:dy + span]), gg1)
        o1[dy, wide:] += tdot(flat(red3[0, dy:dy + span]), gg1)
    gg2 = flat(g2[0])
    for dy in range(3):
        o2[dy] += tdot(flat(fcc[dy:dy + span]), gg2)
    oc[...] += tdot(flat(sec[0]), flat(tgt[0, 2:2 + own_rows]))
    orr[...] += tdot(flat(low[0]), flat(rg[0]))
    spare = jnp.zeros((rg.shape[3] - 3 * red, chans), bf16)
    rb3 = jnp.concatenate([rwt[...]] * 3 + [spare], axis=0)
    for r in range(own_rows):
        lowgrad[0, r] = jnp.dot(rg[0, r], rb3, preferred_element_type=f32)
        lt = lax.dot_general(clst[...], sec[0, r], (((1,), (1,)), ((), ())), preferred_element_type=f32)
        logits[0, :, r] = lt

    @pl.when(m == pl.num_programs(0) - 1)
    def _():
        rows = chans + red
        for dy in range(3):
            for d in range(3):
                at = (3 * dy + d) * rows
                packed[at:at + chans] = o1[dy, d * chans:(d + 1) * chans].astype(bf16)
                packed[at + chans:at + rows] = o1[dy, wide + d * red:wide + (d + 1) * red].astype(bf16)
            packed[9 * rows + dy * wide:9 * rows + (dy + 1) * wide] = o2[dy].astype(bf16)
        at = 9 * rows + 3 * wide
        packed[at:] = jnp.zeros((packed.shape[0] - at, chans), bf16)
        t = orr[...].T
        packed[at:at + red] = (t[0:red] + t[red:2 * red] + t[2 * red:3 * red]).astype(bf16)
        packed[at + red:at + red + 32] = oc[...].T[0:32].astype(bf16)
        if before:
            packed[...] = (packed[...].astype(f32) + earlier[0][...].astype(f32)).astype(bf16)


def packed_rows(chans, red):
    return 9 * (chans + red) + 9 * chans + red + 32


def decode_grads(first, saved, low_input, target, reduce_t, class_t, earlier):
    up, red3, fst, sec, g2, g1, rg = saved
    batch = up.shape[0]
    all_batch, own_rows, cols, low_ch = low_input.shape
    chans = up.shape[3]
    redw = red3.shape[3]
    red = reduce_t.shape[0]
    classes = class_t.shape[0]
    wide = 3 * chans
    keep = own_rows + 3
    rows = packed_rows(chans, red)
    hbm = pl.BlockSpec(memory_space=pl.ANY)
    tots = [(3, wide + redw, chans), (3, wide, chans), (chans, LANE), (low_ch, redw)]
    pers = [(own_rows, cols, low_ch), (classes, own_rows, cols)]
    packed, lowgrad, logits = pl.pallas_call(
        lambda *refs: grads_kernel(own_rows, cols, chans, red, 3 if earlier else 0, *refs),
        grid=(batch,),
        in_specs=[per((keep, cols, chans)), per((keep, cols, redw)), per((keep, cols, chans)), per((own_rows, cols, chans)),
                  per((own_rows + 1, cols, chans)), per((own_rows + 1, cols, chans)), per((own_rows, cols, redw)),
                  per((own_rows, cols, low_ch), first), per(target.shape[1:], first), whole(class_t), whole(reduce_t)]
        + ([whole(earlier[0]), hbm, hbm] if earlier else []),
        out_specs=[total((rows, chans))] + [per(s, first) for s in pers],
        out_shape=[jax.ShapeDtypeStruct((rows, chans), bf16)] + [jax.ShapeDtypeStruct((all_batch,) + s, f32) for s in pers],
        input_output_aliases={12: 1, 13: 2} if earlier else {},
        scratch_shapes=[pltpu.VMEM(s, f32) for s in tots]
        + [pltpu.VMEM((keep, cols, wide), bf16), pltpu.VMEM((keep, cols, wide), bf16)],
        compiler_params=params(),
        name="decode_grads",
        cost_estimate=pl.CostEstimate(flops=1, bytes_accessed=1, transcendentals=1),
    )(up, red3, fst, sec, g2, g1, rg, low_input, target, class_t, reduce_t, *(earlier or ()))
    return packed, lowgrad, logits


def unpack_decoder(packed, chans, red, classes):
    rows = chans + red
    at = 9 * rows + 9 * chans
    v = packed.astype(f32)
    return (v[:9 * rows].reshape(9, rows, chans), v[9 * rows:at].reshape(9, chans, chans),
            v[at:at + red].T, v[at + red:at + red + classes].T)


atrous_rates = (6, 12, 18)
epsilon = 1e-05


def tap_list():
    listed = [(0, 0, 0)]
    for branch_index, rate_value in enumerate(atrous_rates):
        for step_rows in (-1, 0, 1):
            for step_cols in (-1, 0, 1):
                listed.append((rate_value * step_rows, rate_value * step_cols, branch_index + 1))
    return listed


def pixel_places(batch, height, width):
    pixel = np.arange(height * width)
    places = np.stack([np.tile(pixel // width, batch), np.tile(pixel % width, batch), np.repeat(np.arange(batch), height * width)])
    return jnp.asarray(np.pad(places, ((0, 5), (0, 0))), jnp.int32)


class Pixels:
    def __init__(self, places, cuts, batch, height, width):
        self.row, self.col, self.canvas = places[0:1], places[1:2], places[2:3]
        self.height, self.width = height, width
        cut = jnp.full(self.row.shape, cuts[0], jnp.int32)
        for m in range(1, batch):
            cut = jnp.where(self.canvas == m, cuts[m], cut)
        self.cut = cut
        self.band = self.row >= cut

    def valid(self, dr, dc):
        row, col = self.row + dr, self.col + dc
        inside = (row >= 0) & (row < self.height) & (col >= 0) & (col < self.width)
        same = jnp.where(row >= self.cut, 1, 0) == jnp.where(self.band, 1, 0)
        return jnp.where(inside & same, 1.0, 0.0)

    def image(self):
        return IMAGES * self.canvas + jnp.where(self.band, 1, 0)


def image_counts(cuts, batch, height, width):
    index = lax.broadcasted_iota(jnp.int32, (IMAGES * batch, 1), 0)
    out = jnp.zeros((IMAGES * batch, 1), f32)
    for m in range(batch):
        first = cuts[m] * width
        out = jnp.where(index == IMAGES * m, first.astype(f32), out)
        out = jnp.where(index == IMAGES * m + 1, (height * width - first).astype(f32), out)
    return jnp.maximum(out, 1.0)


def branch_kernel(taps, batch, height, width, cuts, x, w, places, pw, br_o, mom_o, pooled_o, y, pool, mom):
    i = pl.program_id(0)
    last = pl.num_programs(0) - 1
    block = x.shape[0]
    total = y.shape[1]
    pixels = total // batch
    own = pw.shape[0]
    at = pl.multiple_of(i * block, block)

    @pl.when(i == 0)
    def _():
        pool[...] = jnp.zeros(pool.shape, f32)
        mom[...] = jnp.zeros(mom.shape, f32)

    def nt(a, b):
        return lax.dot_general(a, b, (((1,), (1,)), ((), ())), preferred_element_type=f32)

    canvas, row = places[2:3, pl.ds(at, block)], places[0:1, pl.ds(at, block)]
    cut = jnp.full(row.shape, cuts[0], jnp.int32)
    for m in range(1, batch):
        cut = jnp.where(canvas == m, cuts[m], cut)
    image = IMAGES * canvas + jnp.where(row >= cut, 1, 0)
    index = lax.broadcasted_iota(jnp.int32, (IMAGES * batch, block), 0)
    member = jnp.where(image == index, 1.0, 0.0).astype(bf16)
    pool[...] += jnp.dot(member, x[...], preferred_element_type=f32)

    @pl.when(i < last)
    def _():
        y[:, pl.ds(at, block)] = nt(w[...], x[...])

    def keep(m, b, v):
        part = slice(b * own, (b + 1) * own)
        br_o[m, part] = v
        mom[part, m:m + 1] = jnp.sum(v, axis=1, keepdims=True)
        mom[part, batch + m:batch + m + 1] = jnp.sum(v * v, axis=1, keepdims=True)

    @pl.when(i == last)
    def _():
        px = Pixels(places, cuts, batch, height, width)
        spans = []
        for b in range(4):
            mine = [t for t, tap in enumerate(taps) if tap[2] == b]
            spans.append((mine[0], mine[-1] + 1))

        def multiply(b):
            lo, hi = spans[b][0] * own, spans[b][1] * own
            y[lo:hi, total - block:] = nt(w[lo:hi], x[...])

        def finish(b):
            acc = None
            for t in range(*spans[b]):
                dr, dc, _ = taps[t]
                v = y[t * own:(t + 1) * own]
                shift = dr * width + dc
                if shift:
                    v = pltpu.roll(v, (-shift) % total, 1) * px.valid(dr, dc)
                acc = v if acc is None else acc + v
            for m in range(batch):
                keep(m, b, acc[:, m * pixels:(m + 1) * pixels])

        multiply(0)
        multiply(1)
        multiply(2)
        finish(0)
        finish(1)
        multiply(3)
        finish(2)
        finish(3)
        pooled = (pool[...] / image_counts(cuts, batch, height, width)).astype(bf16)
        pooled_o[...] = pooled
        po = nt(pw[...], pooled)
        for m in range(batch):
            band = px.band[:, m * pixels:(m + 1) * pixels]
            keep(m, 4, jnp.where(band, po[:, IMAGES * m + 1:IMAGES * m + 2], po[:, IMAGES * m:IMAGES * m + 1]))
        mom_o[...] = mom[...].T[0:mom_o.shape[0]]


def aspp_forward(cuts, x, wt, pwt, batch, height, width):
    all_pixels, in_chans = x.shape
    pixels = height * width
    own = pwt.shape[0]
    taps = tap_list()
    block = all_pixels // 3 if all_pixels % 3 == 0 and (all_pixels // 3) % LANE == 0 else all_pixels
    places = pixel_places(batch, height, width)
    outs = [((batch, 5 * own, pixels), f32), ((2 * batch, 5 * own), f32), ((IMAGES * batch, in_chans), bf16)]
    return pl.pallas_call(
        lambda *refs: branch_kernel(taps, batch, height, width, *refs),
        grid=(all_pixels // block,),
        in_specs=[pl.BlockSpec(memory_space=pltpu.SMEM), pl.BlockSpec((block, in_chans), lambda i: (i, 0)),
                  whole(wt), whole(places), whole(pwt)],
        out_specs=[total(s) for s, _ in outs],
        out_shape=[jax.ShapeDtypeStruct(s, d) for s, d in outs],
        scratch_shapes=[pltpu.VMEM((len(taps) * own, all_pixels), f32), pltpu.VMEM((IMAGES * batch, in_chans), f32),
                        pltpu.VMEM((5 * own, LANE), f32)],
        compiler_params=params(),
        name="aspp_forward",
    )(cuts, x, wt, places, pwt)


def norm_columns(stats, m, batch, count):
    t = stats[...].T
    mean = t[:, m:m + 1] / count
    inv_std = lax.rsqrt(t[:, batch + m:batch + m + 1] / count - mean * mean + epsilon)
    return mean, inv_std, t[:, 2 * batch:2 * batch + 1], t[:, 2 * batch + 1:2 * batch + 2]


def project_kernel(groups, batch, count, coarse_rows, offsets, br, stats, proj, *refs):
    outs, rows = refs[:-1], refs[-1]
    parts = len(outs) // groups
    height, width, chans = rows.shape[0] - 4, rows.shape[1], rows.shape[2]
    held = coarse_rows + 4
    rows[0:2] = jnp.zeros((2, width, chans), f32)
    rows[height + 2:] = jnp.zeros((2, width, chans), f32)
    for m in range(batch):
        mean, inv_std, gain, shift = norm_columns(stats, m, batch, count)
        active, _ = silu_and_slope((br[m] - mean) * inv_std * gain + shift)
        partial = lax.dot_general(active.astype(bf16), proj[...], (((0,), (0,)), ((), ())), preferred_element_type=f32)
        rows[2:height + 2] = partial.reshape(height, width, chans)
        group, at = m // (batch // groups), m % (batch // groups)
        for k in range(parts):
            outs[group * parts + k][at] = rows[pl.ds(offsets[k], held)].astype(bf16)


def project(groups, offsets, br, stats, proj, count, coarse_rows, parts, height, width):
    batch = br.shape[0]
    chans = proj.shape[1]
    shape = (batch // groups, coarse_rows + 4, width, chans)
    outs = pl.pallas_call(
        lambda *refs: project_kernel(groups, batch, count, coarse_rows, *refs),
        grid=(1,),
        in_specs=[pl.BlockSpec(memory_space=pltpu.SMEM), whole(br), whole(stats), whole(proj)],
        out_specs=[total(shape)] * (parts * groups),
        out_shape=[jax.ShapeDtypeStruct(shape, bf16)] * (parts * groups),
        scratch_shapes=[pltpu.VMEM((height + 4, width, chans), f32)],
        compiler_params=params(),
        name="project",
    )(offsets, br, stats, proj)
    return [outs[g * parts:(g + 1) * parts] for g in range(groups)]


def norm_back_kernel(first, count, parts, offsets, br, stats, proj, earlier, *refs):
    pieces = refs[:parts]
    grad_o, sums_o, projgrad_o, rows, sums = refs[parts:]
    height, width, chans = rows.shape[0] - 4, rows.shape[1], rows.shape[2]
    group, held = pieces[0].shape[0], pieces[0].shape[1]
    batch = br.shape[0]
    sums[...] = jnp.zeros(sums.shape, f32)
    projgrad = earlier[...]
    for at in range(group):
        m = first + at
        rows[...] = jnp.zeros(rows.shape, f32)
        for k, piece in enumerate(pieces):
            rows[pl.ds(offsets[k], held)] += piece[at].astype(f32)
        grad = rows[2:height + 2].reshape(height * width, chans).astype(bf16)
        mean, inv_std, gain, shift = norm_columns(stats, m, batch, count)
        scaled = (br[m] - mean) * inv_std
        active, slope = silu_and_slope(scaled * gain + shift)
        back = lax.dot_general(proj[...], grad, (((1,), (1,)), ((), ())), preferred_element_type=f32) * slope
        grad_o[at] = back
        sums[:, at:at + 1] = jnp.sum(back * scaled, axis=1, keepdims=True)
        sums[:, group + at:group + at + 1] = jnp.sum(back, axis=1, keepdims=True)
        projgrad = projgrad + jnp.dot(active.astype(bf16), grad, preferred_element_type=f32)
    projgrad_o[...] = projgrad
    sums_o[...] = sums[...].T[0:sums_o.shape[0]]


def norm_back(first, offsets, br, stats, proj, earlier, pieces, count, height, width):
    batch, chans5, pixels = br.shape
    group = pieces[0].shape[0]
    chans = proj.shape[1]
    outs = [((group, chans5, pixels), f32), ((2 * group, chans5), f32), (proj.shape, f32)]
    return pl.pallas_call(
        lambda *refs: norm_back_kernel(first, count, len(pieces), *refs),
        grid=(1,),
        in_specs=[pl.BlockSpec(memory_space=pltpu.SMEM), whole(br), whole(stats), whole(proj), whole(earlier)]
        + [whole(p) for p in pieces],
        out_specs=[total(s) for s, _ in outs],
        out_shape=[jax.ShapeDtypeStruct(s, d) for s, d in outs],
        scratch_shapes=[pltpu.VMEM((height + 4, width, chans), f32), pltpu.VMEM((chans5, LANE), f32)],
        compiler_params=params(),
        name="norm_back",
    )(offsets, br, stats, proj, earlier, *pieces)


def tap_grad_kernel(taps, batch, groups, height, width, count, cuts, br, stats, places, *refs):
    backs, sums = refs[:groups], refs[groups:2 * groups]
    tg_o, pg_o, both = refs[2 * groups:]
    own = pg_o.shape[0]
    pixels = br.shape[2]
    all_pixels = tg_o.shape[1]
    group = batch // groups
    px = Pixels(places, cuts, batch, height, width)
    pool_grad = jnp.zeros((own, LANE), f32)
    lane = lax.broadcasted_iota(jnp.int32, (own, LANE), 1)
    at = len(taps) * own
    for m in range(batch):
        g, k = m // group, m % group
        t = sums[g][...].T
        mean, inv_std, gain, _ = norm_columns(stats, m, batch, count)
        gain_sum, shift_sum = t[:, k:k + 1], t[:, group + k:group + k + 1]
        scaled = (br[m] - mean) * inv_std
        grad = inv_std * gain * (backs[g][k] - (shift_sum + scaled * gain_sum) / count)
        both[0:4 * own, m * pixels:(m + 1) * pixels] = grad[0:4 * own]
        pool = grad[4 * own:]
        band = px.band[:, m * pixels:(m + 1) * pixels]
        upper = jnp.sum(jnp.where(band, 0.0, pool), axis=1, keepdims=True).astype(bf16).astype(f32)
        lower = jnp.sum(jnp.where(band, pool, 0.0), axis=1, keepdims=True).astype(bf16).astype(f32)
        pool_grad = jnp.where(lane == IMAGES * m, upper, pool_grad)
        pool_grad = jnp.where(lane == IMAGES * m + 1, lower, pool_grad)
        many = (cuts[m] * width).astype(f32)
        spread = jnp.where(band, lower / jnp.maximum(height * width - many, 1.0), upper / jnp.maximum(many, 1.0))
        both[4 * own:, m * pixels:(m + 1) * pixels] = spread
    pg_o[...] = pool_grad[:, 0:pg_o.shape[1]].astype(bf16)
    for k, (dr, dc, b) in enumerate(taps):
        v = both[b * own:(b + 1) * own]
        shift = dr * width + dc
        if shift:
            v = pltpu.roll(v * px.valid(dr, dc), shift % all_pixels, 1)
        tg_o[k * own:(k + 1) * own] = v.astype(bf16)
    tg_o[at:at + own] = both[4 * own:].astype(bf16)
    tg_o[at + own:] = jnp.zeros((tg_o.shape[0] - at - own, all_pixels), bf16)


def tap_grads(rows, cuts, br, stats, backs, sums, count, height, width):
    batch, chans5, pixels = br.shape
    own = chans5 // 5
    places = pixel_places(batch, height, width)
    groups = len(backs)
    outs = [(rows, batch * pixels), (own, IMAGES * batch)]
    return pl.pallas_call(
        lambda *refs: tap_grad_kernel(tap_list(), batch, groups, height, width, count, *refs),
        grid=(1,),
        in_specs=[pl.BlockSpec(memory_space=pltpu.SMEM), whole(br), whole(stats), whole(places)]
        + [whole(v) for v in backs] + [whole(v) for v in sums],
        out_specs=[total(s) for s in outs],
        out_shape=[jax.ShapeDtypeStruct(s, bf16) for s in outs],
        scratch_shapes=[pltpu.VMEM((chans5, batch * pixels), f32)],
        compiler_params=params(),
        name="tap_grads",
    )(cuts, br, stats, places, *backs, *sums)


def weight_grad_kernel(filled, tg, x, projgrad, o):
    o[...] = jnp.dot(tg[...], x[...], preferred_element_type=f32).astype(bf16)
    o[filled:filled + projgrad.shape[0]] = projgrad[...].astype(bf16)


def aspp_weight_grads(tg, x, projgrad, filled):
    rows, all_pixels = tg.shape
    in_chans = x.shape[1]
    block = 512 if in_chans % 512 == 0 else in_chans

    def lanes(a):
        return pl.BlockSpec((a, block), lambda j: (0, j))

    return pl.pallas_call(
        lambda *refs: weight_grad_kernel(filled, *refs),
        grid=(in_chans // block,),
        in_specs=[whole(tg), lanes(all_pixels), lanes(projgrad.shape[0])],
        out_specs=lanes(rows),
        out_shape=jax.ShapeDtypeStruct((rows, in_chans), bf16),
        compiler_params=params(),
        name="aspp_weight_grads",
    )(tg, x, projgrad)


def unpack_weights(summed, *counts):
    rows, in_chans = summed.shape
    block = 512 if in_chans % 512 == 0 else in_chans

    def kernel(v, *outs):
        at = 0
        for o in outs:
            o[...] = v[at:at + o.shape[0]].astype(f32)
            at += o.shape[0]

    def lanes(a):
        return pl.BlockSpec((a, block), lambda j: (0, j))

    return pl.pallas_call(
        kernel,
        grid=(in_chans // block,),
        in_specs=[lanes(rows)],
        out_specs=[lanes(n) for n in counts],
        out_shape=[jax.ShapeDtypeStruct((n, in_chans), f32) for n in counts],
        compiler_params=params(),
        name="unpack_weights",
    )(summed)


def input_grad_kernel(batch, span, height, width, at, cuts, tg, w, pg, pw, band, o):
    i = pl.program_id(0)
    pixels = height * width
    v = lax.dot_general(tg[...], w[...], (((0,), (0,)), ((), ())), preferred_element_type=f32)
    image = lax.dot_general(pg[...], pw[...], (((0,), (0,)), ((), ())), preferred_element_type=f32)
    image = image / image_counts(cuts, batch, height, width)
    index = lax.broadcasted_iota(jnp.int32, (IMAGES * batch, 1), 0)
    row = band[...]
    for k in range(span):
        m = i * span + k
        first = jnp.sum(jnp.where(index == IMAGES * m, image, 0.0), axis=0, keepdims=True)
        second = jnp.sum(jnp.where(index == IMAGES * m + 1, image, 0.0), axis=0, keepdims=True)
        part = slice(k * pixels, (k + 1) * pixels)
        o[part] = (v[part] + jnp.where(row >= cuts[m], second, first)).astype(bf16)


def aspp_input_grad(place, cuts, tg, wt, pool_grad, pwt, parts, height, width):
    rows, in_chans = wt.shape
    all_pixels = tg.shape[1]
    own = pwt.shape[0]
    pixels = height * width
    batch = all_pixels // pixels
    block = in_chans // parts
    span = 2 if (2 * pixels) % LANE == 0 and batch % 2 == 0 else batch
    row_column = jnp.asarray(np.arange(pixels)[:, None] // width, jnp.int32)
    return pl.pallas_call(
        lambda *refs: input_grad_kernel(batch, span, height, width, *refs),
        grid_spec=pltpu.PrefetchScalarGridSpec(
            num_scalar_prefetch=2,
            grid=(batch // span,),
            in_specs=[
                pl.BlockSpec((rows, span * pixels), lambda i, at, cuts: (0, i)),
                pl.BlockSpec((rows, block), lambda i, at, cuts: (0, at[0])),
                whole(pool_grad),
                pl.BlockSpec((own, block), lambda i, at, cuts: (0, at[0])),
                whole(row_column),
            ],
            out_specs=pl.BlockSpec((span * pixels, block), lambda i, at, cuts: (i, 0)),
        ),
        out_shape=jax.ShapeDtypeStruct((all_pixels, block), bf16),
        compiler_params=params(),
        name="aspp_input_grad",
        cost_estimate=pl.CostEstimate(flops=1, bytes_accessed=1, transcendentals=1),
    )(place, cuts, tg, wt, pool_grad, pwt, row_column)


def doubled_sum(value, axis):
    size = lax.axis_size(axis)
    step = 1
    while step < size:
        value = value + lax.ppermute(value, axis, [(i, i ^ step) for i in range(size)])
        step *= 2
    return value


def exchanged(pieces, axis):
    size = lax.axis_size(axis)
    return [pieces[0]] + [lax.ppermute(pieces[k], axis, [(i, i ^ k) for i in range(size)]) for k in range(1, size)]


def added(a, b):
    return (a.astype(f32) + b.astype(f32)).astype(bf16)


def distances(axis):
    size = lax.axis_size(axis)
    return [1 << k for k in range(size.bit_length() - 1)]


def halve(value, axis, step):
    bit = (lax.axis_index(axis) // step) % 2
    half = value.shape[0] // 2
    mine = lax.dynamic_slice_in_dim(value, bit * half, half, 0)
    other = lax.dynamic_slice_in_dim(value, (1 - bit) * half, half, 0)
    return added(mine, lax.ppermute(other, axis, [(i, i ^ step) for i in range(lax.axis_size(axis))]))


def join(value, axis, step):
    bit = (lax.axis_index(axis) // step) % 2
    other = lax.ppermute(value, axis, [(i, i ^ step) for i in range(lax.axis_size(axis))])
    return jnp.where(bit == 0, jnp.concatenate([value, other]), jnp.concatenate([other, value]))


def small_sum_steps():
    steps = [lambda v: halve(v, "dp", 1)]
    steps += [lambda v, d=d: halve(v, "section", d) for d in distances("section")]
    steps += [lambda v, d=d: added(v, lax.ppermute(v, "dp", [(i, i ^ d) for i in range(lax.axis_size("dp"))]))
              for d in distances("dp")[1:]]
    steps += [lambda v, d=d: join(v, "section", d) for d in reversed(distances("section"))]
    steps += [lambda v: join(v, "dp", 1)]
    return steps


def tied(value, *others):
    return lax.optimization_barrier((value,) + others)[0]


def local(aspp_input, low_input, aspp_ids, low_ids, aspp_weight, pool_weight, bn_gain, bn_shift, projection_matrix,
          reduce_weight, merge1_weight, merge2_weight, class_weight, logit_grad):
    section = lax.axis_index("section")
    sections = lax.axis_size("section")
    batch, height, width, in_chans = aspp_input.shape
    taps, own = aspp_weight.shape[1], aspp_weight.shape[2]
    branches = bn_gain.shape[0]
    chans = projection_matrix.shape[2]
    red = reduce_weight.shape[1]
    classes = class_weight.shape[1]
    fine_rows, fine_cols = low_input.shape[1], low_input.shape[2]
    pixels = height * width
    count = pixels * lax.axis_size("dp")
    coarse_rows = fine_rows // 4
    groups = 2
    group = batch // groups

    x = aspp_input.reshape(batch * pixels, in_chans)
    wt = jnp.transpose(aspp_weight, (1, 2, 0)).reshape(taps * own, in_chans)
    pwt = pool_weight.T
    proj = projection_matrix.reshape(branches * own, chans)
    cuts = jnp.sum((aspp_ids[:, :, 0] == 0).astype(jnp.int32), axis=1)
    br, moments, pooled = aspp_forward(cuts, x, wt, pwt, batch, height, width)

    down = [(i, i + 1) for i in range(sections - 1)]
    up = [(i + 1, i) for i in range(sections - 1)]
    low_top = lax.ppermute(low_input[:, -HALO:], "section", down)
    low_end = lax.ppermute(low_input[:, :HALO], "section", up)
    target = jnp.pad(logit_grad, ((0, 0), (0, 0), (0, 0), (0, LANE - classes)))
    target_top = lax.ppermute(target[:, -2:], "section", down)
    target_end = lax.ppermute(target[:, :2], "section", up)
    target = jnp.concatenate([target_top, target, target_end], axis=1)
    tables = row_tables(low_ids[:, :, 0], section, fine_rows, height)
    distance = jnp.arange(sections, dtype=jnp.int32)
    offsets = (section ^ distance) * coarse_rows

    stats = jnp.concatenate([doubled_sum(moments, "dp"), bn_gain.reshape(1, -1), bn_shift.reshape(1, -1)], axis=0)
    parts = project(groups, offsets, br, stats, proj, count, coarse_rows, sections, height, width)
    projs = [exchanged(p, "section") for p in parts]
    saved, pieces = [], []
    for g in range(groups):
        pgrad, kept = decode(g * group, group, tables, low_top, low_input, low_end, projs[g], target, reduce_weight.T,
                             merge1_weight, merge2_weight, class_weight.T)
        saved.append(kept)
        pieces.append(exchanged([pgrad] * sections, "section"))
    backs, sums = [], []
    projgrad = jnp.zeros(proj.shape, f32)
    for g in range(groups):
        back, s, projgrad = norm_back(g * group, offsets, br, stats, proj, projgrad, pieces[g], count, height, width)
        backs.append(back)
        sums.append(doubled_sum(s, "dp"))
    filled = (taps + 1) * own
    proj_rows = projgrad.reshape(-1, in_chans)
    rows = -(-(filled + proj_rows.shape[0]) // 32) * 32
    tg, pool_grad = tap_grads(rows, cuts, br, stats, backs, sums, count, height, width)

    grads = aspp_weight_grads(tg, x, proj_rows, filled)

    order = list(reversed(range(sections)))
    received = {}

    def input_of(k, tg):
        place = (section ^ k).reshape(1).astype(jnp.int32)
        return aspp_input_grad(place, cuts, tg, wt, pool_grad, pwt, sections, height, width)

    def sent(piece, k):
        return lax.ppermute(piece, "section", [(i, i ^ k) for i in range(sections)]) if k else piece

    share = lax.psum_scatter(grads, "dp", tiled=True)
    early, late = order[:len(order) // 2], order[len(order) // 2:]
    piece = input_of(early[0], tied(tg, grads))
    earlier = None
    mark = piece
    received[early[0]] = sent(piece, early[0])
    for g in range(groups):
        first = tied(saved[g][0], mark)
        earlier = decode_grads(g * group, (first,) + saved[g][1:], low_input, target, reduce_weight.T, class_weight.T, earlier)
        mark = earlier[0]
    packed, received[early[0]] = lax.optimization_barrier((earlier[0], received[early[0]]))
    steps = small_sum_steps()
    packed = steps.pop(0)(packed)
    for k in early[1:]:
        received[k] = input_of(k, tied(tg, packed))
    packed = steps.pop(0)(packed)
    held = tuple(received[k] for k in early)
    (share, packed), held = lax.optimization_barrier(((share, packed), held))
    received.update(zip(early, held))
    low_grad, logits = earlier[1:]

    summed = lax.all_gather(share, "dp", tiled=True)
    mark = share
    for k in early[1:]:
        received[k] = sent(received[k], k)
    for k in late:
        piece = input_of(k, tied(tg, mark))
        mark = piece
        received[k] = sent(piece, k)
        packed = tied(steps.pop(0)(packed), piece)
    while len(steps) > 2:
        packed = steps.pop(0)(packed)
    input_grad = sum(received[k].astype(f32) for k in order).reshape(batch, height, width, in_chans // sections)
    packed, input_grad = lax.optimization_barrier((packed, input_grad))
    for step in steps:
        packed = step(packed)
    merge1_grad, merge2_grad, reduce_grad, class_grad = unpack_decoder(packed, chans, red, classes)

    wide, pool_weight_grad, proj_weight_grad = unpack_weights(summed, taps * own, own, proj_rows.shape[0])
    sums = [s.reshape(2, group, -1) for s in sums]
    sums = sum(jnp.sum(s, axis=1) for s in sums)
    return (
        jnp.transpose(logits, (0, 2, 3, 1)),
        input_grad,
        low_grad,
        jnp.transpose(wide.reshape(taps, own, in_chans), (2, 0, 1)),
        pool_weight_grad.T,
        sums[0].reshape(branches, own),
        sums[1].reshape(branches, own),
        proj_weight_grad.reshape(branches, own, chans),
        reduce_grad,
        merge1_grad,
        merge2_grad,
        class_grad,
    )


def solution(mesh):
    return jax.shard_map(
        local,
        mesh=mesh,
        in_specs=(
            P("dp", None, None, None), P("dp", "section", None, None), P("dp", None, None), P("dp", None, None),
            P(None, None, "section"), P(None, "section"), P(None, "section"), P(None, "section"), P(None, "section", None),
            P(), P(), P(), P(), P("dp", "section", None, None),
        ),
        out_specs=(
            P("dp", "section", None, None), P("dp", None, None, "section"), P("dp", "section", None, None),
            P(None, None, "section"), P(None, "section"), P(None, "section"), P(None, "section"), P(None, "section", None),
            P(), P(), P(), P(),
        ),
        check_vma=False,
    )
```

```python
import jax
import jax.numpy as jnp
import numpy as np
from jax import lax
from jax.experimental import pallas as pl
from jax.experimental.pallas import tpu as pltpu
from jax.sharding import PartitionSpec as P

IMAGES = 2
bf16 = jnp.bfloat16
f32 = jnp.float32
HALO = 4
LANE = 128


def upsample_matrix(coarse_count):
    fine = np.arange(4 * coarse_count)
    coarse, phase = fine // 4, fine % 4
    near = np.where(phase < 2, 5 + 2 * phase, 11 - 2 * phase) / 8.0
    far = np.clip(np.where(phase < 2, coarse - 1, coarse + 1), 0, coarse_count - 1)
    matrix = np.zeros((4 * coarse_count, coarse_count), np.float32)
    np.add.at(matrix, (fine, coarse), near)
    np.add.at(matrix, (fine, far), 1.0 - near)
    return matrix


def split_rows(first, stop, target):
    count = stop - first
    pieces = -(-count // target)
    edges = [first + (count * k) // pieces for k in range(pieces + 1)]
    return [(edges[k], edges[k + 1] - edges[k]) for k in range(pieces)]


def silu_and_slope(v):
    s = 0.5 + 0.5 * jnp.tanh(0.5 * v)
    a = v * s
    return a, s * (1.0 + v - a)


def row_tables(ids_rows, section_index, own_rows, coarse_rows):
    fine_total = ids_rows.shape[1]
    window = own_rows + 2 * HALO
    slots = window + 1
    first = section_index * own_rows - HALO
    cut = jnp.sum((ids_rows == 0).astype(jnp.int32), axis=1)[:, None] - first
    gap = jnp.where((cut >= 1) & (cut < window), cut, window)
    slot = jnp.arange(slots, dtype=jnp.int32)[None, :]
    src = slot - (slot > gap).astype(jnp.int32)
    row = src + first
    valid = (slot != gap) & (row >= 0) & (row < fine_total)
    own = valid & (src >= HALO) & (src < own_rows + HALO)
    coarse = row // 4
    phase = row % 4
    near_weight = jnp.where(phase < 2, 5 + 2 * phase, 11 - 2 * phase).astype(f32) / 8.0
    far = jnp.clip(jnp.where(phase < 2, coarse - 1, coarse + 1), 0, coarse_rows - 1)
    base = section_index * (own_rows // 4) - 2
    held = own_rows // 4 + 4
    near_at = jnp.clip(coarse - base, 0, held - 1)
    far_at = jnp.clip(far - base, 0, held - 1)
    validf = valid.astype(f32)
    ownf = own.astype(f32)
    own_at = jnp.where(own, src - HALO, own_rows)
    slot_of = slot + (slot >= gap).astype(jnp.int32)
    inside = ((slot + first >= 0) & (slot + first < fine_total)).astype(f32)
    inside = jnp.broadcast_to(inside, validf.shape)
    ints = jnp.stack(
        [jnp.clip(src, 0, window - 1), near_at, far_at, own_at, slot_of, jnp.broadcast_to(gap, src.shape)], axis=1
    )
    floats = jnp.stack(
        [
            validf,
            ownf,
            near_weight * validf,
            (1.0 - near_weight) * validf,
            near_weight * ownf,
            (1.0 - near_weight) * ownf,
            inside,
        ],
        axis=1,
    )
    batch = ids_rows.shape[0]
    return ints.astype(jnp.int32).reshape(batch, -1), floats.reshape(batch, -1)


def column_sides(v):
    n = v.shape[0]
    col = lax.broadcasted_iota(jnp.int32, v.shape, 0)
    left = jnp.where(col == 0, 0.0, pltpu.roll(v, 1, 0))
    right = jnp.where(col == n - 1, 0.0, pltpu.roll(v, n - 1, 0))
    return left, right


def three_columns(v):
    left, right = column_sides(v)
    return jnp.concatenate([left.astype(bf16), v.astype(bf16), right.astype(bf16)], axis=1)


def decode_kernel(first, own_rows, cols, chans, red, parts, before, itab, ftab, low_top, low, low_end, tgt, colm, colt, rwt, m1, m2, clst, *refs):
    projs, refs = refs[:parts], refs[parts + before:]
    decode_body(first, own_rows, cols, chans, red, projs, itab, ftab, low_top, low, low_end, tgt, colm, colt, rwt, m1, m2, clst, *refs)


def decode_body(first, own_rows, cols, chans, red, projs, itab, ftab, low_top, low, low_end, tgt, colm, colt, rwt, m1, m2, clst,
                  up_h, red_h, fst_h, sec_h, g2_h, g1_h, rg_h, pg_o,
                  jc, fc, sl1, rs, tgg, lift, drop, a0, a1, b0, b1,
                w1, rw3, clsb, wb2, wb1u, wb1r, up_o, red_o, fst_o, sec_o, g2_o, g1_o, rg_o, sems):
    m = pl.program_id(0)
    window = own_rows + 2 * HALO
    slots = window + 1
    held = projs[0].shape[1]
    wide = 3 * chans
    redw = jc.shape[2] - wide
    keep = own_rows + 3
    gc2, gc1 = jc.at[:, :, 0:wide], fc
    held_rows = [(up_o, up_h), (red_o, red_h), (fst_o, fst_h), (sec_o, sec_h), (g2_o, g2_h), (g1_o, g1_h), (rg_o, rg_h)]

    def out_copy(k, at):
        here, there = held_rows[k]
        return pltpu.make_async_copy(here.at[0:there.shape[1]], there.at[first + at], sems.at[k])

    @pl.when(m > 0)
    def _():
        for k in range(6):
            out_copy(k, m - 1).wait()

    @pl.when(m == 0)
    def _():
        w1[:, wide + 3 * red:] = jnp.zeros((3, redw - 3 * red, chans), bf16)
        clsb[...] = jnp.zeros(clsb.shape, bf16)
        clsb[0:clst.shape[0]] = clst[...]
        spare = jnp.zeros((redw - 3 * red, chans), bf16)
        rw3[...] = jnp.concatenate([rwt[...]] * 3 + [spare], axis=0).T
        for r in range(3):
            for d in range(3):
                part = slice(d * chans, (d + 1) * chans)
                w1[r, part] = m1[3 * r + d, 0:chans]
                w1[r, wide + d * red:wide + (d + 1) * red] = m1[3 * r + d, chans:]
                tap = 3 * (2 - r) + 2 - d
                wb2[r, part] = m2[tap].T
                wb1u[r, part] = m1[tap, 0:chans].T
            tails = [m1[3 * (2 - r) + d, chans:] for d in range(3)]
            wb1r[r] = jnp.concatenate(tails + [spare], axis=0).T

    def w2(r):
        return m2[3 * r:3 * r + 3].reshape(wide, chans)

    def it(k, j):
        return itab[first + m, k * slots + j]

    def ft(k, j):
        return ftab[first + m, k * slots + j]

    accs = (a0, a1)
    bccs = (b0, b1)

    def staged(blocks, multiply, finish):
        for k, block in enumerate(blocks):
            multiply(*block, accs[k % 2], bccs[k % 2])
            if k:
                finish(*blocks[k - 1], accs[(k - 1) % 2], bccs[(k - 1) % 2])
        k = len(blocks) - 1
        finish(*blocks[k], accs[k % 2], bccs[k % 2])

    def rows_of(ref, lo, n):
        return ref[lo:lo + n].reshape(n * cols, ref.shape[2])

    def dot(a, b):
        return jnp.dot(a, b, preferred_element_type=f32)

    @pl.when(m == 0)
    def _():
        tgg[...] = jnp.zeros(tgg.shape, bf16)

    for i in range(2):
        tgg[it(4, 2 + i)] = low_top[0, HALO][:, i * LANE:(i + 1) * LANE]
        tgg[it(4, own_rows + HALO + i)] = low_end[0, HALO][:, i * LANE:(i + 1) * LANE]
    for i in range(own_rows):
        tgg[it(4, HALO + i)] = tgt[0, i]
    tgg[it(5, 0)] = jnp.zeros((cols, LANE), bf16)

    lane = lax.broadcasted_iota(jnp.int32, (cols, redw), 1)

    def reduce_mul(ref, lo, n, place, acc, _):
        acc[0:n * cols] = dot(ref[0, lo:lo + n].reshape(n * cols, ref.shape[3]), rw3[...])

    def reduce_fin(ref, lo, n, place, acc, _):
        for r in range(n):
            a, slope = silu_and_slope(acc[r * cols:(r + 1) * cols])
            a = a * ft(6, place + r)
            left, right = column_sides(a)
            a = jnp.where(lane < red, left, jnp.where(lane < 2 * red, a, right))
            jc[it(4, place + r), :, wide:] = a.astype(bf16)
            if HALO <= place + r < own_rows + HALO:
                rs[place + r - HALO] = slope.astype(bf16)

    staged(
        [(low_top, 0, HALO, 0)]
        + [(low, lo, n, lo + HALO) for lo, n in split_rows(0, own_rows, 8)]
        + [(low_end, 0, HALO, own_rows + HALO)],
        reduce_mul, reduce_fin,
    )
    jc[it(5, 0), :, wide:] = jnp.zeros((cols, redw), bf16)

    for k in range(held):
        v = sum(p[0, k].astype(f32) for p in projs).astype(bf16)
        lift[k] = dot(colm[...], v)
    for j in range(slots):
        v = (ft(2, j) * lift[it(1, j)] + ft(3, j) * lift[it(2, j)]).astype(bf16)
        for d in range(3):
            jc[j, :, d * chans:(d + 1) * chans] = v[d * cols:(d + 1) * cols]
        if 3 <= j < 3 + keep:
            up_o[j - 3] = v[cols:2 * cols]

    red_o[...] = jc[3:3 + keep, :, wide:]
    out_copy(0, m).start()
    out_copy(1, m).start()

    def first_mul(lo, n, acc, _):
        acc[0:n * cols] = (
            dot(rows_of(jc, lo - 1, n), w1[0]) + dot(rows_of(jc, lo, n), w1[1]) + dot(rows_of(jc, lo + 1, n), w1[2])
        )

    def first_fin(lo, n, acc, _):
        for r in range(n):
            a, slope = silu_and_slope(acc[r * cols:(r + 1) * cols])
            keep_row = ft(0, lo + r)
            a = a * keep_row
            fc[lo + r] = three_columns(a)
            if 3 <= lo + r < 3 + keep:
                fst_o[lo + r - 3] = a.astype(bf16)
            sl1[lo + r] = (slope * keep_row).astype(bf16)

    staged(split_rows(1, slots - 1, 8), first_mul, first_fin)
    out_copy(2, m).start()

    def second_mul(lo, n, acc, bcc):
        acc[0:n * cols] = (
            dot(rows_of(fc, lo - 1, n), w2(0)) + dot(rows_of(fc, lo, n), w2(1)) + dot(rows_of(fc, lo + 1, n), w2(2))
        )
        bcc[0:n * cols] = dot(rows_of(tgg, lo, n), clsb[...])

    def second_fin(lo, n, acc, bcc):
        for r in range(n):
            j = lo + r
            a, slope = silu_and_slope(acc[r * cols:(r + 1) * cols])
            sec_o[it(3, j)] = a.astype(bf16)
            g = bcc[r * cols:(r + 1) * cols] * slope * ft(0, j)
            gc2[j] = three_columns(g)
            if HALO <= j <= own_rows + HALO:
                g2_o[j - HALO] = (g * ft(1, j)).astype(bf16)

    staged(split_rows(2, slots - 2, 8), second_mul, second_fin)
    out_copy(3, m).start()
    out_copy(4, m).start()

    def back2_mul(lo, n, acc, _):
        acc[0:n * cols] = (
            dot(rows_of(gc2, lo - 1, n), wb2[0]) + dot(rows_of(gc2, lo, n), wb2[1]) + dot(rows_of(gc2, lo + 1, n), wb2[2])
        )

    def back2_fin(lo, n, acc, _):
        for r in range(n):
            j = lo + r
            g = acc[r * cols:(r + 1) * cols] * sl1[j].astype(f32)
            gc1[j] = three_columns(g)
            if HALO <= j <= own_rows + HALO:
                g1_o[j - HALO] = (g * ft(1, j)).astype(bf16)

    staged(split_rows(3, slots - 3, 8), back2_mul, back2_fin)
    out_copy(5, m).start()

    drop[...] = jnp.zeros(drop.shape, f32)

    @pl.when(m > 0)
    def _():
        out_copy(6, m - 1).wait()

    def back1_mul(lo, n, acc, bcc):
        acc[0:n * cols] = (
            dot(rows_of(gc1, lo - 1, n), wb1u[0]) + dot(rows_of(gc1, lo, n), wb1u[1]) + dot(rows_of(gc1, lo + 1, n), wb1u[2])
        )
        mid = slice(chans, 2 * chans)
        bcc[0:n * cols] = (
            dot(rows_of(gc1, lo - 1, n)[:, mid], wb1r[0]) + dot(rows_of(gc1, lo, n)[:, mid], wb1r[1])
            + dot(rows_of(gc1, lo + 1, n)[:, mid], wb1r[2])
        )

    def back1_fin(lo, n, acc, bcc):
        for r in range(n):
            j = lo + r
            up = acc[r * cols:(r + 1) * cols]
            near, far = it(1, j), it(2, j)
            drop[near] += ft(4, j) * up
            drop[far] += ft(5, j) * up
            t = bcc[r * cols:(r + 1) * cols]
            left, right = column_sides(t)
            t = jnp.where(lane < red, right, jnp.where(lane < 2 * red, t, left))
            rg_o[it(3, j)] = (t * rs[it(3, j)].astype(f32)).astype(bf16)

    staged(split_rows(HALO, slots - HALO, 8), back1_mul, back1_fin)
    out_copy(6, m).start()

    for k in range(held):
        pg_o[0, k] = dot(colt[...], drop[k].astype(bf16)).astype(bf16)

    @pl.when(m == pl.num_programs(0) - 1)
    def _():
        for k in range(7):
            out_copy(k, m).wait()


def whole(a):
    return pl.BlockSpec(a.shape, lambda *at: (0,) * a.ndim, pipeline_mode=pl.Buffered(1))


def per(shape, first=0):
    return pl.BlockSpec((1,) + shape, lambda m: (m + first,) + (0,) * len(shape))


def total(shape):
    return pl.BlockSpec(shape, lambda *at: (0,) * len(shape))


def params():
    return pltpu.CompilerParams(vmem_limit_bytes=63 * 2 ** 20)


def decode(first, batch, tables, low_top, low_input, low_end, projs, target, reduce_t, merge1_weight, merge2_weight, class_t, earlier):
    ints, floats = tables
    all_batch, own_rows, cols, low_ch = low_input.shape
    window = own_rows + 2 * HALO
    slots = window + 1
    chans = merge2_weight.shape[1]
    red = reduce_t.shape[0]
    held, coarse_cols = projs[0].shape[1], projs[0].shape[2]
    redw = -(-3 * red // LANE) * LANE
    wide = 3 * chans
    colm = upsample_matrix(coarse_cols)
    zero = np.zeros((1, coarse_cols), np.float32)
    colm3 = jnp.asarray(np.concatenate([zero, colm[:-1], colm, colm[1:], zero], axis=0), bf16)
    colt = jnp.asarray(colm.T, bf16)
    keep = own_rows + 3
    smem = pl.BlockSpec(memory_space=pltpu.SMEM)
    hbm = pl.BlockSpec(memory_space=pl.ANY)
    most = max(n for k in range(5) for _, n in split_rows(k, slots - k, 8))
    consts = (colm3, colt, reduce_t, merge1_weight, merge2_weight, class_t)
    shapes = [(keep, cols, chans), (keep, cols, redw), (keep, cols, chans), (own_rows, cols, chans),
              (own_rows + 1, cols, chans), (own_rows + 1, cols, chans), (own_rows, cols, redw)]
    stage = [(s[0] + (1 if k in (3, 6) else 0),) + s[1:] for k, s in enumerate(shapes)]
    back_shape = (held, coarse_cols, chans)
    saved = pl.pallas_call(
        lambda *refs: decode_kernel(first, own_rows, cols, chans, red, len(projs), len(earlier), *refs),
        grid=(batch,),
        in_specs=[smem, smem] + [per(a.shape[1:], first) for a in (low_top, low_input, low_end, target)]
        + [whole(a) for a in consts] + [per(p.shape[1:]) for p in projs] + [hbm] * len(earlier),
        out_specs=[hbm] * len(shapes) + [per(back_shape)],
        out_shape=[jax.ShapeDtypeStruct((all_batch,) + s, bf16) for s in shapes] + [jax.ShapeDtypeStruct((batch,) + back_shape, bf16)],
        input_output_aliases={6 + len(consts) + len(projs) + k: k for k in range(len(earlier))},
        scratch_shapes=[
            pltpu.VMEM((slots, cols, wide + redw), bf16), pltpu.VMEM((slots, cols, wide), bf16),
            pltpu.VMEM((slots, cols, chans), bf16), pltpu.VMEM((own_rows + 1, cols, redw), bf16),
            pltpu.VMEM((slots, cols, LANE), bf16),
            pltpu.VMEM((held, 3 * cols, chans), f32), pltpu.VMEM((held, cols, chans), f32),
            pltpu.VMEM((most * cols, chans), f32), pltpu.VMEM((most * cols, chans), f32),
            pltpu.VMEM((most * cols, chans), f32), pltpu.VMEM((most * cols, chans), f32),
            pltpu.VMEM((3, wide + redw, chans), bf16), pltpu.VMEM((low_ch, redw), bf16), pltpu.VMEM((LANE, chans), bf16),
            pltpu.VMEM((3, wide, chans), bf16), pltpu.VMEM((3, wide, chans), bf16), pltpu.VMEM((3, chans, redw), bf16),
        ] + [pltpu.VMEM(s, bf16) for s in stage] + [pltpu.SemaphoreType.DMA((7,))],
        compiler_params=params(),
        name="decode",
    )(ints, floats, low_top, low_input, low_end, target, *consts, *projs, *earlier)
    return saved[7], tuple(saved[:7])


def grads_kernel(own_rows, cols, chans, red, before, up, red3, fst, sec, g2, g1, rg, low, tgt, clst, rwt, *refs):
    earlier = refs[:before]
    packed, lowgrad, logits, o1, o2, oc, orr, upc, fcc = refs[before:]
    m = pl.program_id(0)
    keep = own_rows + 3
    wide = 3 * chans
    span = own_rows + 1
    classes = clst.shape[0]

    @pl.when(m == 0)
    def _():
        o1[...] = jnp.zeros(o1.shape, f32)
        o2[...] = jnp.zeros(o2.shape, f32)
        oc[...] = jnp.zeros(oc.shape, f32)
        orr[...] = jnp.zeros(orr.shape, f32)

    def tdot(a, b):
        return lax.dot_general(a, b, (((0,), (0,)), ((), ())), preferred_element_type=f32)

    for j in range(keep):
        upc[j] = three_columns(up[0, j].astype(f32))
    for j in range(keep):
        fcc[j] = three_columns(fst[0, j].astype(f32))

    def flat(v):
        return v.reshape(v.shape[0] * cols, v.shape[2])

    gg1 = flat(g1[0])
    for dy in range(3):
        o1[dy, 0:wide] += tdot(flat(upc[dy:dy + span]), gg1)
        o1[dy, wide:] += tdot(flat(red3[0, dy:dy + span]), gg1)
    gg2 = flat(g2[0])
    for dy in range(3):
        o2[dy] += tdot(flat(fcc[dy:dy + span]), gg2)
    oc[...] += tdot(flat(sec[0]), flat(tgt[0]))
    orr[...] += tdot(flat(low[0]), flat(rg[0]))
    spare = jnp.zeros((rg.shape[3] - 3 * red, chans), bf16)
    rb3 = jnp.concatenate([rwt[...]] * 3 + [spare], axis=0)
    for r in range(own_rows):
        lowgrad[0, r] = jnp.dot(rg[0, r], rb3, preferred_element_type=f32)
        lt = lax.dot_general(clst[...], sec[0, r], (((1,), (1,)), ((), ())), preferred_element_type=f32)
        logits[0, :, r] = lt

    @pl.when(m == pl.num_programs(0) - 1)
    def _():
        rows = chans + red
        for dy in range(3):
            for d in range(3):
                at = (3 * dy + d) * rows
                packed[at:at + chans] = o1[dy, d * chans:(d + 1) * chans].astype(bf16)
                packed[at + chans:at + rows] = o1[dy, wide + d * red:wide + (d + 1) * red].astype(bf16)
            packed[9 * rows + dy * wide:9 * rows + (dy + 1) * wide] = o2[dy].astype(bf16)
        at = 9 * rows + 3 * wide
        packed[at:] = jnp.zeros((packed.shape[0] - at, chans), bf16)
        t = orr[...].T
        packed[at:at + red] = (t[0:red] + t[red:2 * red] + t[2 * red:3 * red]).astype(bf16)
        packed[at + red:at + red + 32] = oc[...].T[0:32].astype(bf16)
        if before:
            packed[...] = (packed[...].astype(f32) + earlier[0][...].astype(f32)).astype(bf16)


def packed_rows(chans, red):
    return 9 * (chans + red) + 9 * chans + red + 32


def decode_grads(first, saved, low_input, target, reduce_t, class_t, earlier):
    up, red3, fst, sec, g2, g1, rg = saved
    batch = up.shape[0]
    all_batch, own_rows, cols, low_ch = low_input.shape
    chans = up.shape[3]
    redw = red3.shape[3]
    red = reduce_t.shape[0]
    classes = class_t.shape[0]
    wide = 3 * chans
    keep = own_rows + 3
    rows = packed_rows(chans, red)
    hbm = pl.BlockSpec(memory_space=pl.ANY)
    tots = [(3, wide + redw, chans), (3, wide, chans), (chans, LANE), (low_ch, redw)]
    pers = [(own_rows, cols, low_ch), (classes, own_rows, cols)]
    packed, lowgrad, logits = pl.pallas_call(
        lambda *refs: grads_kernel(own_rows, cols, chans, red, 3 if earlier else 0, *refs),
        grid=(batch,),
        in_specs=[per((keep, cols, chans)), per((keep, cols, redw)), per((keep, cols, chans)), per((own_rows, cols, chans)),
                  per((own_rows + 1, cols, chans)), per((own_rows + 1, cols, chans)), per((own_rows, cols, redw)),
                  per((own_rows, cols, low_ch), first), per(target.shape[1:], first), whole(class_t), whole(reduce_t)]
        + ([whole(earlier[0]), hbm, hbm] if earlier else []),
        out_specs=[total((rows, chans))] + [per(s, first) for s in pers],
        out_shape=[jax.ShapeDtypeStruct((rows, chans), bf16)] + [jax.ShapeDtypeStruct((all_batch,) + s, f32) for s in pers],
        input_output_aliases={12: 1, 13: 2} if earlier else {},
        scratch_shapes=[pltpu.VMEM(s, f32) for s in tots]
        + [pltpu.VMEM((keep, cols, wide), bf16), pltpu.VMEM((keep, cols, wide), bf16)],
        compiler_params=params(),
        name="decode_grads",
        cost_estimate=pl.CostEstimate(flops=1, bytes_accessed=1, transcendentals=1),
    )(up, red3, fst, sec, g2, g1, rg, low_input, target, class_t, reduce_t, *(earlier or ()))
    return packed, lowgrad, logits


def unpack_decoder(packed, chans, red, classes):
    rows = chans + red
    at = 9 * rows + 9 * chans
    shapes = [(9, rows, chans), (9, chans, chans), (red, chans), (classes, chans)]

    def kernel(v, m1, m2, rw, cw):
        for t in range(9):
            m1[t] = v[t * rows:(t + 1) * rows].astype(f32)
            m2[t] = v[9 * rows + t * chans:9 * rows + (t + 1) * chans].astype(f32)
        rw[...] = v[at:at + red].astype(f32)
        cw[...] = v[at + red:at + red + 32].astype(f32)[0:classes]

    m1, m2, rw, cw = pl.pallas_call(
        kernel,
        grid=(1,),
        in_specs=[whole(packed)],
        out_specs=[total(s) for s in shapes],
        out_shape=[jax.ShapeDtypeStruct(s, f32) for s in shapes],
        compiler_params=params(),
        name="unpack_decoder",
    )(packed)
    return m1, m2, rw.T, cw.T


atrous_rates = (6, 12, 18)
epsilon = 1e-05


def tap_list():
    listed = [(0, 0, 0)]
    for branch_index, rate_value in enumerate(atrous_rates):
        for step_rows in (-1, 0, 1):
            for step_cols in (-1, 0, 1):
                listed.append((rate_value * step_rows, rate_value * step_cols, branch_index + 1))
    return listed


def pixel_places(batch, height, width):
    pixel = np.arange(height * width)
    places = np.stack([np.tile(pixel // width, batch), np.tile(pixel % width, batch), np.repeat(np.arange(batch), height * width)])
    return jnp.asarray(np.pad(places, ((0, 5), (0, 0))), jnp.int32)


class Pixels:
    def __init__(self, places, cuts, batch, height, width):
        self.row, self.col, self.canvas = places[0:1], places[1:2], places[2:3]
        self.height, self.width = height, width
        cut = jnp.full(self.row.shape, cuts[0], jnp.int32)
        for m in range(1, batch):
            cut = jnp.where(self.canvas == m, cuts[m], cut)
        self.cut = cut
        self.band = self.row >= cut

    def valid(self, dr, dc):
        row, col = self.row + dr, self.col + dc
        inside = (row >= 0) & (row < self.height) & (col >= 0) & (col < self.width)
        same = jnp.where(row >= self.cut, 1, 0) == jnp.where(self.band, 1, 0)
        return jnp.where(inside & same, 1.0, 0.0)

    def image(self):
        return IMAGES * self.canvas + jnp.where(self.band, 1, 0)


def image_counts(cuts, batch, height, width):
    index = lax.broadcasted_iota(jnp.int32, (IMAGES * batch, 1), 0)
    out = jnp.zeros((IMAGES * batch, 1), f32)
    for m in range(batch):
        first = cuts[m] * width
        out = jnp.where(index == IMAGES * m, first.astype(f32), out)
        out = jnp.where(index == IMAGES * m + 1, (height * width - first).astype(f32), out)
    return jnp.maximum(out, 1.0)


def branch_kernel(taps, batch, height, width, cuts, x, w, places, pw, br_o, mom_o, pooled_o, y, pool, mom):
    i = pl.program_id(0)
    last = pl.num_programs(0) - 1
    block = x.shape[0]
    total = y.shape[1]
    pixels = total // batch
    own = pw.shape[0]
    at = pl.multiple_of(i * block, block)

    @pl.when(i == 0)
    def _():
        pool[...] = jnp.zeros(pool.shape, f32)
        mom[...] = jnp.zeros(mom.shape, f32)

    def nt(a, b):
        return lax.dot_general(a, b, (((1,), (1,)), ((), ())), preferred_element_type=f32)

    canvas, row = places[2:3, pl.ds(at, block)], places[0:1, pl.ds(at, block)]
    cut = jnp.full(row.shape, cuts[0], jnp.int32)
    for m in range(1, batch):
        cut = jnp.where(canvas == m, cuts[m], cut)
    image = IMAGES * canvas + jnp.where(row >= cut, 1, 0)
    index = lax.broadcasted_iota(jnp.int32, (IMAGES * batch, block), 0)
    member = jnp.where(image == index, 1.0, 0.0).astype(bf16)
    pool[...] += jnp.dot(member, x[...], preferred_element_type=f32)

    @pl.when(i < last)
    def _():
        y[:, pl.ds(at, block)] = nt(w[...], x[...])

    def keep(m, b, v):
        part = slice(b * own, (b + 1) * own)
        br_o[m, part] = v
        mom[part, m:m + 1] = jnp.sum(v, axis=1, keepdims=True)
        mom[part, batch + m:batch + m + 1] = jnp.sum(v * v, axis=1, keepdims=True)

    @pl.when(i == last)
    def _():
        px = Pixels(places, cuts, batch, height, width)
        spans = []
        for b in range(4):
            mine = [t for t, tap in enumerate(taps) if tap[2] == b]
            spans.append((mine[0], mine[-1] + 1))

        def multiply(b):
            lo, hi = spans[b][0] * own, spans[b][1] * own
            y[lo:hi, total - block:] = nt(w[lo:hi], x[...])

        def finish(b):
            acc = None
            for t in range(*spans[b]):
                dr, dc, _ = taps[t]
                v = y[t * own:(t + 1) * own]
                shift = dr * width + dc
                if shift:
                    v = pltpu.roll(v, (-shift) % total, 1) * px.valid(dr, dc)
                acc = v if acc is None else acc + v
            for m in range(batch):
                keep(m, b, acc[:, m * pixels:(m + 1) * pixels])

        multiply(0)
        multiply(1)
        multiply(2)
        finish(0)
        finish(1)
        multiply(3)
        finish(2)
        finish(3)
        pooled = (pool[...] / image_counts(cuts, batch, height, width)).astype(bf16)
        pooled_o[...] = pooled
        po = nt(pw[...], pooled)
        for m in range(batch):
            band = px.band[:, m * pixels:(m + 1) * pixels]
            keep(m, 4, jnp.where(band, po[:, IMAGES * m + 1:IMAGES * m + 2], po[:, IMAGES * m:IMAGES * m + 1]))
        mom_o[...] = mom[...].T[0:mom_o.shape[0]]


def aspp_forward(cuts, x, wt, pwt, batch, height, width):
    all_pixels, in_chans = x.shape
    pixels = height * width
    own = pwt.shape[0]
    taps = tap_list()
    block = all_pixels // 3 if all_pixels % 3 == 0 and (all_pixels // 3) % LANE == 0 else all_pixels
    places = pixel_places(batch, height, width)
    outs = [((batch, 5 * own, pixels), f32), ((2 * batch, 5 * own), f32), ((IMAGES * batch, in_chans), bf16)]
    return pl.pallas_call(
        lambda *refs: branch_kernel(taps, batch, height, width, *refs),
        grid=(all_pixels // block,),
        in_specs=[pl.BlockSpec(memory_space=pltpu.SMEM), pl.BlockSpec((block, in_chans), lambda i: (i, 0)),
                  whole(wt), whole(places), whole(pwt)],
        out_specs=[total(s) for s, _ in outs],
        out_shape=[jax.ShapeDtypeStruct(s, d) for s, d in outs],
        scratch_shapes=[pltpu.VMEM((len(taps) * own, all_pixels), f32), pltpu.VMEM((IMAGES * batch, in_chans), f32),
                        pltpu.VMEM((5 * own, LANE), f32)],
        compiler_params=params(),
        name="aspp_forward",
    )(cuts, x, wt, places, pwt)


def norm_columns(stats, scale, m, batch, count):
    t = stats[...].T
    mean = t[:, m:m + 1] / count
    inv_std = lax.rsqrt(t[:, batch + m:batch + m + 1] / count - mean * mean + epsilon)
    s = scale[...].T
    half = s.shape[1] // 2
    gain = jnp.concatenate([s[:, k:k + 1] for k in range(half)], axis=0)
    shift = jnp.concatenate([s[:, half + k:half + k + 1] for k in range(half)], axis=0)
    return mean, inv_std, gain, shift


def project_kernel(first, group, count, coarse_rows, offsets, br, stats, scale, proj, *refs):
    outs, rows = refs[:-1], refs[-1]
    batch = stats.shape[0] // 2
    height, width, chans = rows.shape[0] - 4, rows.shape[1], rows.shape[2]
    held = coarse_rows + 4
    rows[0:2] = jnp.zeros((2, width, chans), f32)
    rows[height + 2:] = jnp.zeros((2, width, chans), f32)
    for at in range(group):
        mean, inv_std, gain, shift = norm_columns(stats, scale, first + at, batch, count)
        active, _ = silu_and_slope((br[at] - mean) * inv_std * gain + shift)
        partial = lax.dot_general(active.astype(bf16), proj[...], (((0,), (0,)), ((), ())), preferred_element_type=f32)
        rows[2:height + 2] = partial.reshape(height, width, chans)
        for k, o in enumerate(outs):
            o[at] = rows[pl.ds(offsets[k], held)].astype(bf16)


def project(first, group, offsets, br, stats, scale, proj, count, coarse_rows, parts, height, width):
    chans = proj.shape[1]
    shape = (group, coarse_rows + 4, width, chans)
    pixels = br.shape[2]
    return pl.pallas_call(
        lambda *refs: project_kernel(first, group, count, coarse_rows, *refs),
        grid=(1,),
        in_specs=[pl.BlockSpec(memory_space=pltpu.SMEM), pl.BlockSpec((pl.Element(group), pl.Element(br.shape[1]), pl.Element(pixels)), lambda i: (first, 0, 0)),
                  whole(stats), whole(scale), whole(proj)],
        out_specs=[total(shape)] * parts,
        out_shape=[jax.ShapeDtypeStruct(shape, bf16)] * parts,
        scratch_shapes=[pltpu.VMEM((height + 4, width, chans), f32)],
        compiler_params=params(),
        name="project",
    )(offsets, br, stats, scale, proj)


def norm_back_kernel(first, count, parts, offsets, br, stats, scale, proj, earlier, sums_before, *refs):
    pieces = refs[:parts]
    grad_o, sums_o, projgrad_o, rows, sums = refs[parts:]
    height, width, chans = rows.shape[0] - 4, rows.shape[1], rows.shape[2]
    group, held = pieces[0].shape[0], pieces[0].shape[1]
    batch = stats.shape[0] // 2
    sums[...] = jnp.zeros(sums.shape, f32)
    projgrad = earlier[...]
    for at in range(group):
        m = first + at
        rows[...] = jnp.zeros(rows.shape, f32)
        for k, piece in enumerate(pieces):
            rows[pl.ds(offsets[k], held)] += piece[at].astype(f32)
        grad = rows[2:height + 2].reshape(height * width, chans).astype(bf16)
        mean, inv_std, gain, shift = norm_columns(stats, scale, m, batch, count)
        scaled = (br[at] - mean) * inv_std
        active, slope = silu_and_slope(scaled * gain + shift)
        back = lax.dot_general(proj[...], grad, (((1,), (1,)), ((), ())), preferred_element_type=f32) * slope
        grad_o[at] = back
        sums[:, m:m + 1] = jnp.sum(back * scaled, axis=1, keepdims=True)
        sums[:, batch + m:batch + m + 1] = jnp.sum(back, axis=1, keepdims=True)
        projgrad = projgrad + jnp.dot(active.astype(bf16), grad, preferred_element_type=f32)
    projgrad_o[...] = projgrad
    sums_o[...] = sums_before[...] + sums[...].T[0:sums_o.shape[0]]


def norm_back(first, offsets, br, stats, scale, proj, earlier, sums_before, pieces, count, height, width):
    batch, chans5, pixels = br.shape
    group = pieces[0].shape[0]
    outs = [((group, chans5, pixels), f32), (stats.shape, f32), (proj.shape, f32)]
    return pl.pallas_call(
        lambda *refs: norm_back_kernel(first, count, len(pieces), *refs),
        grid=(1,),
        in_specs=[pl.BlockSpec(memory_space=pltpu.SMEM), pl.BlockSpec((pl.Element(group), pl.Element(chans5), pl.Element(pixels)), lambda i: (first, 0, 0)),
                  whole(stats), whole(scale), whole(proj), whole(earlier), whole(sums_before)] + [whole(p) for p in pieces],
        out_specs=[total(s) for s, _ in outs],
        out_shape=[jax.ShapeDtypeStruct(s, d) for s, d in outs],
        scratch_shapes=[pltpu.VMEM((height + 4, width, proj.shape[1]), f32), pltpu.VMEM((chans5, LANE), f32)],
        compiler_params=params(),
        name="norm_back",
    )(offsets, br, stats, scale, proj, earlier, sums_before, *pieces)


def weight_grad_kernel(taps, groups, height, width, count, cuts, br, stats, scale, sums, places, projgrad, x_hbm, *refs):
    backs = refs[:groups]
    wg_hbm, tg_hbm, pg_o, both, x, tg, wg, sems = refs[groups:]
    batch = br.shape[0]
    owner = [(g, k) for g, back in enumerate(backs) for k in range(back.shape[0])]
    own = pg_o.shape[0]
    pixels = br.shape[2]
    rows, all_pixels = tg.shape
    in_chans = x.shape[1]
    filled = (len(taps) + 1) * own
    x_copy = pltpu.make_async_copy(x_hbm, x, sems.at[0])
    x_copy.start()
    px = Pixels(places, cuts, batch, height, width)
    pool_grad = jnp.zeros((own, LANE), f32)
    lane = lax.broadcasted_iota(jnp.int32, (own, LANE), 1)
    t = sums[...].T
    for m, (g, k) in enumerate(owner):
        mean, inv_std, gain, _ = norm_columns(stats, scale, m, batch, count)
        gain_sum, shift_sum = t[:, m:m + 1], t[:, batch + m:batch + m + 1]
        scaled = (br[m] - mean) * inv_std
        grad = inv_std * gain * (backs[g][k] - (shift_sum + scaled * gain_sum) / count)
        both[0:4 * own, m * pixels:(m + 1) * pixels] = grad[0:4 * own]
        pool = grad[4 * own:]
        band = px.band[:, m * pixels:(m + 1) * pixels]
        upper = jnp.sum(jnp.where(band, 0.0, pool), axis=1, keepdims=True).astype(bf16).astype(f32)
        lower = jnp.sum(jnp.where(band, pool, 0.0), axis=1, keepdims=True).astype(bf16).astype(f32)
        pool_grad = jnp.where(lane == IMAGES * m, upper, pool_grad)
        pool_grad = jnp.where(lane == IMAGES * m + 1, lower, pool_grad)
        many = (cuts[m] * width).astype(f32)
        spread = jnp.where(band, lower / jnp.maximum(height * width - many, 1.0), upper / jnp.maximum(many, 1.0))
        both[4 * own:, m * pixels:(m + 1) * pixels] = spread
    pg_o[...] = pool_grad[:, 0:pg_o.shape[1]].astype(bf16)

    pieces = 3
    each = -(-(rows // own) // pieces)
    edges = [min(p * each * own, rows) for p in range(pieces)] + [rows]

    def build(p):
        for k in range(p * each, min((p + 1) * each, len(taps))):
            dr, dc, b = taps[k]
            v = both[b * own:(b + 1) * own]
            shift = dr * width + dc
            if shift:
                v = pltpu.roll(v * px.valid(dr, dc), shift % all_pixels, 1)
            tg[k * own:(k + 1) * own] = v.astype(bf16)
        if p == pieces - 1:
            tg[filled - own:filled] = both[4 * own:].astype(bf16)
            tg[filled:] = jnp.zeros((rows - filled, all_pixels), bf16)
        copy = pltpu.make_async_copy(tg.at[edges[p]:edges[p + 1]], tg_hbm.at[edges[p]:edges[p + 1]], sems.at[1 + p])
        copy.start()
        return copy

    def multiply(p):
        part = slice(edges[p], edges[p + 1])
        step = 512 if in_chans % 512 == 0 else in_chans
        for n in range(0, in_chans, step):
            wg[part, n:n + step] = jnp.dot(tg[part], x[:, n:n + step], preferred_element_type=f32).astype(bf16)
        if p == pieces - 1:
            chans = projgrad.shape[1]
            some = projgrad.shape[0] * chans // in_chans
            for k in range(in_chans // chans):
                wg[filled:filled + some, k * chans:(k + 1) * chans] = projgrad[k * some:(k + 1) * some].astype(bf16)
        copy = pltpu.make_async_copy(wg.at[part], wg_hbm.at[part], sems.at[1 + pieces + p])
        copy.start()
        return copy

    copies = [build(0)]
    x_copy.wait()
    for p in range(pieces):
        copies.append(multiply(p))
        if p + 1 < pieces:
            copies.append(build(p + 1))
    for copy in copies:
        copy.wait()


def aspp_weight_grads(rows, cuts, x, br, stats, scale, sums, projgrad, backs, count, height, width):
    all_pixels, in_chans = x.shape
    batch, chans5, pixels = br.shape
    own = chans5 // 5
    places = pixel_places(batch, height, width)
    groups = len(backs)
    hbm = pl.BlockSpec(memory_space=pl.ANY)
    outs = [(rows, in_chans), (rows, all_pixels), (own, IMAGES * batch)]
    return pl.pallas_call(
        lambda *refs: weight_grad_kernel(tap_list(), groups, height, width, count, *refs),
        grid=(1,),
        in_specs=[pl.BlockSpec(memory_space=pltpu.SMEM)] + [whole(v) for v in (br, stats, scale, sums, places, projgrad)]
        + [hbm] + [whole(v) for v in backs],
        out_specs=[hbm, hbm, total(outs[2])],
        out_shape=[jax.ShapeDtypeStruct(s, bf16) for s in outs],
        scratch_shapes=[pltpu.VMEM((chans5, all_pixels), f32), pltpu.VMEM((all_pixels, in_chans), bf16),
                        pltpu.VMEM((rows, all_pixels), bf16), pltpu.VMEM((rows, in_chans), bf16),
                        pltpu.SemaphoreType.DMA((7,))],
        compiler_params=params(),
        name="aspp_weight_grads",
    )(cuts, br, stats, scale, sums, places, projgrad, x, *backs)


def unpack_weights(summed, wide, own, proj_shape):
    rows, in_chans = summed.shape
    block = 512 if in_chans % 512 == 0 else in_chans
    chans = proj_shape[1]
    pieces = block // chans
    some = proj_shape[0] * chans // in_chans

    def kernel(v, wide_o, pool_o, proj_o):
        wide_o[...] = v[0:wide].astype(f32)
        pool_o[...] = v[wide:wide + own].astype(f32)
        tail = v[wide + own:].astype(f32)
        for k in range(pieces):
            proj_o[k * some:(k + 1) * some] = tail[0:some, k * chans:(k + 1) * chans]

    def lanes(a):
        return pl.BlockSpec((a, block), lambda j: (0, j))

    return pl.pallas_call(
        kernel,
        grid=(in_chans // block,),
        in_specs=[lanes(rows)],
        out_specs=[lanes(wide), lanes(own), pl.BlockSpec((some * pieces, chans), lambda j: (j, 0))],
        out_shape=[jax.ShapeDtypeStruct(s, f32) for s in ((wide, in_chans), (own, in_chans), proj_shape)],
        compiler_params=params(),
        name="unpack_weights",
    )(summed)


def input_grad_kernel(batch, span, height, width, at, cuts, tg, w, pg, pw, band, o):
    i = pl.program_id(0)
    pixels = height * width
    v = lax.dot_general(tg[...], w[...], (((0,), (0,)), ((), ())), preferred_element_type=f32)
    image = lax.dot_general(pg[...], pw[...], (((0,), (0,)), ((), ())), preferred_element_type=f32)
    image = image / image_counts(cuts, batch, height, width)
    index = lax.broadcasted_iota(jnp.int32, (IMAGES * batch, 1), 0)
    row = band[...]
    for k in range(span):
        m = i * span + k
        first = jnp.sum(jnp.where(index == IMAGES * m, image, 0.0), axis=0, keepdims=True)
        second = jnp.sum(jnp.where(index == IMAGES * m + 1, image, 0.0), axis=0, keepdims=True)
        part = slice(k * pixels, (k + 1) * pixels)
        o[part] = (v[part] + jnp.where(row >= cuts[m], second, first)).astype(bf16)


def aspp_input_grad(place, cuts, tg, wt, pool_grad, pwt, parts, height, width):
    rows, in_chans = wt.shape
    all_pixels = tg.shape[1]
    own = pwt.shape[0]
    pixels = height * width
    batch = all_pixels // pixels
    block = in_chans // parts
    span = 2 if (2 * pixels) % LANE == 0 and batch % 2 == 0 else batch
    row_column = jnp.asarray(np.arange(pixels)[:, None] // width, jnp.int32)
    return pl.pallas_call(
        lambda *refs: input_grad_kernel(batch, span, height, width, *refs),
        grid_spec=pltpu.PrefetchScalarGridSpec(
            num_scalar_prefetch=2,
            grid=(batch // span,),
            in_specs=[
                pl.BlockSpec((rows, span * pixels), lambda i, at, cuts: (0, i)),
                pl.BlockSpec((rows, block), lambda i, at, cuts: (0, at[0])),
                whole(pool_grad),
                pl.BlockSpec((own, block), lambda i, at, cuts: (0, at[0])),
                whole(row_column),
            ],
            out_specs=pl.BlockSpec((span * pixels, block), lambda i, at, cuts: (i, 0)),
        ),
        out_shape=jax.ShapeDtypeStruct((all_pixels, block), bf16),
        compiler_params=params(),
        name="aspp_input_grad",
        cost_estimate=pl.CostEstimate(flops=1, bytes_accessed=1, transcendentals=1),
    )(place, cuts, tg, wt, pool_grad, pwt, row_column)


def doubled_sum(value, axis):
    size = lax.axis_size(axis)
    step = 1
    while step < size:
        value = value + lax.ppermute(value, axis, [(i, i ^ step) for i in range(size)])
        step *= 2
    return value


def exchanged(pieces, axis):
    size = lax.axis_size(axis)
    return [pieces[0]] + [lax.ppermute(pieces[k], axis, [(i, i ^ k) for i in range(size)]) for k in range(1, size)]


def added(a, b):
    return (a.astype(f32) + b.astype(f32)).astype(bf16)


def distances(axis):
    size = lax.axis_size(axis)
    return [1 << k for k in range(size.bit_length() - 1)]


def halve(value, axis, step):
    bit = (lax.axis_index(axis) // step) % 2
    half = value.shape[0] // 2
    mine = lax.dynamic_slice_in_dim(value, bit * half, half, 0)
    other = lax.dynamic_slice_in_dim(value, (1 - bit) * half, half, 0)
    return added(mine, lax.ppermute(other, axis, [(i, i ^ step) for i in range(lax.axis_size(axis))]))


def join(value, axis, step):
    bit = (lax.axis_index(axis) // step) % 2
    other = lax.ppermute(value, axis, [(i, i ^ step) for i in range(lax.axis_size(axis))])
    return jnp.where(bit == 0, jnp.concatenate([value, other]), jnp.concatenate([other, value]))


def small_sum_steps():
    order = [("dp", 1)] + [("section", d) for d in distances("section")] + [("dp", d) for d in distances("dp")[1:]]
    steps = [lambda v, a=a, d=d: halve(v, a, d) for a, d in order]
    steps += [lambda v, a=a, d=d: join(v, a, d) for a, d in reversed(order)]
    return steps


def tied(value, *others):
    return lax.optimization_barrier((value,) + others)[0]


def local(aspp_input, low_input, aspp_ids, low_ids, aspp_weight, pool_weight, bn_gain, bn_shift, projection_matrix,
          reduce_weight, merge1_weight, merge2_weight, class_weight, logit_grad):
    section = lax.axis_index("section")
    sections = lax.axis_size("section")
    batch, height, width, in_chans = aspp_input.shape
    taps, own = aspp_weight.shape[1], aspp_weight.shape[2]
    branches = bn_gain.shape[0]
    chans = projection_matrix.shape[2]
    red = reduce_weight.shape[1]
    classes = class_weight.shape[1]
    fine_rows, fine_cols = low_input.shape[1], low_input.shape[2]
    pixels = height * width
    count = pixels * lax.axis_size("dp")
    coarse_rows = fine_rows // 4
    groups = [(0, batch // 2), (batch // 2, batch - batch // 2)]

    x = aspp_input.reshape(batch * pixels, in_chans)
    wt = jnp.transpose(aspp_weight, (1, 2, 0)).reshape(taps * own, in_chans)
    pwt = pool_weight.T
    proj = projection_matrix.reshape(branches * own, chans)
    cuts = jnp.sum((aspp_ids[:, :, 0] == 0).astype(jnp.int32), axis=1)
    br, moments, pooled = aspp_forward(cuts, x, wt, pwt, batch, height, width)

    down = [(i, i + 1) for i in range(sections - 1)]
    up = [(i + 1, i) for i in range(sections - 1)]
    target = jnp.pad(logit_grad, ((0, 0), (0, 0), (0, 0), (0, LANE - classes)))

    def rim(low_rows, target_rows):
        paired = jnp.concatenate([target_rows[:, 0:1], target_rows[:, 1:2]], axis=3)
        return jnp.concatenate([low_rows, paired], axis=1)

    top = lax.ppermute(rim(low_input[:, -HALO:], target[:, -2:]), "section", down)
    end = lax.ppermute(rim(low_input[:, :HALO], target[:, :2]), "section", up)
    tables = row_tables(low_ids[:, :, 0], section, fine_rows, height)
    distance = jnp.arange(sections, dtype=jnp.int32)
    offsets = (section ^ distance) * coarse_rows

    stats = doubled_sum(moments, "dp")
    scale = jnp.concatenate([bn_gain, bn_shift], axis=0)
    projs = []
    for first, size in groups:
        parts = project(first, size, offsets, br, stats, scale, proj, count, coarse_rows, sections, height, width)
        projs.append(exchanged(parts, "section"))
    saved, pieces = (), []
    for g, (first, size) in enumerate(groups):
        pgrad, saved = decode(first, size, tables, top, low_input, end, projs[g], target, reduce_weight.T,
                              merge1_weight, merge2_weight, class_weight.T, saved)
        pieces.append(exchanged([pgrad] * sections, "section"))
    backs = []
    projgrad, sums = jnp.zeros(proj.shape, f32), jnp.zeros(stats.shape, f32)
    for (first, size), piece in zip(groups, pieces):
        back, sums, projgrad = norm_back(first, offsets, br, stats, scale, proj, projgrad, sums, piece, count, height, width)
        backs.append(back)
    sums = doubled_sum(sums, "dp")
    filled = (taps + 1) * own
    rows = -(-(filled + projgrad.size // in_chans) // 32) * 32
    grads, tg, pool_grad = aspp_weight_grads(rows, cuts, x, br, stats, scale, sums, projgrad, backs, count, height, width)

    order = list(reversed(range(sections)))
    received = {}

    def input_of(k, tg):
        place = (section ^ k).reshape(1).astype(jnp.int32)
        return aspp_input_grad(place, cuts, tg, wt, pool_grad, pwt, sections, height, width)

    def sent(piece, k):
        return lax.ppermute(piece, "section", [(i, i ^ k) for i in range(sections)]) if k else piece

    share = lax.psum_scatter(grads, "dp", tiled=True)
    early, late = order[:len(order) // 2], order[len(order) // 2:]
    piece = input_of(early[0], tied(tg, grads))
    far = sent(piece, early[0])
    first = tied(saved[0], piece)
    packed, low_grad, logits = decode_grads(0, (first,) + saved[1:], low_input, target, reduce_weight.T, class_weight.T, None)
    steps = small_sum_steps()
    packed = steps.pop(0)(packed)
    packed, far, tied_tg = lax.optimization_barrier((packed, far, tg))
    packed = steps.pop(0)(packed)
    received[early[0]] = far
    for k in early[1:]:
        received[k] = input_of(k, tied_tg)
        packed = tied(packed, received[k])
    for _ in distances("section")[1:]:
        packed = steps.pop(0)(packed)
    held = tuple(received[k] for k in early)
    (share, packed), held = lax.optimization_barrier(((share, packed), held))
    received.update(zip(early, held))

    summed = lax.all_gather(share, "dp", tiled=True)
    for k in early[1:]:
        received[k] = sent(received[k], k)
    for k in late:
        packed, tied_tg = lax.optimization_barrier((packed, tg) + ((piece,) if k != late[0] else ()))[:2]
        piece = input_of(k, tied_tg)
        packed = steps.pop(0)(packed)
        packed, piece = lax.optimization_barrier((packed, piece))
        received[k] = sent(piece, k)
    while len(steps) > 1:
        packed = steps.pop(0)(packed)
    input_grad = sum(received[k].astype(f32) for k in order).reshape(batch, height, width, in_chans // sections)
    packed, summed, input_grad = lax.optimization_barrier((packed, summed, input_grad))
    packed = steps.pop(0)(packed)
    merge1_grad, merge2_grad, reduce_grad, class_grad = unpack_decoder(packed, chans, red, classes)

    wide, pool_weight_grad, proj_weight_grad = unpack_weights(summed, taps * own, own, proj.shape)
    sums = jnp.sum(sums.reshape(2, batch, -1), axis=1)
    return (
        jnp.transpose(logits, (0, 2, 3, 1)),
        input_grad,
        low_grad,
        jnp.transpose(wide.reshape(taps, own, in_chans), (2, 0, 1)),
        pool_weight_grad.T,
        sums[0].reshape(branches, own),
        sums[1].reshape(branches, own),
        proj_weight_grad.reshape(branches, own, chans),
        reduce_grad,
        merge1_grad,
        merge2_grad,
        class_grad,
    )


def solution(mesh):
    return jax.shard_map(
        local,
        mesh=mesh,
        in_specs=(
            P("dp", None, None, None), P("dp", "section", None, None), P("dp", None, None), P("dp", None, None),
            P(None, None, "section"), P(None, "section"), P(None, "section"), P(None, "section"), P(None, "section", None),
            P(), P(), P(), P(), P("dp", "section", None, None),
        ),
        out_specs=(
            P("dp", "section", None, None), P("dp", None, None, "section"), P("dp", "section", None, None),
            P(None, None, "section"), P(None, "section"), P(None, "section"), P(None, "section"), P(None, "section", None),
            P(), P(), P(), P(),
        ),
        check_vma=False,
    )
```

```python
import jax
import jax.numpy as jnp
import numpy as np
from jax import lax
from jax.experimental import pallas as pl
from jax.experimental.pallas import tpu as pltpu
from jax.sharding import PartitionSpec as P

IMAGES = 2
bf16 = jnp.bfloat16
f32 = jnp.float32
HALO = 4
LANE = 128


def upsample_matrix(coarse_count):
    fine = np.arange(4 * coarse_count)
    coarse, phase = fine // 4, fine % 4
    near = np.where(phase < 2, 5 + 2 * phase, 11 - 2 * phase) / 8.0
    far = np.clip(np.where(phase < 2, coarse - 1, coarse + 1), 0, coarse_count - 1)
    matrix = np.zeros((4 * coarse_count, coarse_count), np.float32)
    np.add.at(matrix, (fine, coarse), near)
    np.add.at(matrix, (fine, far), 1.0 - near)
    return matrix


def split_rows(first, stop, target):
    count = stop - first
    pieces = -(-count // target)
    edges = [first + (count * k) // pieces for k in range(pieces + 1)]
    return [(edges[k], edges[k + 1] - edges[k]) for k in range(pieces)]


def silu_and_slope(v):
    s = 0.5 + 0.5 * jnp.tanh(0.5 * v)
    a = v * s
    return a, s * (1.0 + v - a)


def row_tables(ids_rows, section_index, own_rows, coarse_rows):
    fine_total = ids_rows.shape[1]
    window = own_rows + 2 * HALO
    slots = window + 1
    first = section_index * own_rows - HALO
    cut = jnp.sum((ids_rows == 0).astype(jnp.int32), axis=1)[:, None] - first
    gap = jnp.where((cut >= 1) & (cut < window), cut, window)
    slot = jnp.arange(slots, dtype=jnp.int32)[None, :]
    src = slot - (slot > gap).astype(jnp.int32)
    row = src + first
    valid = (slot != gap) & (row >= 0) & (row < fine_total)
    own = valid & (src >= HALO) & (src < own_rows + HALO)
    coarse = row // 4
    phase = row % 4
    near_weight = jnp.where(phase < 2, 5 + 2 * phase, 11 - 2 * phase).astype(f32) / 8.0
    far = jnp.clip(jnp.where(phase < 2, coarse - 1, coarse + 1), 0, coarse_rows - 1)
    base = section_index * (own_rows // 4) - 2
    held = own_rows // 4 + 4
    near_at = jnp.clip(coarse - base, 0, held - 1)
    far_at = jnp.clip(far - base, 0, held - 1)
    validf = valid.astype(f32)
    ownf = own.astype(f32)
    own_at = jnp.where(own, src - HALO, own_rows)
    slot_of = slot + (slot >= gap).astype(jnp.int32)
    inside = ((slot + first >= 0) & (slot + first < fine_total)).astype(f32)
    inside = jnp.broadcast_to(inside, validf.shape)
    ints = jnp.stack(
        [jnp.clip(src, 0, window - 1), near_at, far_at, own_at, slot_of, jnp.broadcast_to(gap, src.shape)], axis=1
    )
    floats = jnp.stack(
        [
            validf,
            ownf,
            near_weight * validf,
            (1.0 - near_weight) * validf,
            near_weight * ownf,
            (1.0 - near_weight) * ownf,
            inside,
        ],
        axis=1,
    )
    batch = ids_rows.shape[0]
    return ints.astype(jnp.int32).reshape(batch, -1), floats.reshape(batch, -1)


def column_sides(v):
    n = v.shape[0]
    col = lax.broadcasted_iota(jnp.int32, v.shape, 0)
    left = jnp.where(col == 0, 0.0, pltpu.roll(v, 1, 0))
    right = jnp.where(col == n - 1, 0.0, pltpu.roll(v, n - 1, 0))
    return left, right


def three_columns(v):
    left, right = column_sides(v)
    return jnp.concatenate([left.astype(bf16), v.astype(bf16), right.astype(bf16)], axis=1)


def decode_kernel(own_rows, cols, chans, red, parts, before, at, itab, ftab, low_top, low, low_end, tgt, colm, colt, rwt, m1, m2, clst, *refs):
    projs, refs = refs[:parts], refs[parts + before:]
    decode_body(at[0], own_rows, cols, chans, red, projs, itab, ftab, low_top, low, low_end, tgt, colm, colt, rwt, m1, m2, clst, *refs)


def decode_body(first, own_rows, cols, chans, red, projs, itab, ftab, low_top, low, low_end, tgt, colm, colt, rwt, m1, m2, clst,
                  up_h, red_h, fst_h, sec_h, g2_h, g1_h, rg_h, pg_o,
                  jc, fc, sl1, rs, tgg, lift, drop, a0, a1, b0, b1,
                w1, rw3, clsb, wb2, wb1u, wb1r, up_o, red_o, fst_o, sec_o, g2_o, g1_o, rg_o, sems):
    m = pl.program_id(0)
    window = own_rows + 2 * HALO
    slots = window + 1
    held = projs[0].shape[1]
    wide = 3 * chans
    redw = jc.shape[2] - wide
    keep = own_rows + 3
    gc2, gc1 = jc.at[:, :, 0:wide], fc
    held_rows = [(up_o, up_h), (red_o, red_h), (fst_o, fst_h), (sec_o, sec_h), (g2_o, g2_h), (g1_o, g1_h), (rg_o, rg_h)]

    def out_copy(k, at):
        here, there = held_rows[k]
        return pltpu.make_async_copy(here.at[0:there.shape[1]], there.at[first + at], sems.at[k])

    @pl.when(m > 0)
    def _():
        for k in range(6):
            out_copy(k, m - 1).wait()

    @pl.when(m == 0)
    def _():
        w1[:, wide + 3 * red:] = jnp.zeros((3, redw - 3 * red, chans), bf16)
        clsb[...] = jnp.zeros(clsb.shape, bf16)
        clsb[0:clst.shape[0]] = clst[...]
        spare = jnp.zeros((redw - 3 * red, chans), bf16)
        rw3[...] = jnp.concatenate([rwt[...]] * 3 + [spare], axis=0).T
        for r in range(3):
            for d in range(3):
                part = slice(d * chans, (d + 1) * chans)
                w1[r, part] = m1[3 * r + d, 0:chans]
                w1[r, wide + d * red:wide + (d + 1) * red] = m1[3 * r + d, chans:]
                tap = 3 * (2 - r) + 2 - d
                wb2[r, part] = m2[tap].T
                wb1u[r, part] = m1[tap, 0:chans].T
            tails = [m1[3 * (2 - r) + d, chans:] for d in range(3)]
            wb1r[r] = jnp.concatenate(tails + [spare], axis=0).T

    def w2(r):
        return m2[3 * r:3 * r + 3].reshape(wide, chans)

    def it(k, j):
        return itab[first + m, k * slots + j]

    def ft(k, j):
        return ftab[first + m, k * slots + j]

    accs = (a0, a1)
    bccs = (b0, b1)

    def staged(blocks, multiply, finish):
        for k, block in enumerate(blocks):
            multiply(*block, accs[k % 2], bccs[k % 2])
            if k:
                finish(*blocks[k - 1], accs[(k - 1) % 2], bccs[(k - 1) % 2])
        k = len(blocks) - 1
        finish(*blocks[k], accs[k % 2], bccs[k % 2])

    def rows_of(ref, lo, n):
        return ref[lo:lo + n].reshape(n * cols, ref.shape[2])

    def dot(a, b):
        return jnp.dot(a, b, preferred_element_type=f32)

    @pl.when(m == 0)
    def _():
        tgg[...] = jnp.zeros(tgg.shape, bf16)

    for i in range(2):
        tgg[it(4, 2 + i)] = low_top[0, HALO][:, i * LANE:(i + 1) * LANE]
        tgg[it(4, own_rows + HALO + i)] = low_end[0, HALO][:, i * LANE:(i + 1) * LANE]
    for i in range(own_rows):
        tgg[it(4, HALO + i)] = tgt[0, i]
    tgg[it(5, 0)] = jnp.zeros((cols, LANE), bf16)

    lane = lax.broadcasted_iota(jnp.int32, (cols, redw), 1)

    def reduce_mul(ref, lo, n, place, acc, _):
        acc[0:n * cols] = dot(ref[0, lo:lo + n].reshape(n * cols, ref.shape[3]), rw3[...])

    def reduce_fin(ref, lo, n, place, acc, _):
        for r in range(n):
            a, slope = silu_and_slope(acc[r * cols:(r + 1) * cols])
            a = a * ft(6, place + r)
            left, right = column_sides(a)
            a = jnp.where(lane < red, left, jnp.where(lane < 2 * red, a, right))
            jc[it(4, place + r), :, wide:] = a.astype(bf16)
            if HALO <= place + r < own_rows + HALO:
                rs[place + r - HALO] = slope.astype(bf16)

    staged(
        [(low_top, 0, HALO, 0)]
        + [(low, lo, n, lo + HALO) for lo, n in split_rows(0, own_rows, 8)]
        + [(low_end, 0, HALO, own_rows + HALO)],
        reduce_mul, reduce_fin,
    )
    jc[it(5, 0), :, wide:] = jnp.zeros((cols, redw), bf16)

    for k in range(held):
        v = sum(p[0, k].astype(f32) for p in projs).astype(bf16)
        lift[k] = dot(colm[...], v)
    for j in range(slots):
        v = (ft(2, j) * lift[it(1, j)] + ft(3, j) * lift[it(2, j)]).astype(bf16)
        for d in range(3):
            jc[j, :, d * chans:(d + 1) * chans] = v[d * cols:(d + 1) * cols]
        if 3 <= j < 3 + keep:
            up_o[j - 3] = v[cols:2 * cols]

    red_o[...] = jc[3:3 + keep, :, wide:]
    out_copy(0, m).start()
    out_copy(1, m).start()

    def first_mul(lo, n, acc, _):
        acc[0:n * cols] = (
            dot(rows_of(jc, lo - 1, n), w1[0]) + dot(rows_of(jc, lo, n), w1[1]) + dot(rows_of(jc, lo + 1, n), w1[2])
        )

    def first_fin(lo, n, acc, _):
        for r in range(n):
            a, slope = silu_and_slope(acc[r * cols:(r + 1) * cols])
            keep_row = ft(0, lo + r)
            a = a * keep_row
            fc[lo + r] = three_columns(a)
            if 3 <= lo + r < 3 + keep:
                fst_o[lo + r - 3] = a.astype(bf16)
            sl1[lo + r] = (slope * keep_row).astype(bf16)

    staged(split_rows(1, slots - 1, 8), first_mul, first_fin)
    out_copy(2, m).start()

    def second_mul(lo, n, acc, bcc):
        acc[0:n * cols] = (
            dot(rows_of(fc, lo - 1, n), w2(0)) + dot(rows_of(fc, lo, n), w2(1)) + dot(rows_of(fc, lo + 1, n), w2(2))
        )
        bcc[0:n * cols] = dot(rows_of(tgg, lo, n), clsb[...])

    def second_fin(lo, n, acc, bcc):
        for r in range(n):
            j = lo + r
            a, slope = silu_and_slope(acc[r * cols:(r + 1) * cols])
            sec_o[it(3, j)] = a.astype(bf16)
            g = bcc[r * cols:(r + 1) * cols] * slope * ft(0, j)
            gc2[j] = three_columns(g)
            if HALO <= j <= own_rows + HALO:
                g2_o[j - HALO] = (g * ft(1, j)).astype(bf16)

    staged(split_rows(2, slots - 2, 8), second_mul, second_fin)
    out_copy(3, m).start()
    out_copy(4, m).start()

    def back2_mul(lo, n, acc, _):
        acc[0:n * cols] = (
            dot(rows_of(gc2, lo - 1, n), wb2[0]) + dot(rows_of(gc2, lo, n), wb2[1]) + dot(rows_of(gc2, lo + 1, n), wb2[2])
        )

    def back2_fin(lo, n, acc, _):
        for r in range(n):
            j = lo + r
            g = acc[r * cols:(r + 1) * cols] * sl1[j].astype(f32)
            gc1[j] = three_columns(g)
            if HALO <= j <= own_rows + HALO:
                g1_o[j - HALO] = (g * ft(1, j)).astype(bf16)

    staged(split_rows(3, slots - 3, 8), back2_mul, back2_fin)
    out_copy(5, m).start()

    drop[...] = jnp.zeros(drop.shape, f32)

    @pl.when(m > 0)
    def _():
        out_copy(6, m - 1).wait()

    def back1_mul(lo, n, acc, bcc):
        acc[0:n * cols] = (
            dot(rows_of(gc1, lo - 1, n), wb1u[0]) + dot(rows_of(gc1, lo, n), wb1u[1]) + dot(rows_of(gc1, lo + 1, n), wb1u[2])
        )
        mid = slice(chans, 2 * chans)
        bcc[0:n * cols] = (
            dot(rows_of(gc1, lo - 1, n)[:, mid], wb1r[0]) + dot(rows_of(gc1, lo, n)[:, mid], wb1r[1])
            + dot(rows_of(gc1, lo + 1, n)[:, mid], wb1r[2])
        )

    def back1_fin(lo, n, acc, bcc):
        for r in range(n):
            j = lo + r
            up = acc[r * cols:(r + 1) * cols]
            near, far = it(1, j), it(2, j)
            drop[near] += ft(4, j) * up
            drop[far] += ft(5, j) * up
            t = bcc[r * cols:(r + 1) * cols]
            left, right = column_sides(t)
            t = jnp.where(lane < red, right, jnp.where(lane < 2 * red, t, left))
            rg_o[it(3, j)] = (t * rs[it(3, j)].astype(f32)).astype(bf16)

    staged(split_rows(HALO, slots - HALO, 8), back1_mul, back1_fin)
    out_copy(6, m).start()

    for k in range(held):
        pg_o[0, k] = dot(colt[...], drop[k].astype(bf16)).astype(bf16)

    @pl.when(m == pl.num_programs(0) - 1)
    def _():
        for k in range(7):
            out_copy(k, m).wait()


def whole(a):
    return pl.BlockSpec(a.shape, lambda *at: (0,) * a.ndim, pipeline_mode=pl.Buffered(1))


def per(shape):
    return pl.BlockSpec((1,) + shape, lambda m, *at: (m,) + (0,) * len(shape))


def per_from(shape):
    return pl.BlockSpec((1,) + shape, lambda m, at: (m + at[0],) + (0,) * len(shape))


def total(shape):
    return pl.BlockSpec(shape, lambda *at: (0,) * len(shape))


def params():
    return pltpu.CompilerParams(vmem_limit_bytes=63 * 2 ** 20)


def saved_shapes(own_rows, cols, chans, red):
    redw = -(-3 * red // LANE) * LANE
    return [(own_rows + 3, cols, chans), (own_rows + 3, cols, redw), (own_rows + 3, cols, chans), (own_rows, cols, chans),
            (own_rows + 1, cols, chans), (own_rows + 1, cols, chans), (own_rows, cols, redw)]


def blank(batch, shapes):
    return tuple(pl.pallas_call(
        lambda *refs: None,
        out_specs=[pl.BlockSpec(memory_space=pl.ANY)] * len(shapes),
        out_shape=[jax.ShapeDtypeStruct((batch,) + s, bf16) for s in shapes],
        name="blank",
    )())


def decode(first, batch, tables, low_top, low_input, low_end, projs, target, reduce_t, merge1_weight, merge2_weight, class_t, earlier):
    ints, floats = tables
    all_batch, own_rows, cols, low_ch = low_input.shape
    window = own_rows + 2 * HALO
    slots = window + 1
    chans = merge2_weight.shape[1]
    red = reduce_t.shape[0]
    held, coarse_cols = projs[0].shape[1], projs[0].shape[2]
    redw = -(-3 * red // LANE) * LANE
    wide = 3 * chans
    colm = upsample_matrix(coarse_cols)
    zero = np.zeros((1, coarse_cols), np.float32)
    colm3 = jnp.asarray(np.concatenate([zero, colm[:-1], colm, colm[1:], zero], axis=0), bf16)
    colt = jnp.asarray(colm.T, bf16)
    keep = own_rows + 3
    smem = pl.BlockSpec(memory_space=pltpu.SMEM)
    hbm = pl.BlockSpec(memory_space=pl.ANY)
    most = max(n for k in range(5) for _, n in split_rows(k, slots - k, 8))
    consts = (colm3, colt, reduce_t, merge1_weight, merge2_weight, class_t)
    shapes = saved_shapes(own_rows, cols, chans, red)
    stage = [(s[0] + (1 if k in (3, 6) else 0),) + s[1:] for k, s in enumerate(shapes)]
    back_shape = (held, coarse_cols, chans)
    saved = pl.pallas_call(
        lambda *refs: decode_kernel(own_rows, cols, chans, red, len(projs), len(earlier), *refs),
        grid_spec=pltpu.PrefetchScalarGridSpec(
            num_scalar_prefetch=1,
            grid=(batch,),
            in_specs=[smem, smem] + [per_from(a.shape[1:]) for a in (low_top, low_input, low_end, target)]
            + [whole(a) for a in consts] + [per(p.shape[1:]) for p in projs] + [hbm] * len(earlier),
            out_specs=[hbm] * len(shapes) + [per(back_shape)],
            scratch_shapes=[
                pltpu.VMEM((slots, cols, wide + redw), bf16), pltpu.VMEM((slots, cols, wide), bf16),
                pltpu.VMEM((slots, cols, chans), bf16), pltpu.VMEM((own_rows + 1, cols, redw), bf16),
                pltpu.VMEM((slots, cols, LANE), bf16),
                pltpu.VMEM((held, 3 * cols, chans), f32), pltpu.VMEM((held, cols, chans), f32),
                pltpu.VMEM((most * cols, chans), f32), pltpu.VMEM((most * cols, chans), f32),
                pltpu.VMEM((most * cols, chans), f32), pltpu.VMEM((most * cols, chans), f32),
                pltpu.VMEM((3, wide + redw, chans), bf16), pltpu.VMEM((low_ch, redw), bf16), pltpu.VMEM((LANE, chans), bf16),
                pltpu.VMEM((3, wide, chans), bf16), pltpu.VMEM((3, wide, chans), bf16), pltpu.VMEM((3, chans, redw), bf16),
            ] + [pltpu.VMEM(s, bf16) for s in stage] + [pltpu.SemaphoreType.DMA((7,))],
        ),
        out_shape=[jax.ShapeDtypeStruct((all_batch,) + s, bf16) for s in shapes] + [jax.ShapeDtypeStruct((batch,) + back_shape, bf16)],
        input_output_aliases={7 + len(consts) + len(projs) + k: k for k in range(len(earlier))},
        compiler_params=params(),
        name="decode",
    )(jnp.full((1,), first, jnp.int32), ints, floats, low_top, low_input, low_end, target, *consts, *projs, *earlier)
    return saved[7], tuple(saved[:7])


def grads_kernel(own_rows, cols, chans, red, before, up, red3, fst, sec, g2, g1, rg, low, tgt, clst, rwt, *refs):
    earlier = refs[:before]
    packed, lowgrad, logits, o1, o2, oc, orr, upc, fcc = refs[before:]
    m = pl.program_id(0)
    keep = own_rows + 3
    wide = 3 * chans
    span = own_rows + 1
    classes = clst.shape[0]

    @pl.when(m == 0)
    def _():
        o1[...] = jnp.zeros(o1.shape, f32)
        o2[...] = jnp.zeros(o2.shape, f32)
        oc[...] = jnp.zeros(oc.shape, f32)
        orr[...] = jnp.zeros(orr.shape, f32)

    def tdot(a, b):
        return lax.dot_general(a, b, (((0,), (0,)), ((), ())), preferred_element_type=f32)

    for j in range(keep):
        upc[j] = three_columns(up[0, j].astype(f32))
    for j in range(keep):
        fcc[j] = three_columns(fst[0, j].astype(f32))

    def flat(v):
        return v.reshape(v.shape[0] * cols, v.shape[2])

    gg1 = flat(g1[0])
    for dy in range(3):
        o1[dy, 0:wide] += tdot(flat(upc[dy:dy + span]), gg1)
        o1[dy, wide:] += tdot(flat(red3[0, dy:dy + span]), gg1)
    gg2 = flat(g2[0])
    for dy in range(3):
        o2[dy] += tdot(flat(fcc[dy:dy + span]), gg2)
    oc[...] += tdot(flat(sec[0]), flat(tgt[0]))
    orr[...] += tdot(flat(low[0]), flat(rg[0]))
    spare = jnp.zeros((rg.shape[3] - 3 * red, chans), bf16)
    rb3 = jnp.concatenate([rwt[...]] * 3 + [spare], axis=0)
    for r in range(own_rows):
        lowgrad[0, r] = jnp.dot(rg[0, r], rb3, preferred_element_type=f32)
        lt = lax.dot_general(clst[...], sec[0, r], (((1,), (1,)), ((), ())), preferred_element_type=f32)
        logits[0, :, r] = lt

    @pl.when(m == pl.num_programs(0) - 1)
    def _():
        rows = chans + red
        for dy in range(3):
            for d in range(3):
                at = (3 * dy + d) * rows
                packed[at:at + chans] = o1[dy, d * chans:(d + 1) * chans].astype(bf16)
                packed[at + chans:at + rows] = o1[dy, wide + d * red:wide + (d + 1) * red].astype(bf16)
            packed[9 * rows + dy * wide:9 * rows + (dy + 1) * wide] = o2[dy].astype(bf16)
        at = 9 * rows + 3 * wide
        packed[at:] = jnp.zeros((packed.shape[0] - at, chans), bf16)
        t = orr[...].T
        packed[at:at + red] = (t[0:red] + t[red:2 * red] + t[2 * red:3 * red]).astype(bf16)
        packed[at + red:at + red + 32] = oc[...].T[0:32].astype(bf16)
        if before:
            packed[...] = (packed[...].astype(f32) + earlier[0][...].astype(f32)).astype(bf16)


def packed_rows(chans, red):
    return 9 * (chans + red) + 9 * chans + red + 32


def decode_grads(first, saved, low_input, target, reduce_t, class_t, earlier):
    up, red3, fst, sec, g2, g1, rg = saved
    batch = up.shape[0]
    all_batch, own_rows, cols, low_ch = low_input.shape
    chans = up.shape[3]
    redw = red3.shape[3]
    red = reduce_t.shape[0]
    classes = class_t.shape[0]
    wide = 3 * chans
    keep = own_rows + 3
    rows = packed_rows(chans, red)
    hbm = pl.BlockSpec(memory_space=pl.ANY)
    tots = [(3, wide + redw, chans), (3, wide, chans), (chans, LANE), (low_ch, redw)]
    pers = [(own_rows, cols, low_ch), (classes, own_rows, cols)]
    packed, lowgrad, logits = pl.pallas_call(
        lambda *refs: grads_kernel(own_rows, cols, chans, red, 3 if earlier else 0, *refs),
        grid=(batch,),
        in_specs=[per((keep, cols, chans)), per((keep, cols, redw)), per((keep, cols, chans)), per((own_rows, cols, chans)),
                  per((own_rows + 1, cols, chans)), per((own_rows + 1, cols, chans)), per((own_rows, cols, redw)),
                  per((own_rows, cols, low_ch)), per(target.shape[1:]), whole(class_t), whole(reduce_t)]
        + ([whole(earlier[0]), hbm, hbm] if earlier else []),
        out_specs=[total((rows, chans))] + [per(s) for s in pers],
        out_shape=[jax.ShapeDtypeStruct((rows, chans), bf16)] + [jax.ShapeDtypeStruct((all_batch,) + s, f32) for s in pers],
        input_output_aliases={12: 1, 13: 2} if earlier else {},
        scratch_shapes=[pltpu.VMEM(s, f32) for s in tots]
        + [pltpu.VMEM((keep, cols, wide), bf16), pltpu.VMEM((keep, cols, wide), bf16)],
        compiler_params=params(),
        name="decode_grads",
        cost_estimate=pl.CostEstimate(flops=1, bytes_accessed=1, transcendentals=1),
    )(up, red3, fst, sec, g2, g1, rg, low_input, target, class_t, reduce_t, *(earlier or ()))
    return packed, lowgrad, logits


def unpack_decoder(bit, mine, other, chans, red, classes):
    rows = chans + red
    half = mine.shape[0]
    at = 9 * rows + 9 * chans
    shapes = [(9, rows, chans), (9, chans, chans), (red, chans), (classes, chans)]

    def kernel(bit, a, b, m1, m2, rw, cw, v):
        v[pl.ds(pl.multiple_of(bit[0] * half, 16), half)] = a[...]
        v[pl.ds(pl.multiple_of((1 - bit[0]) * half, 16), half)] = b[...]
        for t in range(9):
            m1[t] = v[t * rows:(t + 1) * rows].astype(f32)
            m2[t] = v[9 * rows + t * chans:9 * rows + (t + 1) * chans].astype(f32)
        rw[...] = v[at:at + red].astype(f32)
        cw[...] = v[at + red:at + red + 32].astype(f32)[0:classes]

    m1, m2, rw, cw = pl.pallas_call(
        kernel,
        grid=(1,),
        in_specs=[pl.BlockSpec(memory_space=pltpu.SMEM), whole(mine), whole(other)],
        out_specs=[total(s) for s in shapes],
        out_shape=[jax.ShapeDtypeStruct(s, f32) for s in shapes],
        scratch_shapes=[pltpu.VMEM((2 * half, chans), bf16)],
        compiler_params=params(),
        name="unpack_decoder",
    )(bit, mine, other)
    return m1, m2, rw.T, cw.T


atrous_rates = (6, 12, 18)
epsilon = 1e-05


def tap_list():
    listed = [(0, 0, 0)]
    for branch_index, rate_value in enumerate(atrous_rates):
        for step_rows in (-1, 0, 1):
            for step_cols in (-1, 0, 1):
                listed.append((rate_value * step_rows, rate_value * step_cols, branch_index + 1))
    return listed


def pixel_places(batch, height, width):
    pixel = np.arange(height * width)
    places = np.stack([np.tile(pixel // width, batch), np.tile(pixel % width, batch), np.repeat(np.arange(batch), height * width)])
    return jnp.asarray(np.pad(places, ((0, 5), (0, 0))), jnp.int32)


class Pixels:
    def __init__(self, places, cuts, batch, height, width):
        self.row, self.col, self.canvas = places[0:1], places[1:2], places[2:3]
        self.height, self.width = height, width
        cut = jnp.full(self.row.shape, cuts[0], jnp.int32)
        for m in range(1, batch):
            cut = jnp.where(self.canvas == m, cuts[m], cut)
        self.cut = cut
        self.band = self.row >= cut

    def valid(self, dr, dc):
        row, col = self.row + dr, self.col + dc
        inside = (row >= 0) & (row < self.height) & (col >= 0) & (col < self.width)
        same = jnp.where(row >= self.cut, 1, 0) == jnp.where(self.band, 1, 0)
        return jnp.where(inside & same, 1.0, 0.0)

    def image(self):
        return IMAGES * self.canvas + jnp.where(self.band, 1, 0)


def image_counts(cuts, batch, height, width):
    index = lax.broadcasted_iota(jnp.int32, (IMAGES * batch, 1), 0)
    out = jnp.zeros((IMAGES * batch, 1), f32)
    for m in range(batch):
        first = cuts[m] * width
        out = jnp.where(index == IMAGES * m, first.astype(f32), out)
        out = jnp.where(index == IMAGES * m + 1, (height * width - first).astype(f32), out)
    return jnp.maximum(out, 1.0)


def branch_kernel(taps, batch, height, width, cuts, x, w, places, pw, br_o, mom_o, pooled_o, y, pool, mom):
    i = pl.program_id(0)
    last = pl.num_programs(0) - 1
    block = x.shape[0]
    total = y.shape[1]
    pixels = total // batch
    own = pw.shape[0]
    at = pl.multiple_of(i * block, block)

    @pl.when(i == 0)
    def _():
        pool[...] = jnp.zeros(pool.shape, f32)
        mom[...] = jnp.zeros(mom.shape, f32)

    def nt(a, b):
        return lax.dot_general(a, b, (((1,), (1,)), ((), ())), preferred_element_type=f32)

    canvas, row = places[2:3, pl.ds(at, block)], places[0:1, pl.ds(at, block)]
    cut = jnp.full(row.shape, cuts[0], jnp.int32)
    for m in range(1, batch):
        cut = jnp.where(canvas == m, cuts[m], cut)
    image = IMAGES * canvas + jnp.where(row >= cut, 1, 0)
    index = lax.broadcasted_iota(jnp.int32, (IMAGES * batch, block), 0)
    member = jnp.where(image == index, 1.0, 0.0).astype(bf16)
    pool[...] += jnp.dot(member, x[...], preferred_element_type=f32)

    @pl.when(i < last)
    def _():
        y[:, pl.ds(at, block)] = nt(w[...], x[...])

    def keep(m, b, v):
        part = slice(b * own, (b + 1) * own)
        br_o[m, part] = v
        mom[part, m:m + 1] = jnp.sum(v, axis=1, keepdims=True)
        mom[part, batch + m:batch + m + 1] = jnp.sum(v * v, axis=1, keepdims=True)

    @pl.when(i == last)
    def _():
        px = Pixels(places, cuts, batch, height, width)
        spans = []
        for b in range(4):
            mine = [t for t, tap in enumerate(taps) if tap[2] == b]
            spans.append((mine[0], mine[-1] + 1))

        def multiply(b):
            lo, hi = spans[b][0] * own, spans[b][1] * own
            y[lo:hi, total - block:] = nt(w[lo:hi], x[...])

        def finish(b):
            acc = None
            for t in range(*spans[b]):
                dr, dc, _ = taps[t]
                v = y[t * own:(t + 1) * own]
                shift = dr * width + dc
                if shift:
                    v = pltpu.roll(v, (-shift) % total, 1) * px.valid(dr, dc)
                acc = v if acc is None else acc + v
            for m in range(batch):
                keep(m, b, acc[:, m * pixels:(m + 1) * pixels])

        multiply(0)
        multiply(1)
        multiply(2)
        finish(0)
        finish(1)
        multiply(3)
        finish(2)
        finish(3)
        pooled = (pool[...] / image_counts(cuts, batch, height, width)).astype(bf16)
        pooled_o[...] = pooled
        po = nt(pw[...], pooled)
        for m in range(batch):
            band = px.band[:, m * pixels:(m + 1) * pixels]
            keep(m, 4, jnp.where(band, po[:, IMAGES * m + 1:IMAGES * m + 2], po[:, IMAGES * m:IMAGES * m + 1]))
        mom_o[...] = mom[...].T[0:mom_o.shape[0]]


def aspp_forward(cuts, x, wt, pwt, batch, height, width):
    all_pixels, in_chans = x.shape
    pixels = height * width
    own = pwt.shape[0]
    taps = tap_list()
    block = all_pixels // 3 if all_pixels % 3 == 0 and (all_pixels // 3) % LANE == 0 else all_pixels
    places = pixel_places(batch, height, width)
    outs = [((batch, 5 * own, pixels), f32), ((2 * batch, 5 * own), f32), ((IMAGES * batch, in_chans), bf16)]
    return pl.pallas_call(
        lambda *refs: branch_kernel(taps, batch, height, width, *refs),
        grid=(all_pixels // block,),
        in_specs=[pl.BlockSpec(memory_space=pltpu.SMEM), pl.BlockSpec((block, in_chans), lambda i: (i, 0)),
                  whole(wt), whole(places), whole(pwt)],
        out_specs=[total(s) for s, _ in outs],
        out_shape=[jax.ShapeDtypeStruct(s, d) for s, d in outs],
        scratch_shapes=[pltpu.VMEM((len(taps) * own, all_pixels), f32), pltpu.VMEM((IMAGES * batch, in_chans), f32),
                        pltpu.VMEM((5 * own, LANE), f32)],
        compiler_params=params(),
        name="aspp_forward",
    )(cuts, x, wt, places, pwt)


def column(t, m):
    if isinstance(m, int):
        return t[:, m:m + 1]
    lane = lax.broadcasted_iota(jnp.int32, t.shape, 1)
    return jnp.sum(jnp.where(lane == m, t, 0.0), axis=1, keepdims=True)


def norm_columns(stats, scale, m, batch, count):
    t = stats[...].T
    mean = column(t, m) / count
    inv_std = lax.rsqrt(column(t, batch + m) / count - mean * mean + epsilon)
    s = scale[...].T
    half = s.shape[1] // 2
    gain = jnp.concatenate([s[:, k:k + 1] for k in range(half)], axis=0)
    shift = jnp.concatenate([s[:, half + k:half + k + 1] for k in range(half)], axis=0)
    return mean, inv_std, gain, shift


def project_kernel(group, count, coarse_rows, at_ref, offsets, br, stats, scale, proj, *refs):
    outs, rows = refs[:-1], refs[-1]
    batch = stats.shape[0] // 2
    height, width, chans = rows.shape[0] - 4, rows.shape[1], rows.shape[2]
    held = coarse_rows + 4
    rows[0:2] = jnp.zeros((2, width, chans), f32)
    rows[height + 2:] = jnp.zeros((2, width, chans), f32)
    for at in range(group):
        mean, inv_std, gain, shift = norm_columns(stats, scale, at_ref[0] + at, batch, count)
        active, _ = silu_and_slope((br[at] - mean) * inv_std * gain + shift)
        partial = lax.dot_general(active.astype(bf16), proj[...], (((0,), (0,)), ((), ())), preferred_element_type=f32)
        rows[2:height + 2] = partial.reshape(height, width, chans)
        for k, o in enumerate(outs):
            o[at] = rows[pl.ds(offsets[k], held)].astype(bf16)


def project(first, group, offsets, br, stats, scale, proj, count, coarse_rows, parts, height, width):
    chans = proj.shape[1]
    shape = (group, coarse_rows + 4, width, chans)
    pixels = br.shape[2]
    return pl.pallas_call(
        lambda *refs: project_kernel(group, count, coarse_rows, *refs),
        grid_spec=pltpu.PrefetchScalarGridSpec(
            num_scalar_prefetch=1,
            grid=(1,),
            in_specs=[pl.BlockSpec(memory_space=pltpu.SMEM), pl.BlockSpec((pl.Element(group), pl.Element(br.shape[1]), pl.Element(pixels)), lambda i, at: (at[0], 0, 0)),
                      whole(stats), whole(scale), whole(proj)],
            out_specs=[total(shape)] * parts,
            scratch_shapes=[pltpu.VMEM((height + 4, width, chans), f32)],
        ),
        out_shape=[jax.ShapeDtypeStruct(shape, bf16)] * parts,
        compiler_params=params(),
        name="project",
    )(jnp.full((1,), first, jnp.int32), offsets, br, stats, scale, proj)


def norm_back_kernel(count, parts, at_ref, offsets, br, stats, scale, proj, earlier, sums_before, *refs):
    pieces = refs[:parts]
    grad_o, sums_o, projgrad_o, rows, sums = refs[parts:]
    height, width, chans = rows.shape[0] - 4, rows.shape[1], rows.shape[2]
    group, held = pieces[0].shape[0], pieces[0].shape[1]
    batch = stats.shape[0] // 2
    sums[...] = jnp.zeros(sums.shape, f32)
    projgrad = earlier[...]
    for at in range(group):
        m = at_ref[0] + at
        rows[...] = jnp.zeros(rows.shape, f32)
        for k, piece in enumerate(pieces):
            rows[pl.ds(offsets[k], held)] += piece[at].astype(f32)
        grad = rows[2:height + 2].reshape(height * width, chans).astype(bf16)
        mean, inv_std, gain, shift = norm_columns(stats, scale, m, batch, count)
        scaled = (br[at] - mean) * inv_std
        active, slope = silu_and_slope(scaled * gain + shift)
        back = lax.dot_general(proj[...], grad, (((1,), (1,)), ((), ())), preferred_element_type=f32) * slope
        grad_o[at] = back
        lane = lax.broadcasted_iota(jnp.int32, sums.shape, 1)
        products = jnp.sum(back * scaled, axis=1, keepdims=True)
        sums[...] += jnp.where(lane == m, products, jnp.where(lane == batch + m, jnp.sum(back, axis=1, keepdims=True), 0.0))
        projgrad = projgrad + jnp.dot(active.astype(bf16), grad, preferred_element_type=f32)
    projgrad_o[...] = projgrad
    sums_o[...] = sums_before[...] + sums[...].T[0:sums_o.shape[0]]


def norm_back(first, offsets, br, stats, scale, proj, earlier, sums_before, pieces, count, height, width):
    batch, chans5, pixels = br.shape
    group = pieces[0].shape[0]
    outs = [((group, chans5, pixels), f32), (stats.shape, f32), (proj.shape, f32)]
    return pl.pallas_call(
        lambda *refs: norm_back_kernel(count, len(pieces), *refs),
        grid_spec=pltpu.PrefetchScalarGridSpec(
            num_scalar_prefetch=1,
            grid=(1,),
            in_specs=[pl.BlockSpec(memory_space=pltpu.SMEM), pl.BlockSpec((pl.Element(group), pl.Element(chans5), pl.Element(pixels)), lambda i, at: (at[0], 0, 0)),
                      whole(stats), whole(scale), whole(proj), whole(earlier), whole(sums_before)] + [whole(p) for p in pieces],
            out_specs=[total(s) for s, _ in outs],
            scratch_shapes=[pltpu.VMEM((height + 4, width, proj.shape[1]), f32), pltpu.VMEM((chans5, LANE), f32)],
        ),
        out_shape=[jax.ShapeDtypeStruct(s, d) for s, d in outs],
        compiler_params=params(),
        name="norm_back",
    )(jnp.full((1,), first, jnp.int32), offsets, br, stats, scale, proj, earlier, sums_before, *pieces)


def weight_grad_kernel(taps, groups, height, width, count, cuts, stats, scale, sums, places, projgrad, x_hbm, br_hbm, *refs):
    backs = refs[:groups]
    wg_hbm, tg_hbm, pg_o, both, x, tg, wg, br, back, sems, in_sems = refs[groups:]
    batch = br.shape[0]
    owner = [(g, k) for g, part in enumerate(backs) for k in range(part.shape[0])]

    def in_copies(m):
        g, k = owner[m]
        return (pltpu.make_async_copy(br_hbm.at[m], br.at[m], in_sems.at[m]),
                pltpu.make_async_copy(backs[g].at[k], back.at[m], in_sems.at[batch + m]))

    for m in range(batch):
        for copy in in_copies(m):
            copy.start()
    own = pg_o.shape[0]
    pixels = br.shape[2]
    rows, all_pixels = tg.shape
    in_chans = x.shape[1]
    filled = (len(taps) + 1) * own
    x_copy = pltpu.make_async_copy(x_hbm, x, sems.at[0])
    x_copy.start()
    px = Pixels(places, cuts, batch, height, width)
    pool_grad = jnp.zeros((own, LANE), f32)
    lane = lax.broadcasted_iota(jnp.int32, (own, LANE), 1)
    t = sums[...].T
    for m in range(batch):
        for copy in in_copies(m):
            copy.wait()
        mean, inv_std, gain, _ = norm_columns(stats, scale, m, batch, count)
        gain_sum, shift_sum = t[:, m:m + 1], t[:, batch + m:batch + m + 1]
        scaled = (br[m] - mean) * inv_std
        grad = inv_std * gain * (back[m] - (shift_sum + scaled * gain_sum) / count)
        both[0:4 * own, m * pixels:(m + 1) * pixels] = grad[0:4 * own]
        pool = grad[4 * own:]
        band = px.band[:, m * pixels:(m + 1) * pixels]
        upper = jnp.sum(jnp.where(band, 0.0, pool), axis=1, keepdims=True).astype(bf16).astype(f32)
        lower = jnp.sum(jnp.where(band, pool, 0.0), axis=1, keepdims=True).astype(bf16).astype(f32)
        pool_grad = jnp.where(lane == IMAGES * m, upper, pool_grad)
        pool_grad = jnp.where(lane == IMAGES * m + 1, lower, pool_grad)
        many = (cuts[m] * width).astype(f32)
        spread = jnp.where(band, lower / jnp.maximum(height * width - many, 1.0), upper / jnp.maximum(many, 1.0))
        both[4 * own:, m * pixels:(m + 1) * pixels] = spread
    pg_o[...] = pool_grad[:, 0:pg_o.shape[1]].astype(bf16)

    for k, (dr, dc, b) in enumerate(taps):
        v = both[b * own:(b + 1) * own]
        shift = dr * width + dc
        if shift:
            v = pltpu.roll(v * px.valid(dr, dc), shift % all_pixels, 1)
        tg[k * own:(k + 1) * own] = v.astype(bf16)
    tg[filled - own:] = both[4 * own:].astype(bf16)
    tg_copy = pltpu.make_async_copy(tg, tg_hbm, sems.at[1])
    tg_copy.start()
    x_copy.wait()
    chans = projgrad.shape[1]
    some = projgrad.shape[0] * chans // in_chans
    step = 512 if in_chans % 512 == 0 else in_chans
    wg[filled:] = jnp.zeros((wg.shape[0] - filled, in_chans), bf16)
    for k in range(in_chans // chans):
        wg[filled:filled + some, k * chans:(k + 1) * chans] = projgrad[k * some:(k + 1) * some].astype(bf16)

    def out_copy(n):
        part = pl.ds(pl.multiple_of(n * step, step), step)
        return pltpu.make_async_copy(wg.at[:, part], wg_hbm.at[:, part], sems.at[2 + n])

    def multiply(n, _):
        part = pl.ds(pl.multiple_of(n * step, step), step)
        wg[0:filled, part] = jnp.dot(tg[...], x[:, part], preferred_element_type=f32).astype(bf16)
        out_copy(n).start()
        return 0

    lax.fori_loop(0, in_chans // step, multiply, 0)
    tg_copy.wait()
    for n in range(in_chans // step):
        out_copy(n).wait()


def aspp_weight_grads(rows, cuts, x, br, stats, scale, sums, projgrad, backs, count, height, width):
    all_pixels, in_chans = x.shape
    batch, chans5, pixels = br.shape
    own = chans5 // 5
    places = pixel_places(batch, height, width)
    groups = len(backs)
    hbm = pl.BlockSpec(memory_space=pl.ANY)
    outs = [(rows, in_chans), ((len(tap_list()) + 1) * own, all_pixels), (own, IMAGES * batch)]
    return pl.pallas_call(
        lambda *refs: weight_grad_kernel(tap_list(), groups, height, width, count, *refs),
        grid=(1,),
        in_specs=[pl.BlockSpec(memory_space=pltpu.SMEM)] + [whole(v) for v in (stats, scale, sums, places, projgrad)]
        + [hbm] * (2 + len(backs)),
        out_specs=[hbm, hbm, total(outs[2])],
        out_shape=[jax.ShapeDtypeStruct(s, bf16) for s in outs],
        scratch_shapes=[pltpu.VMEM((chans5, all_pixels), f32), pltpu.VMEM((all_pixels, in_chans), bf16),
                        pltpu.VMEM(outs[1], bf16), pltpu.VMEM(outs[0], bf16),
                        pltpu.VMEM(br.shape, f32), pltpu.VMEM(br.shape, f32),
                        pltpu.SemaphoreType.DMA((2 + in_chans // 512 + 1,)), pltpu.SemaphoreType.DMA((2 * batch,))],
        compiler_params=params(),
        name="aspp_weight_grads",
    )(cuts, stats, scale, sums, places, projgrad, x, br, *backs)


def unpack_weights(summed, wide, own, proj_shape):
    rows, in_chans = summed.shape
    block = 512 if in_chans % 512 == 0 else in_chans
    chans = proj_shape[1]
    pieces = block // chans
    some = proj_shape[0] * chans // in_chans

    def kernel(v, wide_o, pool_o, proj_o):
        wide_o[...] = v[0:wide].astype(f32)
        pool_o[...] = v[wide:wide + own].astype(f32)
        tail = v[wide + own:].astype(f32)
        for k in range(pieces):
            proj_o[k * some:(k + 1) * some] = tail[0:some, k * chans:(k + 1) * chans]

    def lanes(a):
        return pl.BlockSpec((a, block), lambda j: (0, j))

    return pl.pallas_call(
        kernel,
        grid=(in_chans // block,),
        in_specs=[lanes(rows)],
        out_specs=[lanes(wide), lanes(own), pl.BlockSpec((some * pieces, chans), lambda j: (j, 0))],
        out_shape=[jax.ShapeDtypeStruct(s, f32) for s in ((wide, in_chans), (own, in_chans), proj_shape)],
        compiler_params=params(),
        name="unpack_weights",
    )(summed)


def input_grad_kernel(batch, span, height, width, at, cuts, tg, w, pg, pw, band, o):
    i = pl.program_id(0)
    pixels = height * width
    v = lax.dot_general(tg[...], w[...], (((0,), (0,)), ((), ())), preferred_element_type=f32)
    image = lax.dot_general(pg[...], pw[...], (((0,), (0,)), ((), ())), preferred_element_type=f32)
    image = image / image_counts(cuts, batch, height, width)
    index = lax.broadcasted_iota(jnp.int32, (IMAGES * batch, 1), 0)
    row = band[...]
    for k in range(span):
        m = i * span + k
        first = jnp.sum(jnp.where(index == IMAGES * m, image, 0.0), axis=0, keepdims=True)
        second = jnp.sum(jnp.where(index == IMAGES * m + 1, image, 0.0), axis=0, keepdims=True)
        part = slice(k * pixels, (k + 1) * pixels)
        o[part] = (v[part] + jnp.where(row >= cuts[m], second, first)).astype(bf16)


def aspp_input_grad(place, cuts, tg, wt, pool_grad, pwt, parts, height, width):
    rows, in_chans = wt.shape
    all_pixels = tg.shape[1]
    own = pwt.shape[0]
    pixels = height * width
    batch = all_pixels // pixels
    block = in_chans // parts
    span = 2 if (2 * pixels) % LANE == 0 and batch % 2 == 0 else batch
    row_column = jnp.asarray(np.arange(pixels)[:, None] // width, jnp.int32)
    return pl.pallas_call(
        lambda *refs: input_grad_kernel(batch, span, height, width, *refs),
        grid_spec=pltpu.PrefetchScalarGridSpec(
            num_scalar_prefetch=2,
            grid=(batch // span,),
            in_specs=[
                pl.BlockSpec((rows, span * pixels), lambda i, at, cuts: (0, i)),
                pl.BlockSpec((rows, block), lambda i, at, cuts: (0, at[0])),
                whole(pool_grad),
                pl.BlockSpec((own, block), lambda i, at, cuts: (0, at[0])),
                whole(row_column),
            ],
            out_specs=pl.BlockSpec((span * pixels, block), lambda i, at, cuts: (i, 0)),
        ),
        out_shape=jax.ShapeDtypeStruct((all_pixels, block), bf16),
        compiler_params=params(),
        name="aspp_input_grad",
        cost_estimate=pl.CostEstimate(flops=1, bytes_accessed=1, transcendentals=1),
    )(place, cuts, tg, wt, pool_grad, pwt, row_column)


def doubled_sum(value, axis):
    size = lax.axis_size(axis)
    step = 1
    while step < size:
        value = value + lax.ppermute(value, axis, [(i, i ^ step) for i in range(size)])
        step *= 2
    return value


def exchanged(pieces, axis):
    size = lax.axis_size(axis)
    return [pieces[0]] + [lax.ppermute(pieces[k], axis, [(i, i ^ k) for i in range(size)]) for k in range(1, size)]


def added(a, b):
    return (a.astype(f32) + b.astype(f32)).astype(bf16)


def scatter_sum(value, axis, unit):
    size = lax.axis_size(axis)
    count = size // unit
    me = lax.axis_index(axis)
    rows = value.shape[0] // count
    out = None
    for k in range(count):
        piece = lax.dynamic_slice_in_dim(value, ((me // unit) ^ k) * rows, rows, 0)
        if k:
            piece = lax.ppermute(piece, axis, [(i, i ^ (k * unit)) for i in range(size)])
        out = piece.astype(f32) if out is None else out + piece.astype(f32)
    return out.astype(bf16)


def gather(value, axis, unit):
    size = lax.axis_size(axis)
    count = size // unit
    me = lax.axis_index(axis)
    got = [value] + [lax.ppermute(value, axis, [(i, i ^ (k * unit)) for i in range(size)]) for k in range(1, count)]
    rows = value.shape[0]
    out = jnp.zeros((count * rows,) + value.shape[1:], value.dtype)
    for k, piece in enumerate(got):
        out = lax.dynamic_update_slice_in_dim(out, piece, ((me // unit) ^ k) * rows, 0)
    return out


def tied(value, *others):
    return lax.optimization_barrier((value,) + others)[0]


def local(aspp_input, low_input, aspp_ids, low_ids, aspp_weight, pool_weight, bn_gain, bn_shift, projection_matrix,
          reduce_weight, merge1_weight, merge2_weight, class_weight, logit_grad):
    section = lax.axis_index("section")
    sections = lax.axis_size("section")
    batch, height, width, in_chans = aspp_input.shape
    taps, own = aspp_weight.shape[1], aspp_weight.shape[2]
    branches = bn_gain.shape[0]
    chans = projection_matrix.shape[2]
    red = reduce_weight.shape[1]
    classes = class_weight.shape[1]
    fine_rows, fine_cols = low_input.shape[1], low_input.shape[2]
    pixels = height * width
    count = pixels * lax.axis_size("dp")
    coarse_rows = fine_rows // 4
    groups = [(0, batch - 1), (batch - 1, 1)]

    x = aspp_input.reshape(batch * pixels, in_chans)
    wt = jnp.transpose(aspp_weight, (1, 2, 0)).reshape(taps * own, in_chans)
    pwt = pool_weight.T
    proj = projection_matrix.reshape(branches * own, chans)
    cuts = jnp.sum((aspp_ids[:, :, 0] == 0).astype(jnp.int32), axis=1)
    br, moments, pooled = aspp_forward(cuts, x, wt, pwt, batch, height, width)

    down = [(i, i + 1) for i in range(sections - 1)]
    up = [(i + 1, i) for i in range(sections - 1)]
    target = jnp.pad(logit_grad, ((0, 0), (0, 0), (0, 0), (0, LANE - classes)))

    def rim(low_rows, target_rows):
        paired = jnp.concatenate([target_rows[:, 0:1], target_rows[:, 1:2]], axis=3)
        return jnp.concatenate([low_rows, paired], axis=1)

    top = lax.ppermute(rim(low_input[:, -HALO:], target[:, -2:]), "section", down)
    end = lax.ppermute(rim(low_input[:, :HALO], target[:, :2]), "section", up)
    tables = row_tables(low_ids[:, :, 0], section, fine_rows, height)
    distance = jnp.arange(sections, dtype=jnp.int32)
    offsets = (section ^ distance) * coarse_rows

    stats = doubled_sum(moments, "dp")
    scale = jnp.concatenate([bn_gain, bn_shift], axis=0)
    saved = blank(batch, saved_shapes(fine_rows, fine_cols, chans, red))
    parts = []
    for first, size in groups:
        at = tied(offsets, target, *tables, saved[0]) if parts else offsets
        parts.append(project(first, size, at, br, stats, scale, proj, count, coarse_rows, sections, height, width))
    projs = [exchanged(p, "section") for p in parts]
    projs[0][0] = tied(projs[0][0], *[p[0] for p in parts[1:]])
    pieces = []
    for g, (first, size) in enumerate(groups):
        pgrad, saved = decode(first, size, tables, top, low_input, end, projs[g], target, reduce_weight.T,
                              merge1_weight, merge2_weight, class_weight.T, saved)
        if g + 1 < len(groups):
            pgrad, *projs[g + 1] = lax.optimization_barrier((pgrad, *projs[g + 1]))
        pieces.append(exchanged([pgrad] * sections, "section"))
    backs = []
    projgrad, sums = jnp.zeros(proj.shape, f32), jnp.zeros(stats.shape, f32)
    for (first, size), piece in zip(groups, pieces):
        back, sums, projgrad = norm_back(first, offsets, br, stats, scale, proj, projgrad, sums, piece, count, height, width)
        backs.append(back)
    sums = doubled_sum(sums, "dp")
    filled = (taps + 1) * own
    rows = -(-(filled + projgrad.size // in_chans) // 32) * 32
    grads, tg, pool_grad = aspp_weight_grads(rows, cuts, x, br, stats, scale, sums, projgrad, backs, count, height, width)

    order = list(reversed(range(sections)))
    received = {}

    def input_of(k, tg):
        place = (section ^ k).reshape(1).astype(jnp.int32)
        return aspp_input_grad(place, cuts, tg, wt, pool_grad, pwt, sections, height, width)

    def sent(piece, k):
        return lax.ppermute(piece, "section", [(i, i ^ k) for i in range(sections)]) if k else piece

    share = lax.psum_scatter(grads, "dp", tiled=True)
    early, late = order[:len(order) // 2], order[len(order) // 2:]
    piece = input_of(early[0], tied(tg, grads))
    far = sent(piece, early[0])
    first = tied(saved[0], piece)
    packed, low_grad, logits = decode_grads(0, (first,) + saved[1:], low_input, target, reduce_weight.T, class_weight.T, None)
    swap = [(i, i ^ 1) for i in range(lax.axis_size("dp"))]
    bit = lax.axis_index("dp") % 2
    half = packed.shape[0] // 2
    mine = lax.dynamic_slice_in_dim(packed, bit * half, half, 0)
    packed = added(mine, lax.ppermute(lax.dynamic_slice_in_dim(packed, (1 - bit) * half, half, 0), "dp", swap))
    packed, far, tied_tg = lax.optimization_barrier((packed, far, tg))
    packed = scatter_sum(packed, "section", 1)
    received[early[0]] = far
    for k in early[1:]:
        received[k] = input_of(k, tied_tg)
        packed = tied(packed, received[k])
    held = tuple(received[k] for k in early)
    (share, packed), held = lax.optimization_barrier(((share, packed), held))
    received.update(zip(early, held))

    summed = lax.all_gather(share, "dp", tiled=True)
    for k in early[1:]:
        received[k] = sent(received[k], k)
    steps = [lambda v: scatter_sum(v, "dp", 2), lambda v: gather(v, "dp", 2)]
    for k in late:
        packed, tied_tg = lax.optimization_barrier((packed, tg) + ((piece,) if k != late[0] else ()))[:2]
        piece = input_of(k, tied_tg)
        if steps:
            packed = steps.pop(0)(packed)
        packed, piece = lax.optimization_barrier((packed, piece))
        received[k] = sent(piece, k)
    packed = gather(packed, "section", 1)
    input_grad = sum(received[k].astype(f32) for k in order).reshape(batch, height, width, in_chans // sections)
    packed, summed, input_grad = lax.optimization_barrier((packed, summed, input_grad))
    other = lax.ppermute(packed, "dp", swap)
    merge1_grad, merge2_grad, reduce_grad, class_grad = unpack_decoder(bit.reshape(1).astype(jnp.int32), packed, other, chans, red,
                                                                       classes)

    wide, pool_weight_grad, proj_weight_grad = unpack_weights(summed, taps * own, own, proj.shape)
    sums = jnp.sum(sums.reshape(2, batch, -1), axis=1)
    return (
        jnp.transpose(logits, (0, 2, 3, 1)),
        input_grad,
        low_grad,
        jnp.transpose(wide.reshape(taps, own, in_chans), (2, 0, 1)),
        pool_weight_grad.T,
        sums[0].reshape(branches, own),
        sums[1].reshape(branches, own),
        proj_weight_grad.reshape(branches, own, chans),
        reduce_grad,
        merge1_grad,
        merge2_grad,
        class_grad,
    )


def solution(mesh):
    return jax.shard_map(
        local,
        mesh=mesh,
        in_specs=(
            P("dp", None, None, None), P("dp", "section", None, None), P("dp", None, None), P("dp", None, None),
            P(None, None, "section"), P(None, "section"), P(None, "section"), P(None, "section"), P(None, "section", None),
            P(), P(), P(), P(), P("dp", "section", None, None),
        ),
        out_specs=(
            P("dp", "section", None, None), P("dp", None, None, "section"), P("dp", "section", None, None),
            P(None, None, "section"), P(None, "section"), P(None, "section"), P(None, "section"), P(None, "section", None),
            P(), P(), P(), P(),
        ),
        check_vma=False,
    )
```

```python
import jax
import jax.numpy as jnp
import numpy as np
from jax import lax
from jax.experimental import pallas as pl
from jax.experimental.pallas import tpu as pltpu
from jax.sharding import PartitionSpec as P

IMAGES = 2
bf16 = jnp.bfloat16
f32 = jnp.float32
HALO = 4
LANE = 128


def upsample_matrix(coarse_count):
    fine = np.arange(4 * coarse_count)
    coarse, phase = fine // 4, fine % 4
    near = np.where(phase < 2, 5 + 2 * phase, 11 - 2 * phase) / 8.0
    far = np.clip(np.where(phase < 2, coarse - 1, coarse + 1), 0, coarse_count - 1)
    matrix = np.zeros((4 * coarse_count, coarse_count), np.float32)
    np.add.at(matrix, (fine, coarse), near)
    np.add.at(matrix, (fine, far), 1.0 - near)
    return matrix


def split_rows(first, stop, target):
    count = stop - first
    pieces = -(-count // target)
    edges = [first + (count * k) // pieces for k in range(pieces + 1)]
    return [(edges[k], edges[k + 1] - edges[k]) for k in range(pieces)]


def silu_and_slope(v):
    s = 0.5 + 0.5 * jnp.tanh(0.5 * v)
    a = v * s
    return a, s * (1.0 + v - a)


def row_tables(cut, fine_total, section_index, own_rows, coarse_rows):
    window = own_rows + 2 * HALO
    slots = window + 1
    first = section_index * own_rows - HALO
    cut = cut[:, None] - first
    gap = jnp.where((cut >= 1) & (cut < window), cut, window)
    slot = jnp.arange(slots, dtype=jnp.int32)[None, :]
    src = slot - (slot > gap).astype(jnp.int32)
    row = src + first
    valid = (slot != gap) & (row >= 0) & (row < fine_total)
    own = valid & (src >= HALO) & (src < own_rows + HALO)
    coarse = row // 4
    phase = row % 4
    near_weight = jnp.where(phase < 2, 5 + 2 * phase, 11 - 2 * phase).astype(f32) / 8.0
    far = jnp.clip(jnp.where(phase < 2, coarse - 1, coarse + 1), 0, coarse_rows - 1)
    base = section_index * (own_rows // 4) - 2
    held = own_rows // 4 + 4
    near_at = jnp.clip(coarse - base, 0, held - 1)
    far_at = jnp.clip(far - base, 0, held - 1)
    validf = valid.astype(f32)
    ownf = own.astype(f32)
    own_at = jnp.where(own, src - HALO, own_rows)
    slot_of = slot + (slot >= gap).astype(jnp.int32)
    inside = ((slot + first >= 0) & (slot + first < fine_total)).astype(f32)
    inside = jnp.broadcast_to(inside, validf.shape)
    ints = jnp.stack(
        [jnp.clip(src, 0, window - 1), near_at, far_at, own_at, slot_of, jnp.broadcast_to(gap, src.shape)], axis=1
    )
    floats = jnp.stack(
        [
            validf,
            ownf,
            near_weight * validf,
            (1.0 - near_weight) * validf,
            near_weight * ownf,
            (1.0 - near_weight) * ownf,
            inside,
        ],
        axis=1,
    )
    batch = cut.shape[0]
    return ints.astype(jnp.int32).reshape(batch, -1), floats.reshape(batch, -1)


def column_sides(v):
    n = v.shape[0]
    col = lax.broadcasted_iota(jnp.int32, v.shape, 0)
    left = jnp.where(col == 0, 0.0, pltpu.roll(v, 1, 0))
    right = jnp.where(col == n - 1, 0.0, pltpu.roll(v, n - 1, 0))
    return left, right


def three_columns(v):
    left, right = column_sides(v)
    return jnp.concatenate([left.astype(bf16), v.astype(bf16), right.astype(bf16)], axis=1)


def decode_kernel(own_rows, cols, chans, red, parts, before, at, itab, ftab, low_top, low, low_end, tgt, colm, colt, rwt, m1, m2, clst, *refs):
    projs, refs = refs[:parts], refs[parts + before:]
    decode_body(at[0], own_rows, cols, chans, red, projs, itab, ftab, low_top, low, low_end, tgt, colm, colt, rwt, m1, m2, clst, *refs)


def decode_body(first, own_rows, cols, chans, red, projs, itab, ftab, low_top, low, low_end, tgt, colm, colt, rwt, m1, m2, clst,
                  up_h, red_h, fst_h, sec_h, g2_h, g1_h, rg_h, pg_o,
                  jc, fc, sl1, rs, tgg, lift, drop, a0, a1, b0, b1,
                w1, rw3, clsb, wb2, wb1u, wb1r, up_o, red_o, fst_o, sec_o, g2_o, g1_o, rg_o, sems):
    m = pl.program_id(0)
    window = own_rows + 2 * HALO
    slots = window + 1
    held = projs[0].shape[1]
    wide = 3 * chans
    redw = jc.shape[2] - wide
    keep = own_rows + 3
    gc2, gc1 = jc.at[:, :, 0:wide], fc
    held_rows = [(up_o, up_h), (red_o, red_h), (fst_o, fst_h), (sec_o, sec_h), (g2_o, g2_h), (g1_o, g1_h), (rg_o, rg_h)]

    def out_copy(k, at):
        here, there = held_rows[k]
        return pltpu.make_async_copy(here.at[0:there.shape[1]], there.at[first + at], sems.at[k])

    @pl.when(m > 0)
    def _():
        for k in range(6):
            out_copy(k, m - 1).wait()

    @pl.when(m == 0)
    def _():
        w1[:, wide + 3 * red:] = jnp.zeros((3, redw - 3 * red, chans), bf16)
        clsb[...] = jnp.zeros(clsb.shape, bf16)
        clsb[0:clst.shape[0]] = clst[...]
        spare = jnp.zeros((redw - 3 * red, chans), bf16)
        rw3[...] = jnp.concatenate([rwt[...]] * 3 + [spare], axis=0).T
        for r in range(3):
            for d in range(3):
                part = slice(d * chans, (d + 1) * chans)
                w1[r, part] = m1[3 * r + d, 0:chans]
                w1[r, wide + d * red:wide + (d + 1) * red] = m1[3 * r + d, chans:]
                tap = 3 * (2 - r) + 2 - d
                wb2[r, part] = m2[tap].T
                wb1u[r, part] = m1[tap, 0:chans].T
            tails = [m1[3 * (2 - r) + d, chans:] for d in range(3)]
            wb1r[r] = jnp.concatenate(tails + [spare], axis=0).T

    def w2(r):
        return m2[3 * r:3 * r + 3].reshape(wide, chans)

    def it(k, j):
        return itab[first + m, k * slots + j]

    def ft(k, j):
        return ftab[first + m, k * slots + j]

    accs = (a0, a1)
    bccs = (b0, b1)

    def staged(blocks, multiply, finish):
        for k, block in enumerate(blocks):
            multiply(*block, accs[k % 2], bccs[k % 2])
            if k:
                finish(*blocks[k - 1], accs[(k - 1) % 2], bccs[(k - 1) % 2])
        k = len(blocks) - 1
        finish(*blocks[k], accs[k % 2], bccs[k % 2])

    def rows_of(ref, lo, n):
        return ref[lo:lo + n].reshape(n * cols, ref.shape[2])

    def dot(a, b):
        return jnp.dot(a, b, preferred_element_type=f32)

    @pl.when(m == 0)
    def _():
        tgg[...] = jnp.zeros(tgg.shape, bf16)

    for i in range(2):
        tgg[it(4, 2 + i)] = low_top[0, HALO][:, i * LANE:(i + 1) * LANE]
        tgg[it(4, own_rows + HALO + i)] = low_end[0, HALO][:, i * LANE:(i + 1) * LANE]
    for i in range(own_rows):
        tgg[it(4, HALO + i)] = tgt[0, i]
    tgg[it(5, 0)] = jnp.zeros((cols, LANE), bf16)

    lane = lax.broadcasted_iota(jnp.int32, (cols, redw), 1)

    def reduce_mul(ref, lo, n, place, acc, _):
        acc[0:n * cols] = dot(ref[0, lo:lo + n].reshape(n * cols, ref.shape[3]), rw3[...])

    def reduce_fin(ref, lo, n, place, acc, _):
        for r in range(n):
            a, slope = silu_and_slope(acc[r * cols:(r + 1) * cols])
            a = a * ft(6, place + r)
            left, right = column_sides(a)
            a = jnp.where(lane < red, left, jnp.where(lane < 2 * red, a, right))
            jc[it(4, place + r), :, wide:] = a.astype(bf16)
            if HALO <= place + r < own_rows + HALO:
                rs[place + r - HALO] = slope.astype(bf16)

    staged(
        [(low_top, 0, HALO, 0)]
        + [(low, lo, n, lo + HALO) for lo, n in split_rows(0, own_rows, 8)]
        + [(low_end, 0, HALO, own_rows + HALO)],
        reduce_mul, reduce_fin,
    )
    jc[it(5, 0), :, wide:] = jnp.zeros((cols, redw), bf16)

    for k in range(held):
        v = sum(p[0, k].astype(f32) for p in projs).astype(bf16)
        lift[k] = dot(colm[...], v)
    for j in range(slots):
        v = (ft(2, j) * lift[it(1, j)] + ft(3, j) * lift[it(2, j)]).astype(bf16)
        for d in range(3):
            jc[j, :, d * chans:(d + 1) * chans] = v[d * cols:(d + 1) * cols]
        if 3 <= j < 3 + keep:
            up_o[j - 3] = v[cols:2 * cols]

    red_o[...] = jc[3:3 + keep, :, wide:]
    out_copy(0, m).start()
    out_copy(1, m).start()

    def first_mul(lo, n, acc, _):
        acc[0:n * cols] = (
            dot(rows_of(jc, lo - 1, n), w1[0]) + dot(rows_of(jc, lo, n), w1[1]) + dot(rows_of(jc, lo + 1, n), w1[2])
        )

    def first_fin(lo, n, acc, _):
        for r in range(n):
            a, slope = silu_and_slope(acc[r * cols:(r + 1) * cols])
            keep_row = ft(0, lo + r)
            a = a * keep_row
            fc[lo + r] = three_columns(a)
            if 3 <= lo + r < 3 + keep:
                fst_o[lo + r - 3] = a.astype(bf16)
            sl1[lo + r] = (slope * keep_row).astype(bf16)

    staged(split_rows(1, slots - 1, 8), first_mul, first_fin)
    out_copy(2, m).start()

    def second_mul(lo, n, acc, bcc):
        acc[0:n * cols] = (
            dot(rows_of(fc, lo - 1, n), w2(0)) + dot(rows_of(fc, lo, n), w2(1)) + dot(rows_of(fc, lo + 1, n), w2(2))
        )
        bcc[0:n * cols] = dot(rows_of(tgg, lo, n), clsb[...])

    def second_fin(lo, n, acc, bcc):
        for r in range(n):
            j = lo + r
            a, slope = silu_and_slope(acc[r * cols:(r + 1) * cols])
            sec_o[it(3, j)] = a.astype(bf16)
            g = bcc[r * cols:(r + 1) * cols] * slope * ft(0, j)
            gc2[j] = three_columns(g)
            if HALO <= j <= own_rows + HALO:
                g2_o[j - HALO] = (g * ft(1, j)).astype(bf16)

    staged(split_rows(2, slots - 2, 8), second_mul, second_fin)
    out_copy(3, m).start()
    out_copy(4, m).start()

    def back2_mul(lo, n, acc, _):
        acc[0:n * cols] = (
            dot(rows_of(gc2, lo - 1, n), wb2[0]) + dot(rows_of(gc2, lo, n), wb2[1]) + dot(rows_of(gc2, lo + 1, n), wb2[2])
        )

    def back2_fin(lo, n, acc, _):
        for r in range(n):
            j = lo + r
            g = acc[r * cols:(r + 1) * cols] * sl1[j].astype(f32)
            gc1[j] = three_columns(g)
            if HALO <= j <= own_rows + HALO:
                g1_o[j - HALO] = (g * ft(1, j)).astype(bf16)

    staged(split_rows(3, slots - 3, 8), back2_mul, back2_fin)
    out_copy(5, m).start()

    drop[...] = jnp.zeros(drop.shape, f32)

    @pl.when(m > 0)
    def _():
        out_copy(6, m - 1).wait()

    def back1_mul(lo, n, acc, bcc):
        acc[0:n * cols] = (
            dot(rows_of(gc1, lo - 1, n), wb1u[0]) + dot(rows_of(gc1, lo, n), wb1u[1]) + dot(rows_of(gc1, lo + 1, n), wb1u[2])
        )
        mid = slice(chans, 2 * chans)
        bcc[0:n * cols] = (
            dot(rows_of(gc1, lo - 1, n)[:, mid], wb1r[0]) + dot(rows_of(gc1, lo, n)[:, mid], wb1r[1])
            + dot(rows_of(gc1, lo + 1, n)[:, mid], wb1r[2])
        )

    def back1_fin(lo, n, acc, bcc):
        for r in range(n):
            j = lo + r
            up = acc[r * cols:(r + 1) * cols]
            near, far = it(1, j), it(2, j)
            drop[near] += ft(4, j) * up
            drop[far] += ft(5, j) * up
            t = bcc[r * cols:(r + 1) * cols]
            left, right = column_sides(t)
            t = jnp.where(lane < red, right, jnp.where(lane < 2 * red, t, left))
            rg_o[it(3, j)] = (t * rs[it(3, j)].astype(f32)).astype(bf16)

    staged(split_rows(HALO, slots - HALO, 8), back1_mul, back1_fin)
    out_copy(6, m).start()

    for k in range(held):
        pg_o[0, k] = dot(colt[...], drop[k].astype(bf16)).astype(bf16)

    @pl.when(m == pl.num_programs(0) - 1)
    def _():
        for k in range(7):
            out_copy(k, m).wait()


def whole(a):
    return pl.BlockSpec(a.shape, lambda *at: (0,) * a.ndim, pipeline_mode=pl.Buffered(1))


def per(shape):
    return pl.BlockSpec((1,) + shape, lambda m, *at: (m,) + (0,) * len(shape))


def per_from(shape):
    return pl.BlockSpec((1,) + shape, lambda m, at: (m + at[0],) + (0,) * len(shape))


def total(shape):
    return pl.BlockSpec(shape, lambda *at: (0,) * len(shape))


def params():
    return pltpu.CompilerParams(vmem_limit_bytes=63 * 2 ** 20)


def saved_shapes(own_rows, cols, chans, red):
    redw = -(-3 * red // LANE) * LANE
    return [(own_rows + 3, cols, chans), (own_rows + 3, cols, redw), (own_rows + 3, cols, chans), (own_rows, cols, chans),
            (own_rows + 1, cols, chans), (own_rows + 1, cols, chans), (own_rows, cols, redw)]


def blank(batch, shapes):
    return tuple(pl.pallas_call(
        lambda *refs: None,
        out_specs=[pl.BlockSpec(memory_space=pl.ANY)] * len(shapes),
        out_shape=[jax.ShapeDtypeStruct((batch,) + s, bf16) for s in shapes],
        name="blank",
    )())


def decode(first, batch, tables, low_top, low_input, low_end, projs, target, reduce_t, merge1_weight, merge2_weight, class_t, earlier):
    ints, floats = tables
    all_batch, own_rows, cols, low_ch = low_input.shape
    window = own_rows + 2 * HALO
    slots = window + 1
    chans = merge2_weight.shape[1]
    red = reduce_t.shape[0]
    held, coarse_cols = projs[0].shape[1], projs[0].shape[2]
    redw = -(-3 * red // LANE) * LANE
    wide = 3 * chans
    colm = upsample_matrix(coarse_cols)
    zero = np.zeros((1, coarse_cols), np.float32)
    colm3 = jnp.asarray(np.concatenate([zero, colm[:-1], colm, colm[1:], zero], axis=0), bf16)
    colt = jnp.asarray(colm.T, bf16)
    keep = own_rows + 3
    smem = pl.BlockSpec(memory_space=pltpu.SMEM)
    hbm = pl.BlockSpec(memory_space=pl.ANY)
    most = max(n for k in range(5) for _, n in split_rows(k, slots - k, 8))
    consts = (colm3, colt, reduce_t, merge1_weight, merge2_weight, class_t)
    shapes = saved_shapes(own_rows, cols, chans, red)
    stage = [(s[0] + (1 if k in (3, 6) else 0),) + s[1:] for k, s in enumerate(shapes)]
    back_shape = (held, coarse_cols, chans)
    saved = pl.pallas_call(
        lambda *refs: decode_kernel(own_rows, cols, chans, red, len(projs), len(earlier), *refs),
        grid_spec=pltpu.PrefetchScalarGridSpec(
            num_scalar_prefetch=1,
            grid=(batch,),
            in_specs=[smem, smem] + [per_from(a.shape[1:]) for a in (low_top, low_input, low_end, target)]
            + [whole(a) for a in consts] + [per(p.shape[1:]) for p in projs] + [hbm] * len(earlier),
            out_specs=[hbm] * len(shapes) + [per(back_shape)],
            scratch_shapes=[
                pltpu.VMEM((slots, cols, wide + redw), bf16), pltpu.VMEM((slots, cols, wide), bf16),
                pltpu.VMEM((slots, cols, chans), bf16), pltpu.VMEM((own_rows + 1, cols, redw), bf16),
                pltpu.VMEM((slots, cols, LANE), bf16),
                pltpu.VMEM((held, 3 * cols, chans), f32), pltpu.VMEM((held, cols, chans), f32),
                pltpu.VMEM((most * cols, chans), f32), pltpu.VMEM((most * cols, chans), f32),
                pltpu.VMEM((most * cols, chans), f32), pltpu.VMEM((most * cols, chans), f32),
                pltpu.VMEM((3, wide + redw, chans), bf16), pltpu.VMEM((low_ch, redw), bf16), pltpu.VMEM((LANE, chans), bf16),
                pltpu.VMEM((3, wide, chans), bf16), pltpu.VMEM((3, wide, chans), bf16), pltpu.VMEM((3, chans, redw), bf16),
            ] + [pltpu.VMEM(s, bf16) for s in stage] + [pltpu.SemaphoreType.DMA((7,))],
        ),
        out_shape=[jax.ShapeDtypeStruct((all_batch,) + s, bf16) for s in shapes] + [jax.ShapeDtypeStruct((batch,) + back_shape, bf16)],
        input_output_aliases={7 + len(consts) + len(projs) + k: k for k in range(len(earlier))},
        compiler_params=params(),
        name="decode",
    )(jnp.full((1,), first, jnp.int32), ints, floats, low_top, low_input, low_end, target, *consts, *projs, *earlier)
    return saved[7], tuple(saved[:7])


def grads_kernel(own_rows, cols, chans, red, before, up, red3, fst, sec, g2, g1, rg, low, tgt, clst, rwt, *refs):
    earlier = refs[:before]
    packed, lowgrad, logits, o1, o2, oc, orr, upc, fcc = refs[before:]
    m = pl.program_id(0)
    keep = own_rows + 3
    wide = 3 * chans
    span = own_rows + 1
    classes = clst.shape[0]

    @pl.when(m == 0)
    def _():
        o1[...] = jnp.zeros(o1.shape, f32)
        o2[...] = jnp.zeros(o2.shape, f32)
        oc[...] = jnp.zeros(oc.shape, f32)
        orr[...] = jnp.zeros(orr.shape, f32)

    def tdot(a, b):
        return lax.dot_general(a, b, (((0,), (0,)), ((), ())), preferred_element_type=f32)

    for j in range(keep):
        upc[j] = three_columns(up[0, j].astype(f32))
    for j in range(keep):
        fcc[j] = three_columns(fst[0, j].astype(f32))

    def flat(v):
        return v.reshape(v.shape[0] * cols, v.shape[2])

    gg1 = flat(g1[0])
    for dy in range(3):
        o1[dy, 0:wide] += tdot(flat(upc[dy:dy + span]), gg1)
        o1[dy, wide:] += tdot(flat(red3[0, dy:dy + span]), gg1)
    gg2 = flat(g2[0])
    for dy in range(3):
        o2[dy] += tdot(flat(fcc[dy:dy + span]), gg2)
    oc[...] += tdot(flat(sec[0]), flat(tgt[0]))
    orr[...] += tdot(flat(low[0]), flat(rg[0]))
    spare = jnp.zeros((rg.shape[3] - 3 * red, chans), bf16)
    rb3 = jnp.concatenate([rwt[...]] * 3 + [spare], axis=0)
    for r in range(own_rows):
        lowgrad[0, r] = jnp.dot(rg[0, r], rb3, preferred_element_type=f32)
        lt = lax.dot_general(clst[...], sec[0, r], (((1,), (1,)), ((), ())), preferred_element_type=f32)
        logits[0, :, r] = lt

    @pl.when(m == pl.num_programs(0) - 1)
    def _():
        rows = chans + red
        for dy in range(3):
            for d in range(3):
                at = (3 * dy + d) * rows
                packed[at:at + chans] = o1[dy, d * chans:(d + 1) * chans].astype(bf16)
                packed[at + chans:at + rows] = o1[dy, wide + d * red:wide + (d + 1) * red].astype(bf16)
            packed[9 * rows + dy * wide:9 * rows + (dy + 1) * wide] = o2[dy].astype(bf16)
        at = 9 * rows + 3 * wide
        packed[at:] = jnp.zeros((packed.shape[0] - at, chans), bf16)
        t = orr[...].T
        packed[at:at + red] = (t[0:red] + t[red:2 * red] + t[2 * red:3 * red]).astype(bf16)
        packed[at + red:at + red + 32] = oc[...].T[0:32].astype(bf16)
        if before:
            packed[...] = (packed[...].astype(f32) + earlier[0][...].astype(f32)).astype(bf16)


def packed_rows(chans, red):
    return 9 * (chans + red) + 9 * chans + red + 32


def decode_grads(first, saved, low_input, target, reduce_t, class_t, earlier):
    up, red3, fst, sec, g2, g1, rg = saved
    batch = up.shape[0]
    all_batch, own_rows, cols, low_ch = low_input.shape
    chans = up.shape[3]
    redw = red3.shape[3]
    red = reduce_t.shape[0]
    classes = class_t.shape[0]
    wide = 3 * chans
    keep = own_rows + 3
    rows = packed_rows(chans, red)
    hbm = pl.BlockSpec(memory_space=pl.ANY)
    tots = [(3, wide + redw, chans), (3, wide, chans), (chans, LANE), (low_ch, redw)]
    pers = [(own_rows, cols, low_ch), (classes, own_rows, cols)]
    packed, lowgrad, logits = pl.pallas_call(
        lambda *refs: grads_kernel(own_rows, cols, chans, red, 3 if earlier else 0, *refs),
        grid=(batch,),
        in_specs=[per((keep, cols, chans)), per((keep, cols, redw)), per((keep, cols, chans)), per((own_rows, cols, chans)),
                  per((own_rows + 1, cols, chans)), per((own_rows + 1, cols, chans)), per((own_rows, cols, redw)),
                  per((own_rows, cols, low_ch)), per(target.shape[1:]), whole(class_t), whole(reduce_t)]
        + ([whole(earlier[0]), hbm, hbm] if earlier else []),
        out_specs=[total((rows, chans))] + [per(s) for s in pers],
        out_shape=[jax.ShapeDtypeStruct((rows, chans), bf16)] + [jax.ShapeDtypeStruct((all_batch,) + s, f32) for s in pers],
        input_output_aliases={12: 1, 13: 2} if earlier else {},
        scratch_shapes=[pltpu.VMEM(s, f32) for s in tots]
        + [pltpu.VMEM((keep, cols, wide), bf16), pltpu.VMEM((keep, cols, wide), bf16)],
        compiler_params=params(),
        name="decode_grads",
        cost_estimate=pl.CostEstimate(flops=1, bytes_accessed=1, transcendentals=1),
    )(up, red3, fst, sec, g2, g1, rg, low_input, target, class_t, reduce_t, *(earlier or ()))
    return packed, lowgrad, logits


def unpack_decoder(bit, mine, other, chans, red, classes):
    rows = chans + red
    half = mine.shape[0]
    at = 9 * rows + 9 * chans
    shapes = [(9, rows, chans), (9, chans, chans), (red, chans), (classes, chans)]

    def kernel(bit, a, b, m1, m2, rw, cw, v):
        v[pl.ds(pl.multiple_of(bit[0] * half, 16), half)] = a[...]
        v[pl.ds(pl.multiple_of((1 - bit[0]) * half, 16), half)] = b[...]
        for t in range(9):
            m1[t] = v[t * rows:(t + 1) * rows].astype(f32)
            m2[t] = v[9 * rows + t * chans:9 * rows + (t + 1) * chans].astype(f32)
        rw[...] = v[at:at + red].astype(f32)
        cw[...] = v[at + red:at + red + 32].astype(f32)[0:classes]

    m1, m2, rw, cw = pl.pallas_call(
        kernel,
        grid=(1,),
        in_specs=[pl.BlockSpec(memory_space=pltpu.SMEM), whole(mine), whole(other)],
        out_specs=[total(s) for s in shapes],
        out_shape=[jax.ShapeDtypeStruct(s, f32) for s in shapes],
        scratch_shapes=[pltpu.VMEM((2 * half, chans), bf16)],
        compiler_params=params(),
        name="unpack_decoder",
    )(bit, mine, other)
    return m1, m2, rw.T, cw.T


atrous_rates = (6, 12, 18)
epsilon = 1e-05


def tap_list():
    listed = [(0, 0, 0)]
    for branch_index, rate_value in enumerate(atrous_rates):
        for step_rows in (-1, 0, 1):
            for step_cols in (-1, 0, 1):
                listed.append((rate_value * step_rows, rate_value * step_cols, branch_index + 1))
    return listed


def pixel_places(batch, height, width):
    pixel = np.arange(height * width)
    places = np.stack([np.tile(pixel // width, batch), np.tile(pixel % width, batch), np.repeat(np.arange(batch), height * width)])
    return jnp.asarray(np.pad(places, ((0, 5), (0, 0))), jnp.int32)


class Pixels:
    def __init__(self, places, cuts, batch, height, width):
        self.row, self.col, self.canvas = places[0:1], places[1:2], places[2:3]
        self.height, self.width = height, width
        cut = jnp.full(self.row.shape, cuts[0], jnp.int32)
        for m in range(1, batch):
            cut = jnp.where(self.canvas == m, cuts[m], cut)
        self.cut = cut
        self.band = self.row >= cut

    def valid(self, dr, dc):
        row, col = self.row + dr, self.col + dc
        inside = (row >= 0) & (row < self.height) & (col >= 0) & (col < self.width)
        same = jnp.where(row >= self.cut, 1, 0) == jnp.where(self.band, 1, 0)
        return jnp.where(inside & same, 1.0, 0.0)

    def image(self):
        return IMAGES * self.canvas + jnp.where(self.band, 1, 0)


def image_counts(cuts, batch, height, width):
    index = lax.broadcasted_iota(jnp.int32, (IMAGES * batch, 1), 0)
    out = jnp.zeros((IMAGES * batch, 1), f32)
    for m in range(batch):
        first = cuts[m] * width
        out = jnp.where(index == IMAGES * m, first.astype(f32), out)
        out = jnp.where(index == IMAGES * m + 1, (height * width - first).astype(f32), out)
    return jnp.maximum(out, 1.0)


def branch_kernel(taps, batch, height, width, cuts, x, w, places, pw, br_o, mom_o, pooled_o, y, pool, mom):
    i = pl.program_id(0)
    last = pl.num_programs(0) - 1
    block = x.shape[0]
    total = y.shape[1]
    pixels = total // batch
    own = pw.shape[0]
    at = pl.multiple_of(i * block, block)

    @pl.when(i == 0)
    def _():
        pool[...] = jnp.zeros(pool.shape, f32)
        mom[...] = jnp.zeros(mom.shape, f32)

    def nt(a, b):
        return lax.dot_general(a, b, (((1,), (1,)), ((), ())), preferred_element_type=f32)

    canvas, row = places[2:3, pl.ds(at, block)], places[0:1, pl.ds(at, block)]
    cut = jnp.full(row.shape, cuts[0], jnp.int32)
    for m in range(1, batch):
        cut = jnp.where(canvas == m, cuts[m], cut)
    image = IMAGES * canvas + jnp.where(row >= cut, 1, 0)
    index = lax.broadcasted_iota(jnp.int32, (IMAGES * batch, block), 0)
    member = jnp.where(image == index, 1.0, 0.0).astype(bf16)
    pool[...] += jnp.dot(member, x[...], preferred_element_type=f32)

    @pl.when(i < last)
    def _():
        y[:, pl.ds(at, block)] = nt(w[...], x[...])

    def keep(m, b, v):
        part = slice(b * own, (b + 1) * own)
        br_o[m, part] = v
        mom[part, m:m + 1] = jnp.sum(v, axis=1, keepdims=True)
        mom[part, batch + m:batch + m + 1] = jnp.sum(v * v, axis=1, keepdims=True)

    @pl.when(i == last)
    def _():
        px = Pixels(places, cuts, batch, height, width)
        spans = []
        for b in range(4):
            mine = [t for t, tap in enumerate(taps) if tap[2] == b]
            spans.append((mine[0], mine[-1] + 1))

        def multiply(b):
            lo, hi = spans[b][0] * own, spans[b][1] * own
            y[lo:hi, total - block:] = nt(w[lo:hi], x[...])

        def finish(b):
            acc = None
            for t in range(*spans[b]):
                dr, dc, _ = taps[t]
                v = y[t * own:(t + 1) * own]
                shift = dr * width + dc
                if shift:
                    v = pltpu.roll(v, (-shift) % total, 1) * px.valid(dr, dc)
                acc = v if acc is None else acc + v
            for m in range(batch):
                keep(m, b, acc[:, m * pixels:(m + 1) * pixels])

        multiply(0)
        multiply(1)
        multiply(2)
        finish(0)
        finish(1)
        multiply(3)
        finish(2)
        finish(3)
        pooled = (pool[...] / image_counts(cuts, batch, height, width)).astype(bf16)
        pooled_o[...] = pooled
        po = nt(pw[...], pooled)
        for m in range(batch):
            band = px.band[:, m * pixels:(m + 1) * pixels]
            keep(m, 4, jnp.where(band, po[:, IMAGES * m + 1:IMAGES * m + 2], po[:, IMAGES * m:IMAGES * m + 1]))
        mom_o[...] = mom[...].T[0:mom_o.shape[0]]


def aspp_forward(cuts, x, wt, pwt, batch, height, width):
    all_pixels, in_chans = x.shape
    pixels = height * width
    own = pwt.shape[0]
    taps = tap_list()
    block = all_pixels // 3 if all_pixels % 3 == 0 and (all_pixels // 3) % LANE == 0 else all_pixels
    places = pixel_places(batch, height, width)
    outs = [((batch, 5 * own, pixels), f32), ((2 * batch, 5 * own), f32), ((IMAGES * batch, in_chans), bf16)]
    return pl.pallas_call(
        lambda *refs: branch_kernel(taps, batch, height, width, *refs),
        grid=(all_pixels // block,),
        in_specs=[pl.BlockSpec(memory_space=pltpu.SMEM), pl.BlockSpec((block, in_chans), lambda i: (i, 0)),
                  whole(wt), whole(places), whole(pwt)],
        out_specs=[total(s) for s, _ in outs],
        out_shape=[jax.ShapeDtypeStruct(s, d) for s, d in outs],
        scratch_shapes=[pltpu.VMEM((len(taps) * own, all_pixels), f32), pltpu.VMEM((IMAGES * batch, in_chans), f32),
                        pltpu.VMEM((5 * own, LANE), f32)],
        compiler_params=params(),
        name="aspp_forward",
    )(cuts, x, wt, places, pwt)


def column(t, m):
    if isinstance(m, int):
        return t[:, m:m + 1]
    lane = lax.broadcasted_iota(jnp.int32, t.shape, 1)
    return jnp.sum(jnp.where(lane == m, t, 0.0), axis=1, keepdims=True)


def norm_columns(stats, scale, m, batch, count):
    t = stats[...].T
    mean = column(t, m) / count
    inv_std = lax.rsqrt(column(t, batch + m) / count - mean * mean + epsilon)
    s = scale[...].T
    half = s.shape[1] // 2
    gain = jnp.concatenate([s[:, k:k + 1] for k in range(half)], axis=0)
    shift = jnp.concatenate([s[:, half + k:half + k + 1] for k in range(half)], axis=0)
    return mean, inv_std, gain, shift


def project_kernel(group, count, coarse_rows, at_ref, offsets, br, stats, scale, proj, *refs):
    outs, rows = refs[:-1], refs[-1]
    batch = stats.shape[0] // 2
    height, width, chans = rows.shape[0] - 4, rows.shape[1], rows.shape[2]
    held = coarse_rows + 4
    rows[0:2] = jnp.zeros((2, width, chans), f32)
    rows[height + 2:] = jnp.zeros((2, width, chans), f32)
    for at in range(group):
        mean, inv_std, gain, shift = norm_columns(stats, scale, at_ref[0] + at, batch, count)
        active, _ = silu_and_slope((br[at] - mean) * inv_std * gain + shift)
        partial = lax.dot_general(active.astype(bf16), proj[...], (((0,), (0,)), ((), ())), preferred_element_type=f32)
        rows[2:height + 2] = partial.reshape(height, width, chans)
        for k, o in enumerate(outs):
            o[at] = rows[pl.ds(offsets[k], held)].astype(bf16)


def project(first, group, offsets, br, stats, scale, proj, count, coarse_rows, parts, height, width):
    chans = proj.shape[1]
    shape = (group, coarse_rows + 4, width, chans)
    pixels = br.shape[2]
    return pl.pallas_call(
        lambda *refs: project_kernel(group, count, coarse_rows, *refs),
        grid_spec=pltpu.PrefetchScalarGridSpec(
            num_scalar_prefetch=1,
            grid=(1,),
            in_specs=[pl.BlockSpec(memory_space=pltpu.SMEM), pl.BlockSpec((pl.Element(group), pl.Element(br.shape[1]), pl.Element(pixels)), lambda i, at: (at[0], 0, 0)),
                      whole(stats), whole(scale), whole(proj)],
            out_specs=[total(shape)] * parts,
            scratch_shapes=[pltpu.VMEM((height + 4, width, chans), f32)],
        ),
        out_shape=[jax.ShapeDtypeStruct(shape, bf16)] * parts,
        compiler_params=params(),
        name="project",
    )(jnp.full((1,), first, jnp.int32), offsets, br, stats, scale, proj)


def norm_back_kernel(count, parts, at_ref, offsets, br, stats, scale, proj, earlier, sums_before, *refs):
    pieces = refs[:parts]
    grad_o, sums_o, projgrad_o, rows, sums = refs[parts:]
    height, width, chans = rows.shape[0] - 4, rows.shape[1], rows.shape[2]
    group, held = pieces[0].shape[0], pieces[0].shape[1]
    batch = stats.shape[0] // 2
    sums[...] = jnp.zeros(sums.shape, f32)
    projgrad = earlier[...]
    for at in range(group):
        m = at_ref[0] + at
        rows[...] = jnp.zeros(rows.shape, f32)
        for k, piece in enumerate(pieces):
            rows[pl.ds(offsets[k], held)] += piece[at].astype(f32)
        grad = rows[2:height + 2].reshape(height * width, chans).astype(bf16)
        mean, inv_std, gain, shift = norm_columns(stats, scale, m, batch, count)
        scaled = (br[at] - mean) * inv_std
        active, slope = silu_and_slope(scaled * gain + shift)
        back = lax.dot_general(proj[...], grad, (((1,), (1,)), ((), ())), preferred_element_type=f32) * slope
        grad_o[at] = back
        lane = lax.broadcasted_iota(jnp.int32, sums.shape, 1)
        products = jnp.sum(back * scaled, axis=1, keepdims=True)
        sums[...] += jnp.where(lane == m, products, jnp.where(lane == batch + m, jnp.sum(back, axis=1, keepdims=True), 0.0))
        projgrad = projgrad + jnp.dot(active.astype(bf16), grad, preferred_element_type=f32)
    projgrad_o[...] = projgrad
    sums_o[...] = sums_before[...] + sums[...].T[0:sums_o.shape[0]]


def norm_back(first, offsets, br, stats, scale, proj, earlier, sums_before, pieces, count, height, width):
    batch, chans5, pixels = br.shape
    group = pieces[0].shape[0]
    outs = [((group, chans5, pixels), f32), (stats.shape, f32), (proj.shape, f32)]
    return pl.pallas_call(
        lambda *refs: norm_back_kernel(count, len(pieces), *refs),
        grid_spec=pltpu.PrefetchScalarGridSpec(
            num_scalar_prefetch=1,
            grid=(1,),
            in_specs=[pl.BlockSpec(memory_space=pltpu.SMEM), pl.BlockSpec((pl.Element(group), pl.Element(chans5), pl.Element(pixels)), lambda i, at: (at[0], 0, 0)),
                      whole(stats), whole(scale), whole(proj), whole(earlier), whole(sums_before)] + [whole(p) for p in pieces],
            out_specs=[total(s) for s, _ in outs],
            scratch_shapes=[pltpu.VMEM((height + 4, width, proj.shape[1]), f32), pltpu.VMEM((chans5, LANE), f32)],
        ),
        out_shape=[jax.ShapeDtypeStruct(s, d) for s, d in outs],
        compiler_params=params(),
        name="norm_back",
    )(jnp.full((1,), first, jnp.int32), offsets, br, stats, scale, proj, earlier, sums_before, *pieces)


def weight_grad_kernel(taps, groups, height, width, count, cuts, stats, scale, sums, places, projgrad, x_hbm, br_hbm, *refs):
    backs = refs[:groups]
    wg_hbm, tg_hbm, pg_o, both, x, tg, wg, br, back, sems, in_sems = refs[groups:]
    batch = br.shape[0]
    owner = [(g, k) for g, part in enumerate(backs) for k in range(part.shape[0])]

    def in_copies(m):
        g, k = owner[m]
        return (pltpu.make_async_copy(br_hbm.at[m], br.at[m], in_sems.at[m]),
                pltpu.make_async_copy(backs[g].at[k], back.at[m], in_sems.at[batch + m]))

    for m in range(batch):
        for copy in in_copies(m):
            copy.start()
    own = pg_o.shape[0]
    pixels = br.shape[2]
    rows, all_pixels = tg.shape
    in_chans = x.shape[1]
    filled = (len(taps) + 1) * own
    x_copy = pltpu.make_async_copy(x_hbm, x, sems.at[0])
    x_copy.start()
    px = Pixels(places, cuts, batch, height, width)
    pool_grad = jnp.zeros((own, LANE), f32)
    lane = lax.broadcasted_iota(jnp.int32, (own, LANE), 1)
    t = sums[...].T
    for m in range(batch):
        for copy in in_copies(m):
            copy.wait()
        mean, inv_std, gain, _ = norm_columns(stats, scale, m, batch, count)
        gain_sum, shift_sum = t[:, m:m + 1], t[:, batch + m:batch + m + 1]
        scaled = (br[m] - mean) * inv_std
        grad = inv_std * gain * (back[m] - (shift_sum + scaled * gain_sum) / count)
        both[0:4 * own, m * pixels:(m + 1) * pixels] = grad[0:4 * own]
        pool = grad[4 * own:]
        band = px.band[:, m * pixels:(m + 1) * pixels]
        upper = jnp.sum(jnp.where(band, 0.0, pool), axis=1, keepdims=True).astype(bf16).astype(f32)
        lower = jnp.sum(jnp.where(band, pool, 0.0), axis=1, keepdims=True).astype(bf16).astype(f32)
        pool_grad = jnp.where(lane == IMAGES * m, upper, pool_grad)
        pool_grad = jnp.where(lane == IMAGES * m + 1, lower, pool_grad)
        many = (cuts[m] * width).astype(f32)
        spread = jnp.where(band, lower / jnp.maximum(height * width - many, 1.0), upper / jnp.maximum(many, 1.0))
        both[4 * own:, m * pixels:(m + 1) * pixels] = spread
    pg_o[...] = pool_grad[:, 0:pg_o.shape[1]].astype(bf16)

    for k, (dr, dc, b) in enumerate(taps):
        v = both[b * own:(b + 1) * own]
        shift = dr * width + dc
        if shift:
            v = pltpu.roll(v * px.valid(dr, dc), shift % all_pixels, 1)
        tg[k * own:(k + 1) * own] = v.astype(bf16)
    tg[filled - own:] = both[4 * own:].astype(bf16)
    tg_copy = pltpu.make_async_copy(tg, tg_hbm, sems.at[1])
    tg_copy.start()
    x_copy.wait()
    chans = projgrad.shape[1]
    some = projgrad.shape[0] * chans // in_chans
    step = 512 if in_chans % 512 == 0 else in_chans
    wg[filled:] = jnp.zeros((wg.shape[0] - filled, in_chans), bf16)
    for k in range(in_chans // chans):
        wg[filled:filled + some, k * chans:(k + 1) * chans] = projgrad[k * some:(k + 1) * some].astype(bf16)

    def out_copy(n):
        part = pl.ds(pl.multiple_of(n * step, step), step)
        return pltpu.make_async_copy(wg.at[:, part], wg_hbm.at[:, part], sems.at[2 + n])

    def multiply(n, _):
        part = pl.ds(pl.multiple_of(n * step, step), step)
        wg[0:filled, part] = jnp.dot(tg[...], x[:, part], preferred_element_type=f32).astype(bf16)
        out_copy(n).start()
        return 0

    lax.fori_loop(0, in_chans // step, multiply, 0)
    tg_copy.wait()
    for n in range(in_chans // step):
        out_copy(n).wait()


def aspp_weight_grads(rows, cuts, x, br, stats, scale, sums, projgrad, backs, count, height, width):
    all_pixels, in_chans = x.shape
    batch, chans5, pixels = br.shape
    own = chans5 // 5
    places = pixel_places(batch, height, width)
    groups = len(backs)
    hbm = pl.BlockSpec(memory_space=pl.ANY)
    outs = [(rows, in_chans), ((len(tap_list()) + 1) * own, all_pixels), (own, IMAGES * batch)]
    return pl.pallas_call(
        lambda *refs: weight_grad_kernel(tap_list(), groups, height, width, count, *refs),
        grid=(1,),
        in_specs=[pl.BlockSpec(memory_space=pltpu.SMEM)] + [whole(v) for v in (stats, scale, sums, places, projgrad)]
        + [hbm] * (2 + len(backs)),
        out_specs=[hbm, hbm, total(outs[2])],
        out_shape=[jax.ShapeDtypeStruct(s, bf16) for s in outs],
        scratch_shapes=[pltpu.VMEM((chans5, all_pixels), f32), pltpu.VMEM((all_pixels, in_chans), bf16),
                        pltpu.VMEM(outs[1], bf16), pltpu.VMEM(outs[0], bf16),
                        pltpu.VMEM(br.shape, f32), pltpu.VMEM(br.shape, f32),
                        pltpu.SemaphoreType.DMA((2 + in_chans // 512 + 1,)), pltpu.SemaphoreType.DMA((2 * batch,))],
        compiler_params=params(),
        name="aspp_weight_grads",
    )(cuts, stats, scale, sums, places, projgrad, x, br, *backs)


def unpack_weights(summed, wide, own, proj_shape):
    rows, in_chans = summed.shape
    block = 512 if in_chans % 512 == 0 else in_chans
    chans = proj_shape[1]
    pieces = block // chans
    some = proj_shape[0] * chans // in_chans

    def kernel(v, wide_o, pool_o, proj_o):
        wide_o[...] = v[0:wide].astype(f32)
        pool_o[...] = v[wide:wide + own].astype(f32)
        tail = v[wide + own:].astype(f32)
        for k in range(pieces):
            proj_o[k * some:(k + 1) * some] = tail[0:some, k * chans:(k + 1) * chans]

    def lanes(a):
        return pl.BlockSpec((a, block), lambda j: (0, j))

    return pl.pallas_call(
        kernel,
        grid=(in_chans // block,),
        in_specs=[lanes(rows)],
        out_specs=[lanes(wide), lanes(own), pl.BlockSpec((some * pieces, chans), lambda j: (j, 0))],
        out_shape=[jax.ShapeDtypeStruct(s, f32) for s in ((wide, in_chans), (own, in_chans), proj_shape)],
        compiler_params=params(),
        name="unpack_weights",
    )(summed)


def input_grad_kernel(batch, span, height, width, at, cuts, tg, w, pg, pw, band, o):
    i = pl.program_id(0)
    pixels = height * width
    v = lax.dot_general(tg[...], w[...], (((0,), (0,)), ((), ())), preferred_element_type=f32)
    image = lax.dot_general(pg[...], pw[...], (((0,), (0,)), ((), ())), preferred_element_type=f32)
    image = image / image_counts(cuts, batch, height, width)
    index = lax.broadcasted_iota(jnp.int32, (IMAGES * batch, 1), 0)
    row = band[...]
    for k in range(span):
        m = i * span + k
        first = jnp.sum(jnp.where(index == IMAGES * m, image, 0.0), axis=0, keepdims=True)
        second = jnp.sum(jnp.where(index == IMAGES * m + 1, image, 0.0), axis=0, keepdims=True)
        part = slice(k * pixels, (k + 1) * pixels)
        o[part] = (v[part] + jnp.where(row >= cuts[m], second, first)).astype(bf16)


def aspp_input_grad(place, cuts, tg, wt, pool_grad, pwt, parts, height, width):
    rows, in_chans = wt.shape
    all_pixels = tg.shape[1]
    own = pwt.shape[0]
    pixels = height * width
    batch = all_pixels // pixels
    block = in_chans // parts
    span = 2 if (2 * pixels) % LANE == 0 and batch % 2 == 0 else batch
    row_column = jnp.asarray(np.arange(pixels)[:, None] // width, jnp.int32)
    return pl.pallas_call(
        lambda *refs: input_grad_kernel(batch, span, height, width, *refs),
        grid_spec=pltpu.PrefetchScalarGridSpec(
            num_scalar_prefetch=2,
            grid=(batch // span,),
            in_specs=[
                pl.BlockSpec((rows, span * pixels), lambda i, at, cuts: (0, i)),
                pl.BlockSpec((rows, block), lambda i, at, cuts: (0, at[0])),
                whole(pool_grad),
                pl.BlockSpec((own, block), lambda i, at, cuts: (0, at[0])),
                whole(row_column),
            ],
            out_specs=pl.BlockSpec((span * pixels, block), lambda i, at, cuts: (i, 0)),
        ),
        out_shape=jax.ShapeDtypeStruct((all_pixels, block), bf16),
        compiler_params=params(),
        name="aspp_input_grad",
        cost_estimate=pl.CostEstimate(flops=1, bytes_accessed=1, transcendentals=1),
    )(place, cuts, tg, wt, pool_grad, pwt, row_column)


def doubled_sum(value, axis):
    size = lax.axis_size(axis)
    step = 1
    while step < size:
        value = value + lax.ppermute(value, axis, [(i, i ^ step) for i in range(size)])
        step *= 2
    return value


def exchanged(pieces, axis):
    size = lax.axis_size(axis)
    return [pieces[0]] + [lax.ppermute(pieces[k], axis, [(i, i ^ k) for i in range(size)]) for k in range(1, size)]


def added(a, b):
    return (a.astype(f32) + b.astype(f32)).astype(bf16)


def scatter_sum(value, axis, unit):
    size = lax.axis_size(axis)
    count = size // unit
    me = lax.axis_index(axis)
    rows = value.shape[0] // count
    out = None
    for k in range(count):
        piece = lax.dynamic_slice_in_dim(value, ((me // unit) ^ k) * rows, rows, 0)
        if k:
            piece = lax.ppermute(piece, axis, [(i, i ^ (k * unit)) for i in range(size)])
        out = piece.astype(f32) if out is None else out + piece.astype(f32)
    return out.astype(bf16)


def gather(value, axis, unit, beside=()):
    size = lax.axis_size(axis)
    count = size // unit
    me = lax.axis_index(axis)
    got = [value] + [lax.ppermute(value, axis, [(i, i ^ (k * unit)) for i in range(size)]) for k in range(1, count)]
    rows = value.shape[0]
    got, beside = lax.optimization_barrier((got, beside))
    out = jnp.zeros((count * rows,) + value.shape[1:], value.dtype)
    for k, piece in enumerate(got):
        out = lax.dynamic_update_slice_in_dim(out, piece, ((me // unit) ^ k) * rows, 0)
    return out, beside


def tied(value, *others):
    return lax.optimization_barrier((value,) + others)[0]


def local(aspp_input, low_input, aspp_ids, low_ids, aspp_weight, pool_weight, bn_gain, bn_shift, projection_matrix,
          reduce_weight, merge1_weight, merge2_weight, class_weight, logit_grad):
    section = lax.axis_index("section")
    sections = lax.axis_size("section")
    batch, height, width, in_chans = aspp_input.shape
    taps, own = aspp_weight.shape[1], aspp_weight.shape[2]
    branches = bn_gain.shape[0]
    chans = projection_matrix.shape[2]
    red = reduce_weight.shape[1]
    classes = class_weight.shape[1]
    fine_rows, fine_cols = low_input.shape[1], low_input.shape[2]
    pixels = height * width
    count = pixels * lax.axis_size("dp")
    coarse_rows = fine_rows // 4
    groups = [(0, batch - 1), (batch - 1, 1)]

    x = aspp_input.reshape(batch * pixels, in_chans)
    wt = jnp.transpose(aspp_weight, (1, 2, 0)).reshape(taps * own, in_chans)
    pwt = pool_weight.T
    proj = projection_matrix.reshape(branches * own, chans)
    cuts = jnp.sum((aspp_ids[:, :, 0] == 0).astype(jnp.int32), axis=1)
    br, moments, pooled = aspp_forward(cuts, x, wt, pwt, batch, height, width)

    down = [(i, i + 1) for i in range(sections - 1)]
    up = [(i + 1, i) for i in range(sections - 1)]
    target = jnp.pad(logit_grad, ((0, 0), (0, 0), (0, 0), (0, LANE - classes)))

    def rim(low_rows, target_rows):
        paired = jnp.concatenate([target_rows[:, 0:1], target_rows[:, 1:2]], axis=3)
        return jnp.concatenate([low_rows, paired], axis=1)

    top = lax.ppermute(rim(low_input[:, -HALO:], target[:, -2:]), "section", down)
    end = lax.ppermute(rim(low_input[:, :HALO], target[:, :2]), "section", up)
    distance = jnp.arange(sections, dtype=jnp.int32)
    offsets = (section ^ distance) * coarse_rows

    moments, top, end = lax.optimization_barrier((moments, top, end))
    stats = doubled_sum(moments, "dp")
    tables = row_tables(4 * tied(cuts, stats), low_ids.shape[1], section, fine_rows, height)
    scale = jnp.concatenate([bn_gain, bn_shift], axis=0)
    saved = blank(batch, saved_shapes(fine_rows, fine_cols, chans, red))
    parts = []
    for first, size in groups:
        at = tied(offsets, target, *tables, saved[0]) if parts else offsets
        parts.append(project(first, size, at, br, stats, scale, proj, count, coarse_rows, sections, height, width))
    projs = [exchanged(p, "section") for p in parts]
    projs[0][0] = tied(projs[0][0], *[p[0] for p in parts[1:]])
    pieces = []
    for g, (first, size) in enumerate(groups):
        pgrad, saved = decode(first, size, tables, top, low_input, end, projs[g], target, reduce_weight.T,
                              merge1_weight, merge2_weight, class_weight.T, saved)
        if g + 1 < len(groups):
            pgrad, *projs[g + 1] = lax.optimization_barrier((pgrad, *projs[g + 1]))
        pieces.append(exchanged([pgrad] * sections, "section"))
    backs = []
    projgrad, sums = jnp.zeros(proj.shape, f32), jnp.zeros(stats.shape, f32)
    for (first, size), piece in zip(groups, pieces):
        back, sums, projgrad = norm_back(first, offsets, br, stats, scale, proj, projgrad, sums, piece, count, height, width)
        backs.append(back)
    sums = doubled_sum(sums, "dp")
    filled = (taps + 1) * own
    rows = -(-(filled + projgrad.size // in_chans) // 32) * 32
    grads, tg, pool_grad = aspp_weight_grads(rows, cuts, x, br, stats, scale, sums, projgrad, backs, count, height, width)

    order = list(reversed(range(sections)))
    received = {}

    def input_of(k, tg):
        place = (section ^ k).reshape(1).astype(jnp.int32)
        return aspp_input_grad(place, cuts, tg, wt, pool_grad, pwt, sections, height, width)

    def sent(piece, k):
        return lax.ppermute(piece, "section", [(i, i ^ k) for i in range(sections)]) if k else piece

    share = lax.psum_scatter(grads, "dp", tiled=True)
    early, late = order[:len(order) // 2], order[len(order) // 2:]
    piece = input_of(early[0], tied(tg, grads))
    far = sent(piece, early[0])
    first = tied(saved[0], piece)
    packed, low_grad, logits = decode_grads(0, (first,) + saved[1:], low_input, target, reduce_weight.T, class_weight.T, None)
    swap = [(i, i ^ 1) for i in range(lax.axis_size("dp"))]
    bit = lax.axis_index("dp") % 2
    half = packed.shape[0] // 2
    mine = lax.dynamic_slice_in_dim(packed, bit * half, half, 0)
    packed = added(mine, lax.ppermute(lax.dynamic_slice_in_dim(packed, (1 - bit) * half, half, 0), "dp", swap))
    packed, far, tied_tg = lax.optimization_barrier((packed, far, tg))
    packed = scatter_sum(packed, "section", 1)
    received[early[0]] = far
    for k in early[1:]:
        received[k] = input_of(k, tied_tg)
        packed = tied(packed, received[k])
    held = tuple(received[k] for k in early)
    (share, packed), held = lax.optimization_barrier(((share, packed), held))
    received.update(zip(early, held))

    summed = lax.all_gather(share, "dp", tiled=True)
    for k in early[1:]:
        received[k] = sent(received[k], k)
    steps = [lambda v: scatter_sum(v, "dp", 2), lambda v: gather(v, "dp", 2)[0]]
    for k in late:
        packed, tied_tg = lax.optimization_barrier((packed, tg) + ((piece,) if k != late[0] else ()))[:2]
        piece = input_of(k, tied_tg)
        if steps:
            packed = steps.pop(0)(packed)
        packed, piece = lax.optimization_barrier((packed, piece))
        received[k] = sent(piece, k)
    input_grad = sum(received[k].astype(f32) for k in order).reshape(batch, height, width, in_chans // sections)
    packed, input_grad = gather(packed, "section", 1, input_grad)
    packed, summed = lax.optimization_barrier((packed, summed))
    other = lax.ppermute(packed, "dp", swap)
    merge1_grad, merge2_grad, reduce_grad, class_grad = unpack_decoder(bit.reshape(1).astype(jnp.int32), packed, other, chans, red,
                                                                       classes)

    wide, pool_weight_grad, proj_weight_grad = unpack_weights(summed, taps * own, own, proj.shape)
    sums = jnp.sum(sums.reshape(2, batch, -1), axis=1)
    return (
        jnp.transpose(logits, (0, 2, 3, 1)),
        input_grad,
        low_grad,
        jnp.transpose(wide.reshape(taps, own, in_chans), (2, 0, 1)),
        pool_weight_grad.T,
        sums[0].reshape(branches, own),
        sums[1].reshape(branches, own),
        proj_weight_grad.reshape(branches, own, chans),
        reduce_grad,
        merge1_grad,
        merge2_grad,
        class_grad,
    )


def solution(mesh):
    return jax.shard_map(
        local,
        mesh=mesh,
        in_specs=(
            P("dp", None, None, None), P("dp", "section", None, None), P("dp", None, None), P("dp", None, None),
            P(None, None, "section"), P(None, "section"), P(None, "section"), P(None, "section"), P(None, "section", None),
            P(), P(), P(), P(), P("dp", "section", None, None),
        ),
        out_specs=(
            P("dp", "section", None, None), P("dp", None, None, "section"), P("dp", "section", None, None),
            P(None, None, "section"), P(None, "section"), P(None, "section"), P(None, "section"), P(None, "section", None),
            P(), P(), P(), P(),
        ),
        check_vma=False,
    )
```

```python
import jax
import jax.numpy as jnp
import numpy as np
from jax import lax
from jax.experimental import pallas as pl
from jax.experimental.pallas import tpu as pltpu
from jax.sharding import PartitionSpec as P

IMAGES = 2
bf16 = jnp.bfloat16
f32 = jnp.float32
HALO = 4
LANE = 128


def upsample_matrix(coarse_count):
    fine = np.arange(4 * coarse_count)
    coarse, phase = fine // 4, fine % 4
    near = np.where(phase < 2, 5 + 2 * phase, 11 - 2 * phase) / 8.0
    far = np.clip(np.where(phase < 2, coarse - 1, coarse + 1), 0, coarse_count - 1)
    matrix = np.zeros((4 * coarse_count, coarse_count), np.float32)
    np.add.at(matrix, (fine, coarse), near)
    np.add.at(matrix, (fine, far), 1.0 - near)
    return matrix


def split_rows(first, stop, target):
    count = stop - first
    pieces = -(-count // target)
    edges = [first + (count * k) // pieces for k in range(pieces + 1)]
    return [(edges[k], edges[k + 1] - edges[k]) for k in range(pieces)]


def silu_and_slope(v):
    s = 0.5 + 0.5 * jnp.tanh(0.5 * v)
    a = v * s
    return a, s * (1.0 + v - a)


def row_tables(cut, fine_total, section_index, own_rows, coarse_rows):
    window = own_rows + 2 * HALO
    slots = window + 1
    first = section_index * own_rows - HALO
    cut = cut[:, None] - first
    gap = jnp.where((cut >= 1) & (cut < window), cut, window)
    slot = jnp.arange(slots, dtype=jnp.int32)[None, :]
    src = slot - (slot > gap).astype(jnp.int32)
    row = src + first
    valid = (slot != gap) & (row >= 0) & (row < fine_total)
    own = valid & (src >= HALO) & (src < own_rows + HALO)
    coarse = row // 4
    phase = row % 4
    near_weight = jnp.where(phase < 2, 5 + 2 * phase, 11 - 2 * phase).astype(f32) / 8.0
    far = jnp.clip(jnp.where(phase < 2, coarse - 1, coarse + 1), 0, coarse_rows - 1)
    base = section_index * (own_rows // 4) - 2
    held = own_rows // 4 + 4
    near_at = jnp.clip(coarse - base, 0, held - 1)
    far_at = jnp.clip(far - base, 0, held - 1)
    validf = valid.astype(f32)
    ownf = own.astype(f32)
    own_at = jnp.where(own, src - HALO, own_rows)
    slot_of = slot + (slot >= gap).astype(jnp.int32)
    inside = ((slot + first >= 0) & (slot + first < fine_total)).astype(f32)
    inside = jnp.broadcast_to(inside, validf.shape)
    ints = jnp.stack(
        [jnp.clip(src, 0, window - 1), near_at, far_at, own_at, slot_of, jnp.broadcast_to(gap, src.shape)], axis=1
    )
    floats = jnp.stack(
        [
            validf,
            ownf,
            near_weight * validf,
            (1.0 - near_weight) * validf,
            near_weight * ownf,
            (1.0 - near_weight) * ownf,
            inside,
        ],
        axis=1,
    )
    batch = cut.shape[0]
    return ints.astype(jnp.int32).reshape(batch, -1), floats.reshape(batch, -1)


def column_sides(v):
    n = v.shape[0]
    col = lax.broadcasted_iota(jnp.int32, v.shape, 0)
    left = jnp.where(col == 0, 0.0, pltpu.roll(v, 1, 0))
    right = jnp.where(col == n - 1, 0.0, pltpu.roll(v, n - 1, 0))
    return left, right


def three_columns(v):
    left, right = column_sides(v)
    return jnp.concatenate([left.astype(bf16), v.astype(bf16), right.astype(bf16)], axis=1)


def decode_kernel(own_rows, cols, chans, red, parts, before, at, itab, ftab, low_top, low, low_end, tgt, colm, colt, rwt, m1, m2, clst, *refs):
    projs, refs = refs[:parts], refs[parts + before:]
    decode_body(at[0], own_rows, cols, chans, red, projs, itab, ftab, low_top, low, low_end, tgt, colm, colt, rwt, m1, m2, clst, *refs)


def decode_body(first, own_rows, cols, chans, red, projs, itab, ftab, low_top, low, low_end, tgt, colm, colt, rwt, m1, m2, clst,
                  up_h, red_h, fst_h, sec_h, g2_h, g1_h, rg_h, pg_o,
                  jc, fc, sl1, rs, tgg, lift, drop, a0, a1, b0, b1,
                w1, rw3, clsb, wb2, wb1u, wb1r, up_o, red_o, fst_o, sec_o, g2_o, g1_o, rg_o, sems):
    m = pl.program_id(0)
    window = own_rows + 2 * HALO
    slots = window + 1
    held = projs[0].shape[1]
    wide = 3 * chans
    redw = jc.shape[2] - wide
    keep = own_rows + 3
    gc2, gc1 = jc.at[:, :, 0:wide], fc
    held_rows = [(up_o, up_h), (red_o, red_h), (fst_o, fst_h), (sec_o, sec_h), (g2_o, g2_h), (g1_o, g1_h), (rg_o, rg_h)]

    def out_copy(k, at):
        here, there = held_rows[k]
        return pltpu.make_async_copy(here.at[0:there.shape[1]], there.at[first + at], sems.at[k])

    @pl.when(m > 0)
    def _():
        for k in range(6):
            out_copy(k, m - 1).wait()

    @pl.when(m == 0)
    def _():
        w1[:, wide + 3 * red:] = jnp.zeros((3, redw - 3 * red, chans), bf16)
        clsb[...] = jnp.zeros(clsb.shape, bf16)
        clsb[0:clst.shape[0]] = clst[...]
        spare = jnp.zeros((redw - 3 * red, chans), bf16)
        rw3[...] = jnp.concatenate([rwt[...]] * 3 + [spare], axis=0).T
        for r in range(3):
            for d in range(3):
                part = slice(d * chans, (d + 1) * chans)
                w1[r, part] = m1[3 * r + d, 0:chans]
                w1[r, wide + d * red:wide + (d + 1) * red] = m1[3 * r + d, chans:]
                tap = 3 * (2 - r) + 2 - d
                wb2[r, part] = m2[tap].T
                wb1u[r, part] = m1[tap, 0:chans].T
            tails = [m1[3 * (2 - r) + d, chans:] for d in range(3)]
            wb1r[r] = jnp.concatenate(tails + [spare], axis=0).T

    def w2(r):
        return m2[3 * r:3 * r + 3].reshape(wide, chans)

    def it(k, j):
        return itab[first + m, k * slots + j]

    def ft(k, j):
        return ftab[first + m, k * slots + j]

    accs = (a0, a1)
    bccs = (b0, b1)

    def staged(blocks, multiply, finish):
        for k, block in enumerate(blocks):
            multiply(*block, accs[k % 2], bccs[k % 2])
            if k:
                finish(*blocks[k - 1], accs[(k - 1) % 2], bccs[(k - 1) % 2])
        k = len(blocks) - 1
        finish(*blocks[k], accs[k % 2], bccs[k % 2])

    def rows_of(ref, lo, n):
        return ref[lo:lo + n].reshape(n * cols, ref.shape[2])

    def dot(a, b):
        return jnp.dot(a, b, preferred_element_type=f32)

    @pl.when(m == 0)
    def _():
        tgg[...] = jnp.zeros(tgg.shape, bf16)

    for i in range(2):
        tgg[it(4, 2 + i)] = low_top[0, HALO][:, i * LANE:(i + 1) * LANE]
        tgg[it(4, own_rows + HALO + i)] = low_end[0, HALO][:, i * LANE:(i + 1) * LANE]
    for i in range(own_rows):
        tgg[it(4, HALO + i)] = tgt[0, i]
    tgg[it(5, 0)] = jnp.zeros((cols, LANE), bf16)

    lane = lax.broadcasted_iota(jnp.int32, (cols, redw), 1)

    def reduce_mul(ref, lo, n, place, acc, _):
        acc[0:n * cols] = dot(ref[0, lo:lo + n].reshape(n * cols, ref.shape[3]), rw3[...])

    def reduce_fin(ref, lo, n, place, acc, _):
        for r in range(n):
            a, slope = silu_and_slope(acc[r * cols:(r + 1) * cols])
            a = a * ft(6, place + r)
            left, right = column_sides(a)
            a = jnp.where(lane < red, left, jnp.where(lane < 2 * red, a, right))
            jc[it(4, place + r), :, wide:] = a.astype(bf16)
            if HALO <= place + r < own_rows + HALO:
                rs[place + r - HALO] = slope.astype(bf16)

    staged(
        [(low_top, 0, HALO, 0)]
        + [(low, lo, n, lo + HALO) for lo, n in split_rows(0, own_rows, 8)]
        + [(low_end, 0, HALO, own_rows + HALO)],
        reduce_mul, reduce_fin,
    )
    jc[it(5, 0), :, wide:] = jnp.zeros((cols, redw), bf16)

    for k in range(held):
        v = sum(p[0, k].astype(f32) for p in projs).astype(bf16)
        lift[k] = dot(colm[...], v)
    for j in range(slots):
        v = (ft(2, j) * lift[it(1, j)] + ft(3, j) * lift[it(2, j)]).astype(bf16)
        for d in range(3):
            jc[j, :, d * chans:(d + 1) * chans] = v[d * cols:(d + 1) * cols]
        if 3 <= j < 3 + keep:
            up_o[j - 3] = v[cols:2 * cols]

    red_o[...] = jc[3:3 + keep, :, wide:]
    out_copy(0, m).start()
    out_copy(1, m).start()

    def first_mul(lo, n, acc, _):
        acc[0:n * cols] = (
            dot(rows_of(jc, lo - 1, n), w1[0]) + dot(rows_of(jc, lo, n), w1[1]) + dot(rows_of(jc, lo + 1, n), w1[2])
        )

    def first_fin(lo, n, acc, _):
        for r in range(n):
            a, slope = silu_and_slope(acc[r * cols:(r + 1) * cols])
            keep_row = ft(0, lo + r)
            a = a * keep_row
            fc[lo + r] = three_columns(a)
            if 3 <= lo + r < 3 + keep:
                fst_o[lo + r - 3] = a.astype(bf16)
            sl1[lo + r] = (slope * keep_row).astype(bf16)

    staged(split_rows(1, slots - 1, 8), first_mul, first_fin)
    out_copy(2, m).start()

    def second_mul(lo, n, acc, bcc):
        acc[0:n * cols] = (
            dot(rows_of(fc, lo - 1, n), w2(0)) + dot(rows_of(fc, lo, n), w2(1)) + dot(rows_of(fc, lo + 1, n), w2(2))
        )
        bcc[0:n * cols] = dot(rows_of(tgg, lo, n), clsb[...])

    def second_fin(lo, n, acc, bcc):
        for r in range(n):
            j = lo + r
            a, slope = silu_and_slope(acc[r * cols:(r + 1) * cols])
            sec_o[it(3, j)] = a.astype(bf16)
            g = bcc[r * cols:(r + 1) * cols] * slope * ft(0, j)
            gc2[j] = three_columns(g)
            if HALO <= j <= own_rows + HALO:
                g2_o[j - HALO] = (g * ft(1, j)).astype(bf16)

    staged(split_rows(2, slots - 2, 8), second_mul, second_fin)
    out_copy(3, m).start()
    out_copy(4, m).start()

    def back2_mul(lo, n, acc, _):
        acc[0:n * cols] = (
            dot(rows_of(gc2, lo - 1, n), wb2[0]) + dot(rows_of(gc2, lo, n), wb2[1]) + dot(rows_of(gc2, lo + 1, n), wb2[2])
        )

    def back2_fin(lo, n, acc, _):
        for r in range(n):
            j = lo + r
            g = acc[r * cols:(r + 1) * cols] * sl1[j].astype(f32)
            gc1[j] = three_columns(g)
            if HALO <= j <= own_rows + HALO:
                g1_o[j - HALO] = (g * ft(1, j)).astype(bf16)

    staged(split_rows(3, slots - 3, 8), back2_mul, back2_fin)
    out_copy(5, m).start()

    drop[...] = jnp.zeros(drop.shape, f32)

    @pl.when(m > 0)
    def _():
        out_copy(6, m - 1).wait()

    def back1_mul(lo, n, acc, bcc):
        acc[0:n * cols] = (
            dot(rows_of(gc1, lo - 1, n), wb1u[0]) + dot(rows_of(gc1, lo, n), wb1u[1]) + dot(rows_of(gc1, lo + 1, n), wb1u[2])
        )
        mid = slice(chans, 2 * chans)
        bcc[0:n * cols] = (
            dot(rows_of(gc1, lo - 1, n)[:, mid], wb1r[0]) + dot(rows_of(gc1, lo, n)[:, mid], wb1r[1])
            + dot(rows_of(gc1, lo + 1, n)[:, mid], wb1r[2])
        )

    def back1_fin(lo, n, acc, bcc):
        for r in range(n):
            j = lo + r
            up = acc[r * cols:(r + 1) * cols]
            near, far = it(1, j), it(2, j)
            drop[near] += ft(4, j) * up
            drop[far] += ft(5, j) * up
            t = bcc[r * cols:(r + 1) * cols]
            left, right = column_sides(t)
            t = jnp.where(lane < red, right, jnp.where(lane < 2 * red, t, left))
            rg_o[it(3, j)] = (t * rs[it(3, j)].astype(f32)).astype(bf16)

    staged(split_rows(HALO, slots - HALO, 8), back1_mul, back1_fin)
    out_copy(6, m).start()

    for k in range(held):
        pg_o[0, k] = dot(colt[...], drop[k].astype(bf16)).astype(bf16)

    @pl.when(m == pl.num_programs(0) - 1)
    def _():
        for k in range(7):
            out_copy(k, m).wait()


def whole(a):
    return pl.BlockSpec(a.shape, lambda *at: (0,) * a.ndim, pipeline_mode=pl.Buffered(1))


def per(shape):
    return pl.BlockSpec((1,) + shape, lambda m, *at: (m,) + (0,) * len(shape))


def per_from(shape):
    return pl.BlockSpec((1,) + shape, lambda m, at: (m + at[0],) + (0,) * len(shape))


def total(shape):
    return pl.BlockSpec(shape, lambda *at: (0,) * len(shape))


def params():
    return pltpu.CompilerParams(vmem_limit_bytes=63 * 2 ** 20)


def saved_shapes(own_rows, cols, chans, red):
    redw = -(-3 * red // LANE) * LANE
    return [(own_rows + 3, cols, chans), (own_rows + 3, cols, redw), (own_rows + 3, cols, chans), (own_rows, cols, chans),
            (own_rows + 1, cols, chans), (own_rows + 1, cols, chans), (own_rows, cols, redw)]


def blank(batch, shapes):
    return tuple(pl.pallas_call(
        lambda *refs: None,
        out_specs=[pl.BlockSpec(memory_space=pl.ANY)] * len(shapes),
        out_shape=[jax.ShapeDtypeStruct((batch,) + s, bf16) for s in shapes],
        name="blank",
    )())


def decode(first, batch, tables, low_top, low_input, low_end, projs, target, reduce_t, merge1_weight, merge2_weight, class_t, earlier):
    ints, floats = tables
    all_batch, own_rows, cols, low_ch = low_input.shape
    window = own_rows + 2 * HALO
    slots = window + 1
    chans = merge2_weight.shape[1]
    red = reduce_t.shape[0]
    held, coarse_cols = projs[0].shape[1], projs[0].shape[2]
    redw = -(-3 * red // LANE) * LANE
    wide = 3 * chans
    colm = upsample_matrix(coarse_cols)
    zero = np.zeros((1, coarse_cols), np.float32)
    colm3 = jnp.asarray(np.concatenate([zero, colm[:-1], colm, colm[1:], zero], axis=0), bf16)
    colt = jnp.asarray(colm.T, bf16)
    keep = own_rows + 3
    smem = pl.BlockSpec(memory_space=pltpu.SMEM)
    hbm = pl.BlockSpec(memory_space=pl.ANY)
    most = max(n for k in range(5) for _, n in split_rows(k, slots - k, 8))
    consts = (colm3, colt, reduce_t, merge1_weight, merge2_weight, class_t)
    shapes = saved_shapes(own_rows, cols, chans, red)
    stage = [(s[0] + (1 if k in (3, 6) else 0),) + s[1:] for k, s in enumerate(shapes)]
    back_shape = (held, coarse_cols, chans)
    saved = pl.pallas_call(
        lambda *refs: decode_kernel(own_rows, cols, chans, red, len(projs), len(earlier), *refs),
        grid_spec=pltpu.PrefetchScalarGridSpec(
            num_scalar_prefetch=1,
            grid=(batch,),
            in_specs=[smem, smem] + [per_from(a.shape[1:]) for a in (low_top, low_input, low_end, target)]
            + [whole(a) for a in consts] + [per(p.shape[1:]) for p in projs] + [hbm] * len(earlier),
            out_specs=[hbm] * len(shapes) + [per(back_shape)],
            scratch_shapes=[
                pltpu.VMEM((slots, cols, wide + redw), bf16), pltpu.VMEM((slots, cols, wide), bf16),
                pltpu.VMEM((slots, cols, chans), bf16), pltpu.VMEM((own_rows + 1, cols, redw), bf16),
                pltpu.VMEM((slots, cols, LANE), bf16),
                pltpu.VMEM((held, 3 * cols, chans), f32), pltpu.VMEM((held, cols, chans), f32),
                pltpu.VMEM((most * cols, chans), f32), pltpu.VMEM((most * cols, chans), f32),
                pltpu.VMEM((most * cols, chans), f32), pltpu.VMEM((most * cols, chans), f32),
                pltpu.VMEM((3, wide + redw, chans), bf16), pltpu.VMEM((low_ch, redw), bf16), pltpu.VMEM((LANE, chans), bf16),
                pltpu.VMEM((3, wide, chans), bf16), pltpu.VMEM((3, wide, chans), bf16), pltpu.VMEM((3, chans, redw), bf16),
            ] + [pltpu.VMEM(s, bf16) for s in stage] + [pltpu.SemaphoreType.DMA((7,))],
        ),
        out_shape=[jax.ShapeDtypeStruct((all_batch,) + s, bf16) for s in shapes] + [jax.ShapeDtypeStruct((batch,) + back_shape, bf16)],
        input_output_aliases={7 + len(consts) + len(projs) + k: k for k in range(len(earlier))},
        compiler_params=params(),
        name="decode",
    )(jnp.full((1,), first, jnp.int32), ints, floats, low_top, low_input, low_end, target, *consts, *projs, *earlier)
    return saved[7], tuple(saved[:7])


def grads_kernel(own_rows, cols, chans, red, before, up, red3, fst, sec, g2, g1, rg, low, tgt, clst, rwt, *refs):
    earlier = refs[:before]
    packed, lowgrad, logits, o1, o2, oc, orr, upc, fcc = refs[before:]
    m = pl.program_id(0)
    keep = own_rows + 3
    wide = 3 * chans
    span = own_rows + 1
    classes = clst.shape[0]

    @pl.when(m == 0)
    def _():
        o1[...] = jnp.zeros(o1.shape, f32)
        o2[...] = jnp.zeros(o2.shape, f32)
        oc[...] = jnp.zeros(oc.shape, f32)
        orr[...] = jnp.zeros(orr.shape, f32)

    def tdot(a, b):
        return lax.dot_general(a, b, (((0,), (0,)), ((), ())), preferred_element_type=f32)

    for j in range(keep):
        upc[j] = three_columns(up[0, j].astype(f32))
    for j in range(keep):
        fcc[j] = three_columns(fst[0, j].astype(f32))

    def flat(v):
        return v.reshape(v.shape[0] * cols, v.shape[2])

    gg1 = flat(g1[0])
    for dy in range(3):
        o1[dy, 0:wide] += tdot(flat(upc[dy:dy + span]), gg1)
        o1[dy, wide:] += tdot(flat(red3[0, dy:dy + span]), gg1)
    gg2 = flat(g2[0])
    for dy in range(3):
        o2[dy] += tdot(flat(fcc[dy:dy + span]), gg2)
    oc[...] += tdot(flat(sec[0]), flat(tgt[0]))
    orr[...] += tdot(flat(low[0]), flat(rg[0]))
    spare = jnp.zeros((rg.shape[3] - 3 * red, chans), bf16)
    rb3 = jnp.concatenate([rwt[...]] * 3 + [spare], axis=0)
    for r in range(own_rows):
        lowgrad[0, r] = jnp.dot(rg[0, r], rb3, preferred_element_type=f32)
        lt = lax.dot_general(clst[...], sec[0, r], (((1,), (1,)), ((), ())), preferred_element_type=f32)
        logits[0, :, r] = lt

    @pl.when(m == pl.num_programs(0) - 1)
    def _():
        rows = chans + red
        for dy in range(3):
            for d in range(3):
                at = (3 * dy + d) * rows
                packed[at:at + chans] = o1[dy, d * chans:(d + 1) * chans].astype(bf16)
                packed[at + chans:at + rows] = o1[dy, wide + d * red:wide + (d + 1) * red].astype(bf16)
            packed[9 * rows + dy * wide:9 * rows + (dy + 1) * wide] = o2[dy].astype(bf16)
        at = 9 * rows + 3 * wide
        packed[at:] = jnp.zeros((packed.shape[0] - at, chans), bf16)
        t = orr[...].T
        packed[at:at + red] = (t[0:red] + t[red:2 * red] + t[2 * red:3 * red]).astype(bf16)
        packed[at + red:at + red + 32] = oc[...].T[0:32].astype(bf16)
        if before:
            packed[...] = (packed[...].astype(f32) + earlier[0][...].astype(f32)).astype(bf16)


def packed_rows(chans, red):
    return 9 * (chans + red) + 9 * chans + red + 32


def decode_grads(first, saved, low_input, target, reduce_t, class_t, earlier):
    up, red3, fst, sec, g2, g1, rg = saved
    batch = up.shape[0]
    all_batch, own_rows, cols, low_ch = low_input.shape
    chans = up.shape[3]
    redw = red3.shape[3]
    red = reduce_t.shape[0]
    classes = class_t.shape[0]
    wide = 3 * chans
    keep = own_rows + 3
    rows = packed_rows(chans, red)
    hbm = pl.BlockSpec(memory_space=pl.ANY)
    tots = [(3, wide + redw, chans), (3, wide, chans), (chans, LANE), (low_ch, redw)]
    pers = [(own_rows, cols, low_ch), (classes, own_rows, cols)]
    packed, lowgrad, logits = pl.pallas_call(
        lambda *refs: grads_kernel(own_rows, cols, chans, red, 3 if earlier else 0, *refs),
        grid=(batch,),
        in_specs=[per((keep, cols, chans)), per((keep, cols, redw)), per((keep, cols, chans)), per((own_rows, cols, chans)),
                  per((own_rows + 1, cols, chans)), per((own_rows + 1, cols, chans)), per((own_rows, cols, redw)),
                  per((own_rows, cols, low_ch)), per(target.shape[1:]), whole(class_t), whole(reduce_t)]
        + ([whole(earlier[0]), hbm, hbm] if earlier else []),
        out_specs=[total((rows, chans))] + [per(s) for s in pers],
        out_shape=[jax.ShapeDtypeStruct((rows, chans), bf16)] + [jax.ShapeDtypeStruct((all_batch,) + s, f32) for s in pers],
        input_output_aliases={12: 1, 13: 2} if earlier else {},
        scratch_shapes=[pltpu.VMEM(s, f32) for s in tots]
        + [pltpu.VMEM((keep, cols, wide), bf16), pltpu.VMEM((keep, cols, wide), bf16)],
        compiler_params=params(),
        name="decode_grads",
        cost_estimate=pl.CostEstimate(flops=1, bytes_accessed=1, transcendentals=1),
    )(up, red3, fst, sec, g2, g1, rg, low_input, target, class_t, reduce_t, *(earlier or ()))
    return packed, lowgrad, logits


def unpack_decoder(bit, mine, other, chans, red, classes):
    rows = chans + red
    half = mine.shape[0]
    at = 9 * rows + 9 * chans
    shapes = [(9, rows, chans), (9, chans, chans), (red, chans), (classes, chans)]

    def kernel(bit, a, b, m1, m2, rw, cw, v):
        v[pl.ds(pl.multiple_of(bit[0] * half, 16), half)] = a[...]
        v[pl.ds(pl.multiple_of((1 - bit[0]) * half, 16), half)] = b[...]
        for t in range(9):
            m1[t] = v[t * rows:(t + 1) * rows].astype(f32)
            m2[t] = v[9 * rows + t * chans:9 * rows + (t + 1) * chans].astype(f32)
        rw[...] = v[at:at + red].astype(f32)
        cw[...] = v[at + red:at + red + 32].astype(f32)[0:classes]

    m1, m2, rw, cw = pl.pallas_call(
        kernel,
        grid=(1,),
        in_specs=[pl.BlockSpec(memory_space=pltpu.SMEM), whole(mine), whole(other)],
        out_specs=[total(s) for s in shapes],
        out_shape=[jax.ShapeDtypeStruct(s, f32) for s in shapes],
        scratch_shapes=[pltpu.VMEM((2 * half, chans), bf16)],
        compiler_params=params(),
        name="unpack_decoder",
    )(bit, mine, other)
    return m1, m2, rw.T, cw.T


atrous_rates = (6, 12, 18)
epsilon = 1e-05


def tap_list():
    listed = [(0, 0, 0)]
    for branch_index, rate_value in enumerate(atrous_rates):
        for step_rows in (-1, 0, 1):
            for step_cols in (-1, 0, 1):
                listed.append((rate_value * step_rows, rate_value * step_cols, branch_index + 1))
    return listed


def pixel_places(batch, height, width):
    pixel = np.arange(height * width)
    places = np.stack([np.tile(pixel // width, batch), np.tile(pixel % width, batch), np.repeat(np.arange(batch), height * width)])
    return jnp.asarray(np.pad(places, ((0, 5), (0, 0))), jnp.int32)


class Pixels:
    def __init__(self, places, cuts, batch, height, width):
        self.row, self.col, self.canvas = places[0:1], places[1:2], places[2:3]
        self.height, self.width = height, width
        cut = jnp.full(self.row.shape, cuts[0], jnp.int32)
        for m in range(1, batch):
            cut = jnp.where(self.canvas == m, cuts[m], cut)
        self.cut = cut
        self.band = self.row >= cut

    def valid(self, dr, dc):
        row, col = self.row + dr, self.col + dc
        inside = (row >= 0) & (row < self.height) & (col >= 0) & (col < self.width)
        same = jnp.where(row >= self.cut, 1, 0) == jnp.where(self.band, 1, 0)
        return jnp.where(inside & same, 1.0, 0.0)

    def image(self):
        return IMAGES * self.canvas + jnp.where(self.band, 1, 0)


def image_counts(cuts, batch, height, width):
    index = lax.broadcasted_iota(jnp.int32, (IMAGES * batch, 1), 0)
    out = jnp.zeros((IMAGES * batch, 1), f32)
    for m in range(batch):
        first = cuts[m] * width
        out = jnp.where(index == IMAGES * m, first.astype(f32), out)
        out = jnp.where(index == IMAGES * m + 1, (height * width - first).astype(f32), out)
    return jnp.maximum(out, 1.0)


def branch_kernel(taps, batch, height, width, cuts, x, w, places, pw, br_o, mom_o, pooled_o, y, pool, mom):
    i = pl.program_id(0)
    last = pl.num_programs(0) - 1
    block = x.shape[0]
    total = y.shape[1]
    pixels = total // batch
    own = pw.shape[0]
    at = pl.multiple_of(i * block, block)

    @pl.when(i == 0)
    def _():
        pool[...] = jnp.zeros(pool.shape, f32)
        mom[...] = jnp.zeros(mom.shape, f32)

    def nt(a, b):
        return lax.dot_general(a, b, (((1,), (1,)), ((), ())), preferred_element_type=f32)

    canvas, row = places[2:3, pl.ds(at, block)], places[0:1, pl.ds(at, block)]
    cut = jnp.full(row.shape, cuts[0], jnp.int32)
    for m in range(1, batch):
        cut = jnp.where(canvas == m, cuts[m], cut)
    image = IMAGES * canvas + jnp.where(row >= cut, 1, 0)
    index = lax.broadcasted_iota(jnp.int32, (IMAGES * batch, block), 0)
    member = jnp.where(image == index, 1.0, 0.0).astype(bf16)
    pool[...] += jnp.dot(member, x[...], preferred_element_type=f32)

    @pl.when(i < last)
    def _():
        y[:, pl.ds(at, block)] = nt(w[...], x[...])

    def keep(m, b, v):
        part = slice(b * own, (b + 1) * own)
        br_o[m, part] = v
        mom[part, m:m + 1] = jnp.sum(v, axis=1, keepdims=True)
        mom[part, batch + m:batch + m + 1] = jnp.sum(v * v, axis=1, keepdims=True)

    @pl.when(i == last)
    def _():
        px = Pixels(places, cuts, batch, height, width)
        spans = []
        for b in range(4):
            mine = [t for t, tap in enumerate(taps) if tap[2] == b]
            spans.append((mine[0], mine[-1] + 1))

        def multiply(b):
            lo, hi = spans[b][0] * own, spans[b][1] * own
            y[lo:hi, total - block:] = nt(w[lo:hi], x[...])

        def finish(b):
            acc = None
            for t in range(*spans[b]):
                dr, dc, _ = taps[t]
                v = y[t * own:(t + 1) * own]
                shift = dr * width + dc
                if shift:
                    v = pltpu.roll(v, (-shift) % total, 1) * px.valid(dr, dc)
                acc = v if acc is None else acc + v
            for m in range(batch):
                keep(m, b, acc[:, m * pixels:(m + 1) * pixels])

        multiply(0)
        multiply(1)
        multiply(2)
        finish(0)
        finish(1)
        multiply(3)
        finish(2)
        finish(3)
        pooled = (pool[...] / image_counts(cuts, batch, height, width)).astype(bf16)
        pooled_o[...] = pooled
        po = nt(pw[...], pooled)
        for m in range(batch):
            band = px.band[:, m * pixels:(m + 1) * pixels]
            keep(m, 4, jnp.where(band, po[:, IMAGES * m + 1:IMAGES * m + 2], po[:, IMAGES * m:IMAGES * m + 1]))
        mom_o[...] = mom[...].T[0:mom_o.shape[0]]


def aspp_forward(cuts, x, wt, pwt, batch, height, width):
    all_pixels, in_chans = x.shape
    pixels = height * width
    own = pwt.shape[0]
    taps = tap_list()
    block = all_pixels // 3 if all_pixels % 3 == 0 and (all_pixels // 3) % LANE == 0 else all_pixels
    places = pixel_places(batch, height, width)
    outs = [((batch, 5 * own, pixels), f32), ((2 * batch, 5 * own), f32), ((IMAGES * batch, in_chans), bf16)]
    return pl.pallas_call(
        lambda *refs: branch_kernel(taps, batch, height, width, *refs),
        grid=(all_pixels // block,),
        in_specs=[pl.BlockSpec(memory_space=pltpu.SMEM), pl.BlockSpec((block, in_chans), lambda i: (i, 0)),
                  whole(wt), whole(places), whole(pwt)],
        out_specs=[total(s) for s, _ in outs],
        out_shape=[jax.ShapeDtypeStruct(s, d) for s, d in outs],
        scratch_shapes=[pltpu.VMEM((len(taps) * own, all_pixels), f32), pltpu.VMEM((IMAGES * batch, in_chans), f32),
                        pltpu.VMEM((5 * own, LANE), f32)],
        compiler_params=params(),
        name="aspp_forward",
    )(cuts, x, wt, places, pwt)


def column(t, m):
    if isinstance(m, int):
        return t[:, m:m + 1]
    lane = lax.broadcasted_iota(jnp.int32, t.shape, 1)
    return jnp.sum(jnp.where(lane == m, t, 0.0), axis=1, keepdims=True)


def norm_columns(stats, scale, m, batch, count):
    t = stats[...].T
    mean = column(t, m) / count
    inv_std = lax.rsqrt(column(t, batch + m) / count - mean * mean + epsilon)
    s = scale[...].T
    half = s.shape[1] // 2
    gain = jnp.concatenate([s[:, k:k + 1] for k in range(half)], axis=0)
    shift = jnp.concatenate([s[:, half + k:half + k + 1] for k in range(half)], axis=0)
    return mean, inv_std, gain, shift


def project_kernel(group, count, coarse_rows, at_ref, offsets, br, stats, scale, proj, *refs):
    outs, rows = refs[:-1], refs[-1]
    batch = stats.shape[0] // 2
    height, width, chans = rows.shape[0] - 4, rows.shape[1], rows.shape[2]
    held = coarse_rows + 4
    rows[0:2] = jnp.zeros((2, width, chans), f32)
    rows[height + 2:] = jnp.zeros((2, width, chans), f32)
    for at in range(group):
        mean, inv_std, gain, shift = norm_columns(stats, scale, at_ref[0] + at, batch, count)
        active, _ = silu_and_slope((br[at] - mean) * inv_std * gain + shift)
        partial = lax.dot_general(active.astype(bf16), proj[...], (((0,), (0,)), ((), ())), preferred_element_type=f32)
        rows[2:height + 2] = partial.reshape(height, width, chans)
        for k, o in enumerate(outs):
            o[at] = rows[pl.ds(offsets[k], held)].astype(bf16)


def project(first, group, offsets, br, stats, scale, proj, count, coarse_rows, parts, height, width):
    chans = proj.shape[1]
    shape = (group, coarse_rows + 4, width, chans)
    pixels = br.shape[2]
    return pl.pallas_call(
        lambda *refs: project_kernel(group, count, coarse_rows, *refs),
        grid_spec=pltpu.PrefetchScalarGridSpec(
            num_scalar_prefetch=1,
            grid=(1,),
            in_specs=[pl.BlockSpec(memory_space=pltpu.SMEM), pl.BlockSpec((pl.Element(group), pl.Element(br.shape[1]), pl.Element(pixels)), lambda i, at: (at[0], 0, 0)),
                      whole(stats), whole(scale), whole(proj)],
            out_specs=[total(shape)] * parts,
            scratch_shapes=[pltpu.VMEM((height + 4, width, chans), f32)],
        ),
        out_shape=[jax.ShapeDtypeStruct(shape, bf16)] * parts,
        compiler_params=params(),
        name="project",
    )(jnp.full((1,), first, jnp.int32), offsets, br, stats, scale, proj)


def norm_back_kernel(count, parts, at_ref, offsets, br, stats, scale, proj, earlier, sums_before, *refs):
    pieces = refs[:parts]
    grad_o, sums_o, projgrad_o, rows, sums = refs[parts:]
    height, width, chans = rows.shape[0] - 4, rows.shape[1], rows.shape[2]
    group, held = pieces[0].shape[0], pieces[0].shape[1]
    batch = stats.shape[0] // 2
    sums[...] = jnp.zeros(sums.shape, f32)
    projgrad = earlier[...]
    for at in range(group):
        m = at_ref[0] + at
        rows[...] = jnp.zeros(rows.shape, f32)
        for k, piece in enumerate(pieces):
            rows[pl.ds(offsets[k], held)] += piece[at].astype(f32)
        grad = rows[2:height + 2].reshape(height * width, chans).astype(bf16)
        mean, inv_std, gain, shift = norm_columns(stats, scale, m, batch, count)
        scaled = (br[at] - mean) * inv_std
        active, slope = silu_and_slope(scaled * gain + shift)
        back = lax.dot_general(proj[...], grad, (((1,), (1,)), ((), ())), preferred_element_type=f32) * slope
        grad_o[at] = back
        lane = lax.broadcasted_iota(jnp.int32, sums.shape, 1)
        products = jnp.sum(back * scaled, axis=1, keepdims=True)
        sums[...] += jnp.where(lane == m, products, jnp.where(lane == batch + m, jnp.sum(back, axis=1, keepdims=True), 0.0))
        projgrad = projgrad + jnp.dot(active.astype(bf16), grad, preferred_element_type=f32)
    projgrad_o[...] = projgrad
    sums_o[...] = sums_before[...] + sums[...].T[0:sums_o.shape[0]]


def norm_back(first, offsets, br, stats, scale, proj, earlier, sums_before, pieces, count, height, width):
    batch, chans5, pixels = br.shape
    group = pieces[0].shape[0]
    outs = [((group, chans5, pixels), f32), (stats.shape, f32), (proj.shape, f32)]
    return pl.pallas_call(
        lambda *refs: norm_back_kernel(count, len(pieces), *refs),
        grid_spec=pltpu.PrefetchScalarGridSpec(
            num_scalar_prefetch=1,
            grid=(1,),
            in_specs=[pl.BlockSpec(memory_space=pltpu.SMEM), pl.BlockSpec((pl.Element(group), pl.Element(chans5), pl.Element(pixels)), lambda i, at: (at[0], 0, 0)),
                      whole(stats), whole(scale), whole(proj), whole(earlier), whole(sums_before)] + [whole(p) for p in pieces],
            out_specs=[total(s) for s, _ in outs],
            scratch_shapes=[pltpu.VMEM((height + 4, width, proj.shape[1]), f32), pltpu.VMEM((chans5, LANE), f32)],
        ),
        out_shape=[jax.ShapeDtypeStruct(s, d) for s, d in outs],
        compiler_params=params(),
        name="norm_back",
    )(jnp.full((1,), first, jnp.int32), offsets, br, stats, scale, proj, earlier, sums_before, *pieces)


def weight_grad_kernel(taps, groups, height, width, count, cuts, stats, scale, sums, places, projgrad, x_hbm, br_hbm, *refs):
    backs = refs[:groups]
    wg_hbm, tg_hbm, pg_o, both, x, tg, wg, br, back, sems, in_sems = refs[groups:]
    batch = br.shape[0]
    owner = [(g, k) for g, part in enumerate(backs) for k in range(part.shape[0])]

    def in_copies(m):
        g, k = owner[m]
        return (pltpu.make_async_copy(br_hbm.at[m], br.at[m], in_sems.at[m]),
                pltpu.make_async_copy(backs[g].at[k], back.at[m], in_sems.at[batch + m]))

    for m in range(batch):
        for copy in in_copies(m):
            copy.start()
    own = pg_o.shape[0]
    pixels = br.shape[2]
    rows, all_pixels = tg.shape
    in_chans = x.shape[1]
    filled = (len(taps) + 1) * own
    x_copy = pltpu.make_async_copy(x_hbm, x, sems.at[0])
    x_copy.start()
    px = Pixels(places, cuts, batch, height, width)
    pool_grad = jnp.zeros((own, LANE), f32)
    lane = lax.broadcasted_iota(jnp.int32, (own, LANE), 1)
    t = sums[...].T
    for m in range(batch):
        for copy in in_copies(m):
            copy.wait()
        mean, inv_std, gain, _ = norm_columns(stats, scale, m, batch, count)
        gain_sum, shift_sum = t[:, m:m + 1], t[:, batch + m:batch + m + 1]
        scaled = (br[m] - mean) * inv_std
        grad = inv_std * gain * (back[m] - (shift_sum + scaled * gain_sum) / count)
        both[0:4 * own, m * pixels:(m + 1) * pixels] = grad[0:4 * own]
        pool = grad[4 * own:]
        band = px.band[:, m * pixels:(m + 1) * pixels]
        upper = jnp.sum(jnp.where(band, 0.0, pool), axis=1, keepdims=True).astype(bf16).astype(f32)
        lower = jnp.sum(jnp.where(band, pool, 0.0), axis=1, keepdims=True).astype(bf16).astype(f32)
        pool_grad = jnp.where(lane == IMAGES * m, upper, pool_grad)
        pool_grad = jnp.where(lane == IMAGES * m + 1, lower, pool_grad)
        many = (cuts[m] * width).astype(f32)
        spread = jnp.where(band, lower / jnp.maximum(height * width - many, 1.0), upper / jnp.maximum(many, 1.0))
        both[4 * own:, m * pixels:(m + 1) * pixels] = spread
    pg_o[...] = pool_grad[:, 0:pg_o.shape[1]].astype(bf16)

    for k, (dr, dc, b) in enumerate(taps):
        v = both[b * own:(b + 1) * own]
        shift = dr * width + dc
        if shift:
            v = pltpu.roll(v * px.valid(dr, dc), shift % all_pixels, 1)
        tg[k * own:(k + 1) * own] = v.astype(bf16)
    tg[filled - own:] = both[4 * own:].astype(bf16)
    tg_copy = pltpu.make_async_copy(tg, tg_hbm, sems.at[1])
    tg_copy.start()
    x_copy.wait()
    chans = projgrad.shape[1]
    some = projgrad.shape[0] * chans // in_chans
    step = 512 if in_chans % 512 == 0 else in_chans
    wg[filled:] = jnp.zeros((wg.shape[0] - filled, in_chans), bf16)
    for k in range(in_chans // chans):
        wg[filled:filled + some, k * chans:(k + 1) * chans] = projgrad[k * some:(k + 1) * some].astype(bf16)

    def out_copy(n):
        part = pl.ds(pl.multiple_of(n * step, step), step)
        return pltpu.make_async_copy(wg.at[:, part], wg_hbm.at[:, part], sems.at[2 + n])

    def multiply(n, _):
        part = pl.ds(pl.multiple_of(n * step, step), step)
        wg[0:filled, part] = jnp.dot(tg[...], x[:, part], preferred_element_type=f32).astype(bf16)
        out_copy(n).start()
        return 0

    lax.fori_loop(0, in_chans // step, multiply, 0)
    tg_copy.wait()
    for n in range(in_chans // step):
        out_copy(n).wait()


def aspp_weight_grads(rows, cuts, x, br, stats, scale, sums, projgrad, backs, count, height, width):
    all_pixels, in_chans = x.shape
    batch, chans5, pixels = br.shape
    own = chans5 // 5
    places = pixel_places(batch, height, width)
    groups = len(backs)
    hbm = pl.BlockSpec(memory_space=pl.ANY)
    outs = [(rows, in_chans), ((len(tap_list()) + 1) * own, all_pixels), (own, IMAGES * batch)]
    return pl.pallas_call(
        lambda *refs: weight_grad_kernel(tap_list(), groups, height, width, count, *refs),
        grid=(1,),
        in_specs=[pl.BlockSpec(memory_space=pltpu.SMEM)] + [whole(v) for v in (stats, scale, sums, places, projgrad)]
        + [hbm] * (2 + len(backs)),
        out_specs=[hbm, hbm, total(outs[2])],
        out_shape=[jax.ShapeDtypeStruct(s, bf16) for s in outs],
        scratch_shapes=[pltpu.VMEM((chans5, all_pixels), f32), pltpu.VMEM((all_pixels, in_chans), bf16),
                        pltpu.VMEM(outs[1], bf16), pltpu.VMEM(outs[0], bf16),
                        pltpu.VMEM(br.shape, f32), pltpu.VMEM(br.shape, f32),
                        pltpu.SemaphoreType.DMA((2 + in_chans // 512 + 1,)), pltpu.SemaphoreType.DMA((2 * batch,))],
        compiler_params=params(),
        name="aspp_weight_grads",
    )(cuts, stats, scale, sums, places, projgrad, x, br, *backs)


def unpack_weights(summed, wide, own, proj_shape):
    rows, in_chans = summed.shape
    block = 512 if in_chans % 512 == 0 else in_chans
    chans = proj_shape[1]
    pieces = block // chans
    some = proj_shape[0] * chans // in_chans

    def kernel(v, wide_o, pool_o, proj_o):
        wide_o[...] = v[0:wide].astype(f32)
        pool_o[...] = v[wide:wide + own].astype(f32)
        tail = v[wide + own:].astype(f32)
        for k in range(pieces):
            proj_o[k * some:(k + 1) * some] = tail[0:some, k * chans:(k + 1) * chans]

    def lanes(a):
        return pl.BlockSpec((a, block), lambda j: (0, j))

    return pl.pallas_call(
        kernel,
        grid=(in_chans // block,),
        in_specs=[lanes(rows)],
        out_specs=[lanes(wide), lanes(own), pl.BlockSpec((some * pieces, chans), lambda j: (j, 0))],
        out_shape=[jax.ShapeDtypeStruct(s, f32) for s in ((wide, in_chans), (own, in_chans), proj_shape)],
        compiler_params=params(),
        name="unpack_weights",
    )(summed)


def input_grad_kernel(batch, span, height, width, at, cuts, tg, w, pg, pw, band, o):
    i = pl.program_id(0)
    pixels = height * width
    v = lax.dot_general(tg[...], w[...], (((0,), (0,)), ((), ())), preferred_element_type=f32)
    image = lax.dot_general(pg[...], pw[...], (((0,), (0,)), ((), ())), preferred_element_type=f32)
    image = image / image_counts(cuts, batch, height, width)
    index = lax.broadcasted_iota(jnp.int32, (IMAGES * batch, 1), 0)
    row = band[...]
    for k in range(span):
        m = i * span + k
        first = jnp.sum(jnp.where(index == IMAGES * m, image, 0.0), axis=0, keepdims=True)
        second = jnp.sum(jnp.where(index == IMAGES * m + 1, image, 0.0), axis=0, keepdims=True)
        part = slice(k * pixels, (k + 1) * pixels)
        o[part] = (v[part] + jnp.where(row >= cuts[m], second, first)).astype(bf16)


def aspp_input_grad(place, cuts, tg, wt, pool_grad, pwt, parts, height, width):
    rows, in_chans = wt.shape
    all_pixels = tg.shape[1]
    own = pwt.shape[0]
    pixels = height * width
    batch = all_pixels // pixels
    block = in_chans // parts
    span = 2 if (2 * pixels) % LANE == 0 and batch % 2 == 0 else batch
    row_column = jnp.asarray(np.arange(pixels)[:, None] // width, jnp.int32)
    return pl.pallas_call(
        lambda *refs: input_grad_kernel(batch, span, height, width, *refs),
        grid_spec=pltpu.PrefetchScalarGridSpec(
            num_scalar_prefetch=2,
            grid=(batch // span,),
            in_specs=[
                pl.BlockSpec((rows, span * pixels), lambda i, at, cuts: (0, i)),
                pl.BlockSpec((rows, block), lambda i, at, cuts: (0, at[0])),
                whole(pool_grad),
                pl.BlockSpec((own, block), lambda i, at, cuts: (0, at[0])),
                whole(row_column),
            ],
            out_specs=pl.BlockSpec((span * pixels, block), lambda i, at, cuts: (i, 0)),
        ),
        out_shape=jax.ShapeDtypeStruct((all_pixels, block), bf16),
        compiler_params=params(),
        name="aspp_input_grad",
        cost_estimate=pl.CostEstimate(flops=1, bytes_accessed=1, transcendentals=1),
    )(place, cuts, tg, wt, pool_grad, pwt, row_column)


def doubled_sum(value, axis):
    size = lax.axis_size(axis)
    step = 1
    while step < size:
        value = value + lax.ppermute(value, axis, [(i, i ^ step) for i in range(size)])
        step *= 2
    return value


def exchanged(pieces, axis):
    size = lax.axis_size(axis)
    return [pieces[0]] + [lax.ppermute(pieces[k], axis, [(i, i ^ k) for i in range(size)]) for k in range(1, size)]


def added(a, b):
    return (a.astype(f32) + b.astype(f32)).astype(bf16)


def scatter_sum(value, axis, unit):
    size = lax.axis_size(axis)
    count = size // unit
    me = lax.axis_index(axis)
    rows = value.shape[0] // count
    out = None
    for k in range(count):
        piece = lax.dynamic_slice_in_dim(value, ((me // unit) ^ k) * rows, rows, 0)
        if k:
            piece = lax.ppermute(piece, axis, [(i, i ^ (k * unit)) for i in range(size)])
        out = piece.astype(f32) if out is None else out + piece.astype(f32)
    return out.astype(bf16)


def gather(value, axis, unit, beside=()):
    size = lax.axis_size(axis)
    count = size // unit
    me = lax.axis_index(axis)
    got = [value] + [lax.ppermute(value, axis, [(i, i ^ (k * unit)) for i in range(size)]) for k in range(1, count)]
    rows = value.shape[0]
    got, beside = lax.optimization_barrier((got, beside))
    out = jnp.zeros((count * rows,) + value.shape[1:], value.dtype)
    for k, piece in enumerate(got):
        out = lax.dynamic_update_slice_in_dim(out, piece, ((me // unit) ^ k) * rows, 0)
    return out, beside


def tied(value, *others):
    return lax.optimization_barrier((value,) + others)[0]


def local(aspp_input, low_input, aspp_ids, low_ids, aspp_weight, pool_weight, bn_gain, bn_shift, projection_matrix,
          reduce_weight, merge1_weight, merge2_weight, class_weight, logit_grad):
    section = lax.axis_index("section")
    sections = lax.axis_size("section")
    batch, height, width, in_chans = aspp_input.shape
    taps, own = aspp_weight.shape[1], aspp_weight.shape[2]
    branches = bn_gain.shape[0]
    chans = projection_matrix.shape[2]
    red = reduce_weight.shape[1]
    classes = class_weight.shape[1]
    fine_rows, fine_cols = low_input.shape[1], low_input.shape[2]
    pixels = height * width
    count = pixels * lax.axis_size("dp")
    coarse_rows = fine_rows // 4
    groups = [(0, batch - 1), (batch - 1, 1)]

    x = aspp_input.reshape(batch * pixels, in_chans)
    wt = jnp.transpose(aspp_weight, (1, 2, 0)).reshape(taps * own, in_chans)
    pwt = pool_weight.T
    proj = projection_matrix.reshape(branches * own, chans)
    cuts = jnp.sum((aspp_ids[:, :, 0] == 0).astype(jnp.int32), axis=1)
    br, moments, pooled = aspp_forward(cuts, x, wt, pwt, batch, height, width)

    down = [(i, i + 1) for i in range(sections - 1)]
    up = [(i + 1, i) for i in range(sections - 1)]
    target = jnp.pad(logit_grad, ((0, 0), (0, 0), (0, 0), (0, LANE - classes)))

    def rim(low_rows, target_rows):
        paired = jnp.concatenate([target_rows[:, 0:1], target_rows[:, 1:2]], axis=3)
        return jnp.concatenate([low_rows, paired], axis=1)

    top = lax.ppermute(rim(low_input[:, -HALO:], target[:, -2:]), "section", down)
    end = lax.ppermute(rim(low_input[:, :HALO], target[:, :2]), "section", up)
    distance = jnp.arange(sections, dtype=jnp.int32)
    offsets = (section ^ distance) * coarse_rows

    stats = doubled_sum(moments, "dp")
    tables = row_tables(4 * cuts, low_ids.shape[1], section, fine_rows, height)
    scale = jnp.concatenate([bn_gain, bn_shift], axis=0)
    saved = blank(batch, saved_shapes(fine_rows, fine_cols, chans, red))
    parts = []
    for first, size in groups:
        at = tied(offsets, target, *tables, saved[0]) if parts else offsets
        parts.append(project(first, size, at, br, stats, scale, proj, count, coarse_rows, sections, height, width))
    projs = [exchanged(p, "section") for p in parts]
    projs[0][0] = tied(projs[0][0], *[p[0] for p in parts[1:]])
    pieces = []
    for g, (first, size) in enumerate(groups):
        pgrad, saved = decode(first, size, tables, top, low_input, end, projs[g], target, reduce_weight.T,
                              merge1_weight, merge2_weight, class_weight.T, saved)
        if g + 1 < len(groups):
            pgrad, *projs[g + 1] = lax.optimization_barrier((pgrad, *projs[g + 1]))
        pieces.append(exchanged([pgrad] * sections, "section"))
    backs = []
    projgrad, sums = jnp.zeros(proj.shape, f32), jnp.zeros(stats.shape, f32)
    for (first, size), piece in zip(groups, pieces):
        back, sums, projgrad = norm_back(first, offsets, br, stats, scale, proj, projgrad, sums, piece, count, height, width)
        backs.append(back)
    sums = doubled_sum(sums, "dp")
    filled = (taps + 1) * own
    rows = -(-(filled + projgrad.size // in_chans) // 32) * 32
    grads, tg, pool_grad = aspp_weight_grads(rows, cuts, x, br, stats, scale, sums, projgrad, backs, count, height, width)

    order = list(reversed(range(sections)))
    received = {}

    def input_of(k, tg):
        place = (section ^ k).reshape(1).astype(jnp.int32)
        return aspp_input_grad(place, cuts, tg, wt, pool_grad, pwt, sections, height, width)

    def sent(piece, k):
        return lax.ppermute(piece, "section", [(i, i ^ k) for i in range(sections)]) if k else piece

    share = lax.psum_scatter(grads, "dp", tiled=True)
    early, late = order[:len(order) // 2], order[len(order) // 2:]
    piece = input_of(early[0], tied(tg, grads))
    far = sent(piece, early[0])
    first = tied(saved[0], piece)
    packed, low_grad, logits = decode_grads(0, (first,) + saved[1:], low_input, target, reduce_weight.T, class_weight.T, None)
    swap = [(i, i ^ 1) for i in range(lax.axis_size("dp"))]
    bit = lax.axis_index("dp") % 2
    half = packed.shape[0] // 2
    mine = lax.dynamic_slice_in_dim(packed, bit * half, half, 0)
    packed = added(mine, lax.ppermute(lax.dynamic_slice_in_dim(packed, (1 - bit) * half, half, 0), "dp", swap))
    packed, far, tied_tg = lax.optimization_barrier((packed, far, tg))
    packed = scatter_sum(packed, "section", 1)
    received[early[0]] = far
    for k in early[1:]:
        received[k] = input_of(k, tied_tg)
        packed = tied(packed, received[k])
    held = tuple(received[k] for k in early)
    (share, packed), held = lax.optimization_barrier(((share, packed), held))
    received.update(zip(early, held))

    summed = lax.all_gather(share, "dp", tiled=True)
    for k in early[1:]:
        received[k] = sent(received[k], k)
    steps = [lambda v: scatter_sum(v, "dp", 2), lambda v: gather(v, "dp", 2)[0]]
    for k in late:
        packed, tied_tg = lax.optimization_barrier((packed, tg) + ((piece,) if k != late[0] else ()))[:2]
        piece = input_of(k, tied_tg)
        if steps:
            packed = steps.pop(0)(packed)
        packed, piece = lax.optimization_barrier((packed, piece))
        received[k] = sent(piece, k)
    input_grad = sum(received[k].astype(f32) for k in order).reshape(batch, height, width, in_chans // sections)
    packed, input_grad = gather(packed, "section", 1, input_grad)
    packed, summed = lax.optimization_barrier((packed, summed))
    other = lax.ppermute(packed, "dp", swap)
    merge1_grad, merge2_grad, reduce_grad, class_grad = unpack_decoder(bit.reshape(1).astype(jnp.int32), packed, other, chans, red,
                                                                       classes)

    wide, pool_weight_grad, proj_weight_grad = unpack_weights(summed, taps * own, own, proj.shape)
    sums = jnp.sum(sums.reshape(2, batch, -1), axis=1)
    return (
        jnp.transpose(logits, (0, 2, 3, 1)),
        input_grad,
        low_grad,
        jnp.transpose(wide.reshape(taps, own, in_chans), (2, 0, 1)),
        pool_weight_grad.T,
        sums[0].reshape(branches, own),
        sums[1].reshape(branches, own),
        proj_weight_grad.reshape(branches, own, chans),
        reduce_grad,
        merge1_grad,
        merge2_grad,
        class_grad,
    )


def solution(mesh):
    return jax.shard_map(
        local,
        mesh=mesh,
        in_specs=(
            P("dp", None, None, None), P("dp", "section", None, None), P("dp", None, None), P("dp", None, None),
            P(None, None, "section"), P(None, "section"), P(None, "section"), P(None, "section"), P(None, "section", None),
            P(), P(), P(), P(), P("dp", "section", None, None),
        ),
        out_specs=(
            P("dp", "section", None, None), P("dp", None, None, "section"), P("dp", "section", None, None),
            P(None, None, "section"), P(None, "section"), P(None, "section"), P(None, "section"), P(None, "section", None),
            P(), P(), P(), P(),
        ),
        check_vma=False,
    )
```

```python
import jax
import jax.numpy as jnp
import numpy as np
from jax import lax
from jax.experimental import pallas as pl
from jax.experimental.pallas import tpu as pltpu
from jax.sharding import PartitionSpec as P

IMAGES = 2
bf16 = jnp.bfloat16
f32 = jnp.float32
HALO = 4
LANE = 128


def upsample_matrix(coarse_count):
    fine = np.arange(4 * coarse_count)
    coarse, phase = fine // 4, fine % 4
    near = np.where(phase < 2, 5 + 2 * phase, 11 - 2 * phase) / 8.0
    far = np.clip(np.where(phase < 2, coarse - 1, coarse + 1), 0, coarse_count - 1)
    matrix = np.zeros((4 * coarse_count, coarse_count), np.float32)
    np.add.at(matrix, (fine, coarse), near)
    np.add.at(matrix, (fine, far), 1.0 - near)
    return matrix


def split_rows(first, stop, target):
    count = stop - first
    pieces = -(-count // target)
    edges = [first + (count * k) // pieces for k in range(pieces + 1)]
    return [(edges[k], edges[k + 1] - edges[k]) for k in range(pieces)]


def silu_and_slope(v):
    s = 0.5 + 0.5 * jnp.tanh(0.5 * v)
    a = v * s
    return a, s * (1.0 + v - a)


def row_tables(cut, fine_total, section_index, own_rows, coarse_rows):
    window = own_rows + 2 * HALO
    slots = window + 1
    first = section_index * own_rows - HALO
    cut = cut[:, None] - first
    gap = jnp.where((cut >= 1) & (cut < window), cut, window)
    slot = jnp.arange(slots, dtype=jnp.int32)[None, :]
    src = slot - (slot > gap).astype(jnp.int32)
    row = src + first
    valid = (slot != gap) & (row >= 0) & (row < fine_total)
    own = valid & (src >= HALO) & (src < own_rows + HALO)
    coarse = row // 4
    phase = row % 4
    near_weight = jnp.where(phase < 2, 5 + 2 * phase, 11 - 2 * phase).astype(f32) / 8.0
    far = jnp.clip(jnp.where(phase < 2, coarse - 1, coarse + 1), 0, coarse_rows - 1)
    base = section_index * (own_rows // 4) - 2
    held = own_rows // 4 + 4
    near_at = jnp.clip(coarse - base, 0, held - 1)
    far_at = jnp.clip(far - base, 0, held - 1)
    validf = valid.astype(f32)
    ownf = own.astype(f32)
    own_at = jnp.where(own, src - HALO, own_rows)
    slot_of = slot + (slot >= gap).astype(jnp.int32)
    inside = ((slot + first >= 0) & (slot + first < fine_total)).astype(f32)
    inside = jnp.broadcast_to(inside, validf.shape)
    ints = jnp.stack(
        [jnp.clip(src, 0, window - 1), near_at, far_at, own_at, slot_of, jnp.broadcast_to(gap, src.shape)], axis=1
    )
    floats = jnp.stack(
        [
            validf,
            ownf,
            near_weight * validf,
            (1.0 - near_weight) * validf,
            near_weight * ownf,
            (1.0 - near_weight) * ownf,
            inside,
        ],
        axis=1,
    )
    batch = cut.shape[0]
    return ints.astype(jnp.int32).reshape(batch, -1), floats.reshape(batch, -1)


def column_sides(v):
    n = v.shape[0]
    col = lax.broadcasted_iota(jnp.int32, v.shape, 0)
    left = jnp.where(col == 0, 0.0, pltpu.roll(v, 1, 0))
    right = jnp.where(col == n - 1, 0.0, pltpu.roll(v, n - 1, 0))
    return left, right


def three_columns(v):
    left, right = column_sides(v)
    return jnp.concatenate([left.astype(bf16), v.astype(bf16), right.astype(bf16)], axis=1)


def decode_kernel(own_rows, cols, chans, red, parts, before, at, itab, ftab, low_top, low, low_end, tgt, colm, colt, rwt, m1, m2, clst, *refs):
    projs, refs = refs[:parts], refs[parts + before:]
    decode_body(at[0], own_rows, cols, chans, red, projs, itab, ftab, low_top, low, low_end, tgt, colm, colt, rwt, m1, m2, clst, *refs)


def decode_body(first, own_rows, cols, chans, red, projs, itab, ftab, low_top, low, low_end, tgt, colm, colt, rwt, m1, m2, clst,
                  up_h, red_h, fst_h, sec_h, g2_h, g1_h, rg_h, pg_o,
                  jc, fc, sl1, rs, tgg, lift, drop, a0, a1, b0, b1,
                w1, rw3, clsb, wb2, wb1u, wb1r, up_o, red_o, fst_o, sec_o, g2_o, g1_o, rg_o, sems):
    m = pl.program_id(0)
    window = own_rows + 2 * HALO
    slots = window + 1
    held = projs[0].shape[1]
    wide = 3 * chans
    redw = jc.shape[2] - wide
    keep = own_rows + 3
    gc2, gc1 = jc.at[:, :, 0:wide], fc
    held_rows = [(up_o, up_h), (red_o, red_h), (fst_o, fst_h), (sec_o, sec_h), (g2_o, g2_h), (g1_o, g1_h), (rg_o, rg_h)]

    def out_copy(k, at):
        here, there = held_rows[k]
        return pltpu.make_async_copy(here.at[0:there.shape[1]], there.at[first + at], sems.at[k])

    @pl.when(m > 0)
    def _():
        for k in range(6):
            out_copy(k, m - 1).wait()

    @pl.when(m == 0)
    def _():
        w1[:, wide + 3 * red:] = jnp.zeros((3, redw - 3 * red, chans), bf16)
        clsb[...] = jnp.zeros(clsb.shape, bf16)
        clsb[0:clst.shape[0]] = clst[...]
        spare = jnp.zeros((redw - 3 * red, chans), bf16)
        rw3[...] = jnp.concatenate([rwt[...]] * 3 + [spare], axis=0).T
        for r in range(3):
            for d in range(3):
                part = slice(d * chans, (d + 1) * chans)
                w1[r, part] = m1[3 * r + d, 0:chans]
                w1[r, wide + d * red:wide + (d + 1) * red] = m1[3 * r + d, chans:]
                tap = 3 * (2 - r) + 2 - d
                wb2[r, part] = m2[tap].T
                wb1u[r, part] = m1[tap, 0:chans].T
            tails = [m1[3 * (2 - r) + d, chans:] for d in range(3)]
            wb1r[r] = jnp.concatenate(tails + [spare], axis=0).T

    def w2(r):
        return m2[3 * r:3 * r + 3].reshape(wide, chans)

    def it(k, j):
        return itab[first + m, k * slots + j]

    def ft(k, j):
        return ftab[first + m, k * slots + j]

    accs = (a0, a1)
    bccs = (b0, b1)

    def staged(blocks, multiply, finish):
        for k, block in enumerate(blocks):
            multiply(*block, accs[k % 2], bccs[k % 2])
            if k:
                finish(*blocks[k - 1], accs[(k - 1) % 2], bccs[(k - 1) % 2])
        k = len(blocks) - 1
        finish(*blocks[k], accs[k % 2], bccs[k % 2])

    def rows_of(ref, lo, n):
        return ref[lo:lo + n].reshape(n * cols, ref.shape[2])

    def dot(a, b):
        return jnp.dot(a, b, preferred_element_type=f32)

    @pl.when(m == 0)
    def _():
        tgg[...] = jnp.zeros(tgg.shape, bf16)

    for i in range(2):
        tgg[it(4, 2 + i)] = low_top[0, HALO][:, i * LANE:(i + 1) * LANE]
        tgg[it(4, own_rows + HALO + i)] = low_end[0, HALO][:, i * LANE:(i + 1) * LANE]
    for i in range(own_rows):
        tgg[it(4, HALO + i)] = tgt[0, i]
    tgg[it(5, 0)] = jnp.zeros((cols, LANE), bf16)

    lane = lax.broadcasted_iota(jnp.int32, (cols, redw), 1)

    def reduce_mul(ref, lo, n, place, acc, _):
        acc[0:n * cols] = dot(ref[0, lo:lo + n].reshape(n * cols, ref.shape[3]), rw3[...])

    def reduce_fin(ref, lo, n, place, acc, _):
        for r in range(n):
            a, slope = silu_and_slope(acc[r * cols:(r + 1) * cols])
            a = a * ft(6, place + r)
            left, right = column_sides(a)
            a = jnp.where(lane < red, left, jnp.where(lane < 2 * red, a, right))
            jc[it(4, place + r), :, wide:] = a.astype(bf16)
            if HALO <= place + r < own_rows + HALO:
                rs[place + r - HALO] = slope.astype(bf16)

    staged(
        [(low_top, 0, HALO, 0)]
        + [(low, lo, n, lo + HALO) for lo, n in split_rows(0, own_rows, 8)]
        + [(low_end, 0, HALO, own_rows + HALO)],
        reduce_mul, reduce_fin,
    )
    jc[it(5, 0), :, wide:] = jnp.zeros((cols, redw), bf16)

    for k in range(held):
        v = sum(p[0, k].astype(f32) for p in projs).astype(bf16)
        lift[k] = dot(colm[...], v)
    for j in range(slots):
        v = (ft(2, j) * lift[it(1, j)] + ft(3, j) * lift[it(2, j)]).astype(bf16)
        for d in range(3):
            jc[j, :, d * chans:(d + 1) * chans] = v[d * cols:(d + 1) * cols]
        if 3 <= j < 3 + keep:
            up_o[j - 3] = v[cols:2 * cols]

    red_o[...] = jc[3:3 + keep, :, wide:]
    out_copy(0, m).start()
    out_copy(1, m).start()

    def first_mul(lo, n, acc, _):
        acc[0:n * cols] = (
            dot(rows_of(jc, lo - 1, n), w1[0]) + dot(rows_of(jc, lo, n), w1[1]) + dot(rows_of(jc, lo + 1, n), w1[2])
        )

    def first_fin(lo, n, acc, _):
        for r in range(n):
            a, slope = silu_and_slope(acc[r * cols:(r + 1) * cols])
            keep_row = ft(0, lo + r)
            a = a * keep_row
            fc[lo + r] = three_columns(a)
            if 3 <= lo + r < 3 + keep:
                fst_o[lo + r - 3] = a.astype(bf16)
            sl1[lo + r] = (slope * keep_row).astype(bf16)

    staged(split_rows(1, slots - 1, 8), first_mul, first_fin)
    out_copy(2, m).start()

    def second_mul(lo, n, acc, bcc):
        acc[0:n * cols] = (
            dot(rows_of(fc, lo - 1, n), w2(0)) + dot(rows_of(fc, lo, n), w2(1)) + dot(rows_of(fc, lo + 1, n), w2(2))
        )
        bcc[0:n * cols] = dot(rows_of(tgg, lo, n), clsb[...])

    def second_fin(lo, n, acc, bcc):
        for r in range(n):
            j = lo + r
            a, slope = silu_and_slope(acc[r * cols:(r + 1) * cols])
            sec_o[it(3, j)] = a.astype(bf16)
            g = bcc[r * cols:(r + 1) * cols] * slope * ft(0, j)
            gc2[j] = three_columns(g)
            if HALO <= j <= own_rows + HALO:
                g2_o[j - HALO] = (g * ft(1, j)).astype(bf16)

    staged(split_rows(2, slots - 2, 8), second_mul, second_fin)
    out_copy(3, m).start()
    out_copy(4, m).start()

    def back2_mul(lo, n, acc, _):
        acc[0:n * cols] = (
            dot(rows_of(gc2, lo - 1, n), wb2[0]) + dot(rows_of(gc2, lo, n), wb2[1]) + dot(rows_of(gc2, lo + 1, n), wb2[2])
        )

    def back2_fin(lo, n, acc, _):
        for r in range(n):
            j = lo + r
            g = acc[r * cols:(r + 1) * cols] * sl1[j].astype(f32)
            gc1[j] = three_columns(g)
            if HALO <= j <= own_rows + HALO:
                g1_o[j - HALO] = (g * ft(1, j)).astype(bf16)

    staged(split_rows(3, slots - 3, 8), back2_mul, back2_fin)
    out_copy(5, m).start()

    drop[...] = jnp.zeros(drop.shape, f32)

    @pl.when(m > 0)
    def _():
        out_copy(6, m - 1).wait()

    def back1_mul(lo, n, acc, bcc):
        acc[0:n * cols] = (
            dot(rows_of(gc1, lo - 1, n), wb1u[0]) + dot(rows_of(gc1, lo, n), wb1u[1]) + dot(rows_of(gc1, lo + 1, n), wb1u[2])
        )
        mid = slice(chans, 2 * chans)
        bcc[0:n * cols] = (
            dot(rows_of(gc1, lo - 1, n)[:, mid], wb1r[0]) + dot(rows_of(gc1, lo, n)[:, mid], wb1r[1])
            + dot(rows_of(gc1, lo + 1, n)[:, mid], wb1r[2])
        )

    def back1_fin(lo, n, acc, bcc):
        for r in range(n):
            j = lo + r
            up = acc[r * cols:(r + 1) * cols]
            near, far = it(1, j), it(2, j)
            drop[near] += ft(4, j) * up
            drop[far] += ft(5, j) * up
            t = bcc[r * cols:(r + 1) * cols]
            left, right = column_sides(t)
            t = jnp.where(lane < red, right, jnp.where(lane < 2 * red, t, left))
            rg_o[it(3, j)] = (t * rs[it(3, j)].astype(f32)).astype(bf16)

    staged(split_rows(HALO, slots - HALO, 8), back1_mul, back1_fin)
    out_copy(6, m).start()

    for k in range(held):
        pg_o[0, k] = dot(colt[...], drop[k].astype(bf16)).astype(bf16)

    @pl.when(m == pl.num_programs(0) - 1)
    def _():
        for k in range(7):
            out_copy(k, m).wait()


def whole(a):
    return pl.BlockSpec(a.shape, lambda *at: (0,) * a.ndim, pipeline_mode=pl.Buffered(1))


def per(shape):
    return pl.BlockSpec((1,) + shape, lambda m, *at: (m,) + (0,) * len(shape))


def per_from(shape):
    return pl.BlockSpec((1,) + shape, lambda m, at: (m + at[0],) + (0,) * len(shape))


def total(shape):
    return pl.BlockSpec(shape, lambda *at: (0,) * len(shape))


def params():
    return pltpu.CompilerParams(vmem_limit_bytes=63 * 2 ** 20)


def saved_shapes(own_rows, cols, chans, red):
    redw = -(-3 * red // LANE) * LANE
    return [(own_rows + 3, cols, chans), (own_rows + 3, cols, redw), (own_rows + 3, cols, chans), (own_rows, cols, chans),
            (own_rows + 1, cols, chans), (own_rows + 1, cols, chans), (own_rows, cols, redw)]


def blank(batch, shapes):
    return tuple(pl.pallas_call(
        lambda *refs: None,
        out_specs=[pl.BlockSpec(memory_space=pl.ANY)] * len(shapes),
        out_shape=[jax.ShapeDtypeStruct((batch,) + s, bf16) for s in shapes],
        name="blank",
    )())


def decode(first, batch, tables, low_top, low_input, low_end, projs, target, reduce_t, merge1_weight, merge2_weight, class_t, earlier):
    ints, floats = tables
    all_batch, own_rows, cols, low_ch = low_input.shape
    window = own_rows + 2 * HALO
    slots = window + 1
    chans = merge2_weight.shape[1]
    red = reduce_t.shape[0]
    held, coarse_cols = projs[0].shape[1], projs[0].shape[2]
    redw = -(-3 * red // LANE) * LANE
    wide = 3 * chans
    colm = upsample_matrix(coarse_cols)
    zero = np.zeros((1, coarse_cols), np.float32)
    colm3 = jnp.asarray(np.concatenate([zero, colm[:-1], colm, colm[1:], zero], axis=0), bf16)
    colt = jnp.asarray(colm.T, bf16)
    keep = own_rows + 3
    smem = pl.BlockSpec(memory_space=pltpu.SMEM)
    hbm = pl.BlockSpec(memory_space=pl.ANY)
    most = max(n for k in range(5) for _, n in split_rows(k, slots - k, 8))
    consts = (colm3, colt, reduce_t, merge1_weight, merge2_weight, class_t)
    shapes = saved_shapes(own_rows, cols, chans, red)
    stage = [(s[0] + (1 if k in (3, 6) else 0),) + s[1:] for k, s in enumerate(shapes)]
    back_shape = (held, coarse_cols, chans)
    saved = pl.pallas_call(
        lambda *refs: decode_kernel(own_rows, cols, chans, red, len(projs), len(earlier), *refs),
        grid_spec=pltpu.PrefetchScalarGridSpec(
            num_scalar_prefetch=1,
            grid=(batch,),
            in_specs=[smem, smem] + [per_from(a.shape[1:]) for a in (low_top, low_input, low_end, target)]
            + [whole(a) for a in consts] + [per(p.shape[1:]) for p in projs] + [hbm] * len(earlier),
            out_specs=[hbm] * len(shapes) + [per(back_shape)],
            scratch_shapes=[
                pltpu.VMEM((slots, cols, wide + redw), bf16), pltpu.VMEM((slots, cols, wide), bf16),
                pltpu.VMEM((slots, cols, chans), bf16), pltpu.VMEM((own_rows + 1, cols, redw), bf16),
                pltpu.VMEM((slots, cols, LANE), bf16),
                pltpu.VMEM((held, 3 * cols, chans), f32), pltpu.VMEM((held, cols, chans), f32),
                pltpu.VMEM((most * cols, chans), f32), pltpu.VMEM((most * cols, chans), f32),
                pltpu.VMEM((most * cols, chans), f32), pltpu.VMEM((most * cols, chans), f32),
                pltpu.VMEM((3, wide + redw, chans), bf16), pltpu.VMEM((low_ch, redw), bf16), pltpu.VMEM((LANE, chans), bf16),
                pltpu.VMEM((3, wide, chans), bf16), pltpu.VMEM((3, wide, chans), bf16), pltpu.VMEM((3, chans, redw), bf16),
            ] + [pltpu.VMEM(s, bf16) for s in stage] + [pltpu.SemaphoreType.DMA((7,))],
        ),
        out_shape=[jax.ShapeDtypeStruct((all_batch,) + s, bf16) for s in shapes] + [jax.ShapeDtypeStruct((batch,) + back_shape, bf16)],
        input_output_aliases={7 + len(consts) + len(projs) + k: k for k in range(len(earlier))},
        compiler_params=params(),
        name="decode",
    )(jnp.full((1,), first, jnp.int32), ints, floats, low_top, low_input, low_end, target, *consts, *projs, *earlier)
    return saved[7], tuple(saved[:7])


def grads_kernel(own_rows, cols, chans, red, before, up, red3, fst, sec, g2, g1, rg, low, tgt, clst, rwt, *refs):
    earlier = refs[:before]
    packed, lowgrad, logits, o1, o2, oc, orr, upc, fcc = refs[before:]
    m = pl.program_id(0)
    keep = own_rows + 3
    wide = 3 * chans
    span = own_rows + 1
    classes = clst.shape[0]

    @pl.when(m == 0)
    def _():
        o1[...] = jnp.zeros(o1.shape, f32)
        o2[...] = jnp.zeros(o2.shape, f32)
        oc[...] = jnp.zeros(oc.shape, f32)
        orr[...] = jnp.zeros(orr.shape, f32)

    def tdot(a, b):
        return lax.dot_general(a, b, (((0,), (0,)), ((), ())), preferred_element_type=f32)

    for j in range(keep):
        upc[j] = three_columns(up[0, j].astype(f32))
    for j in range(keep):
        fcc[j] = three_columns(fst[0, j].astype(f32))

    def flat(v):
        return v.reshape(v.shape[0] * cols, v.shape[2])

    gg1 = flat(g1[0])
    for dy in range(3):
        o1[dy, 0:wide] += tdot(flat(upc[dy:dy + span]), gg1)
        o1[dy, wide:] += tdot(flat(red3[0, dy:dy + span]), gg1)
    gg2 = flat(g2[0])
    for dy in range(3):
        o2[dy] += tdot(flat(fcc[dy:dy + span]), gg2)
    oc[...] += tdot(flat(sec[0]), flat(tgt[0]))
    orr[...] += tdot(flat(low[0]), flat(rg[0]))
    spare = jnp.zeros((rg.shape[3] - 3 * red, chans), bf16)
    rb3 = jnp.concatenate([rwt[...]] * 3 + [spare], axis=0)
    for r in range(own_rows):
        lowgrad[0, r] = jnp.dot(rg[0, r], rb3, preferred_element_type=f32)
        lt = lax.dot_general(clst[...], sec[0, r], (((1,), (1,)), ((), ())), preferred_element_type=f32)
        logits[0, :, r] = lt

    @pl.when(m == pl.num_programs(0) - 1)
    def _():
        rows = chans + red
        for dy in range(3):
            for d in range(3):
                at = (3 * dy + d) * rows
                packed[at:at + chans] = o1[dy, d * chans:(d + 1) * chans].astype(bf16)
                packed[at + chans:at + rows] = o1[dy, wide + d * red:wide + (d + 1) * red].astype(bf16)
            packed[9 * rows + dy * wide:9 * rows + (dy + 1) * wide] = o2[dy].astype(bf16)
        at = 9 * rows + 3 * wide
        packed[at:] = jnp.zeros((packed.shape[0] - at, chans), bf16)
        t = orr[...].T
        packed[at:at + red] = (t[0:red] + t[red:2 * red] + t[2 * red:3 * red]).astype(bf16)
        packed[at + red:at + red + 32] = oc[...].T[0:32].astype(bf16)
        if before:
            packed[...] = (packed[...].astype(f32) + earlier[0][...].astype(f32)).astype(bf16)


def packed_rows(chans, red):
    return 9 * (chans + red) + 9 * chans + red + 32


def decode_grads(first, saved, low_input, target, reduce_t, class_t, earlier):
    up, red3, fst, sec, g2, g1, rg = saved
    batch = up.shape[0]
    all_batch, own_rows, cols, low_ch = low_input.shape
    chans = up.shape[3]
    redw = red3.shape[3]
    red = reduce_t.shape[0]
    classes = class_t.shape[0]
    wide = 3 * chans
    keep = own_rows + 3
    rows = packed_rows(chans, red)
    hbm = pl.BlockSpec(memory_space=pl.ANY)
    tots = [(3, wide + redw, chans), (3, wide, chans), (chans, LANE), (low_ch, redw)]
    pers = [(own_rows, cols, low_ch), (classes, own_rows, cols)]
    packed, lowgrad, logits = pl.pallas_call(
        lambda *refs: grads_kernel(own_rows, cols, chans, red, 3 if earlier else 0, *refs),
        grid=(batch,),
        in_specs=[per((keep, cols, chans)), per((keep, cols, redw)), per((keep, cols, chans)), per((own_rows, cols, chans)),
                  per((own_rows + 1, cols, chans)), per((own_rows + 1, cols, chans)), per((own_rows, cols, redw)),
                  per((own_rows, cols, low_ch)), per(target.shape[1:]), whole(class_t), whole(reduce_t)]
        + ([whole(earlier[0]), hbm, hbm] if earlier else []),
        out_specs=[total((rows, chans))] + [per(s) for s in pers],
        out_shape=[jax.ShapeDtypeStruct((rows, chans), bf16)] + [jax.ShapeDtypeStruct((all_batch,) + s, f32) for s in pers],
        input_output_aliases={12: 1, 13: 2} if earlier else {},
        scratch_shapes=[pltpu.VMEM(s, f32) for s in tots]
        + [pltpu.VMEM((keep, cols, wide), bf16), pltpu.VMEM((keep, cols, wide), bf16)],
        compiler_params=params(),
        name="decode_grads",
        cost_estimate=pl.CostEstimate(flops=1, bytes_accessed=1, transcendentals=1),
    )(up, red3, fst, sec, g2, g1, rg, low_input, target, class_t, reduce_t, *(earlier or ()))
    return packed, lowgrad, logits


def unpack_decoder(bit, mine, other, chans, red, classes):
    rows = chans + red
    half = mine.shape[0]
    at = 9 * rows + 9 * chans
    shapes = [(9, rows, chans), (9, chans, chans), (red, chans), (classes, chans)]

    def kernel(bit, a, b, m1, m2, rw, cw, v):
        v[pl.ds(pl.multiple_of(bit[0] * half, 16), half)] = a[...]
        v[pl.ds(pl.multiple_of((1 - bit[0]) * half, 16), half)] = b[...]
        for t in range(9):
            m1[t] = v[t * rows:(t + 1) * rows].astype(f32)
            m2[t] = v[9 * rows + t * chans:9 * rows + (t + 1) * chans].astype(f32)
        rw[...] = v[at:at + red].astype(f32)
        cw[...] = v[at + red:at + red + 32].astype(f32)[0:classes]

    m1, m2, rw, cw = pl.pallas_call(
        kernel,
        grid=(1,),
        in_specs=[pl.BlockSpec(memory_space=pltpu.SMEM), whole(mine), whole(other)],
        out_specs=[total(s) for s in shapes],
        out_shape=[jax.ShapeDtypeStruct(s, f32) for s in shapes],
        scratch_shapes=[pltpu.VMEM((2 * half, chans), bf16)],
        compiler_params=params(),
        name="unpack_decoder",
    )(bit, mine, other)
    return m1, m2, rw.T, cw.T


atrous_rates = (6, 12, 18)
epsilon = 1e-05


def tap_list():
    listed = [(0, 0, 0)]
    for branch_index, rate_value in enumerate(atrous_rates):
        for step_rows in (-1, 0, 1):
            for step_cols in (-1, 0, 1):
                listed.append((rate_value * step_rows, rate_value * step_cols, branch_index + 1))
    return listed


def pixel_places(batch, height, width):
    pixel = np.arange(height * width)
    places = np.stack([np.tile(pixel // width, batch), np.tile(pixel % width, batch), np.repeat(np.arange(batch), height * width)])
    return jnp.asarray(np.pad(places, ((0, 5), (0, 0))), jnp.int32)


class Pixels:
    def __init__(self, places, cuts, batch, height, width):
        self.row, self.col, self.canvas = places[0:1], places[1:2], places[2:3]
        self.height, self.width = height, width
        cut = jnp.full(self.row.shape, cuts[0], jnp.int32)
        for m in range(1, batch):
            cut = jnp.where(self.canvas == m, cuts[m], cut)
        self.cut = cut
        self.band = self.row >= cut

    def valid(self, dr, dc):
        row, col = self.row + dr, self.col + dc
        inside = (row >= 0) & (row < self.height) & (col >= 0) & (col < self.width)
        same = jnp.where(row >= self.cut, 1, 0) == jnp.where(self.band, 1, 0)
        return jnp.where(inside & same, 1.0, 0.0)

    def image(self):
        return IMAGES * self.canvas + jnp.where(self.band, 1, 0)


def image_counts(cuts, batch, height, width):
    index = lax.broadcasted_iota(jnp.int32, (IMAGES * batch, 1), 0)
    out = jnp.zeros((IMAGES * batch, 1), f32)
    for m in range(batch):
        first = cuts[m] * width
        out = jnp.where(index == IMAGES * m, first.astype(f32), out)
        out = jnp.where(index == IMAGES * m + 1, (height * width - first).astype(f32), out)
    return jnp.maximum(out, 1.0)


def branch_kernel(taps, batch, height, width, cuts, x, w, places, pw, br_o, mom_o, pooled_o, y, pool, mom):
    i = pl.program_id(0)
    last = pl.num_programs(0) - 1
    block = x.shape[0]
    total = y.shape[1]
    pixels = total // batch
    own = pw.shape[0]
    at = pl.multiple_of(i * block, block)

    @pl.when(i == 0)
    def _():
        pool[...] = jnp.zeros(pool.shape, f32)
        mom[...] = jnp.zeros(mom.shape, f32)

    def nt(a, b):
        return lax.dot_general(a, b, (((1,), (1,)), ((), ())), preferred_element_type=f32)

    canvas, row = places[2:3, pl.ds(at, block)], places[0:1, pl.ds(at, block)]
    cut = jnp.full(row.shape, cuts[0], jnp.int32)
    for m in range(1, batch):
        cut = jnp.where(canvas == m, cuts[m], cut)
    image = IMAGES * canvas + jnp.where(row >= cut, 1, 0)
    index = lax.broadcasted_iota(jnp.int32, (IMAGES * batch, block), 0)
    member = jnp.where(image == index, 1.0, 0.0).astype(bf16)
    pool[...] += jnp.dot(member, x[...], preferred_element_type=f32)

    @pl.when(i < last)
    def _():
        y[:, pl.ds(at, block)] = nt(w[...], x[...])

    def keep(m, b, v):
        part = slice(b * own, (b + 1) * own)
        br_o[m, part] = v
        mom[part, m:m + 1] = jnp.sum(v, axis=1, keepdims=True)
        mom[part, batch + m:batch + m + 1] = jnp.sum(v * v, axis=1, keepdims=True)

    @pl.when(i == last)
    def _():
        px = Pixels(places, cuts, batch, height, width)
        spans = []
        for b in range(4):
            mine = [t for t, tap in enumerate(taps) if tap[2] == b]
            spans.append((mine[0], mine[-1] + 1))

        def multiply(b):
            lo, hi = spans[b][0] * own, spans[b][1] * own
            y[lo:hi, total - block:] = nt(w[lo:hi], x[...])

        def finish(b):
            acc = None
            for t in range(*spans[b]):
                dr, dc, _ = taps[t]
                v = y[t * own:(t + 1) * own]
                shift = dr * width + dc
                if shift:
                    v = pltpu.roll(v, (-shift) % total, 1) * px.valid(dr, dc)
                acc = v if acc is None else acc + v
            for m in range(batch):
                keep(m, b, acc[:, m * pixels:(m + 1) * pixels])

        multiply(0)
        multiply(1)
        multiply(2)
        finish(0)
        finish(1)
        multiply(3)
        finish(2)
        finish(3)
        pooled = (pool[...] / image_counts(cuts, batch, height, width)).astype(bf16)
        pooled_o[...] = pooled
        po = nt(pw[...], pooled)
        for m in range(batch):
            band = px.band[:, m * pixels:(m + 1) * pixels]
            keep(m, 4, jnp.where(band, po[:, IMAGES * m + 1:IMAGES * m + 2], po[:, IMAGES * m:IMAGES * m + 1]))
        mom_o[...] = mom[...].T[0:mom_o.shape[0]]


def aspp_forward(cuts, x, wt, pwt, batch, height, width):
    all_pixels, in_chans = x.shape
    pixels = height * width
    own = pwt.shape[0]
    taps = tap_list()
    block = all_pixels // 3 if all_pixels % 3 == 0 and (all_pixels // 3) % LANE == 0 else all_pixels
    places = pixel_places(batch, height, width)
    outs = [((batch, 5 * own, pixels), f32), ((2 * batch, 5 * own), f32), ((IMAGES * batch, in_chans), bf16)]
    return pl.pallas_call(
        lambda *refs: branch_kernel(taps, batch, height, width, *refs),
        grid=(all_pixels // block,),
        in_specs=[pl.BlockSpec(memory_space=pltpu.SMEM), pl.BlockSpec((block, in_chans), lambda i: (i, 0)),
                  whole(wt), whole(places), whole(pwt)],
        out_specs=[total(s) for s, _ in outs],
        out_shape=[jax.ShapeDtypeStruct(s, d) for s, d in outs],
        scratch_shapes=[pltpu.VMEM((len(taps) * own, all_pixels), f32), pltpu.VMEM((IMAGES * batch, in_chans), f32),
                        pltpu.VMEM((5 * own, LANE), f32)],
        compiler_params=params(),
        name="aspp_forward",
    )(cuts, x, wt, places, pwt)


def column(t, m):
    if isinstance(m, int):
        return t[:, m:m + 1]
    lane = lax.broadcasted_iota(jnp.int32, t.shape, 1)
    return jnp.sum(jnp.where(lane == m, t, 0.0), axis=1, keepdims=True)


def norm_columns(stats, scale, m, batch, count):
    t = stats[...].T
    mean = column(t, m) / count
    inv_std = lax.rsqrt(column(t, batch + m) / count - mean * mean + epsilon)
    s = scale[...].T
    half = s.shape[1] // 2
    gain = jnp.concatenate([s[:, k:k + 1] for k in range(half)], axis=0)
    shift = jnp.concatenate([s[:, half + k:half + k + 1] for k in range(half)], axis=0)
    return mean, inv_std, gain, shift


def project_kernel(group, count, coarse_rows, at_ref, offsets, br, stats, scale, proj, *refs):
    outs, rows = refs[:-1], refs[-1]
    batch = stats.shape[0] // 2
    height, width, chans = rows.shape[0] - 4, rows.shape[1], rows.shape[2]
    held = coarse_rows + 4
    rows[0:2] = jnp.zeros((2, width, chans), f32)
    rows[height + 2:] = jnp.zeros((2, width, chans), f32)
    for at in range(group):
        mean, inv_std, gain, shift = norm_columns(stats, scale, at_ref[0] + at, batch, count)
        active, _ = silu_and_slope((br[at] - mean) * inv_std * gain + shift)
        partial = lax.dot_general(active.astype(bf16), proj[...], (((0,), (0,)), ((), ())), preferred_element_type=f32)
        rows[2:height + 2] = partial.reshape(height, width, chans)
        for k, o in enumerate(outs):
            o[at] = rows[pl.ds(offsets[k], held)].astype(bf16)


def project(first, group, offsets, br, stats, scale, proj, count, coarse_rows, parts, height, width):
    chans = proj.shape[1]
    shape = (group, coarse_rows + 4, width, chans)
    pixels = br.shape[2]
    return pl.pallas_call(
        lambda *refs: project_kernel(group, count, coarse_rows, *refs),
        grid_spec=pltpu.PrefetchScalarGridSpec(
            num_scalar_prefetch=1,
            grid=(1,),
            in_specs=[pl.BlockSpec(memory_space=pltpu.SMEM), pl.BlockSpec((pl.Element(group), pl.Element(br.shape[1]), pl.Element(pixels)), lambda i, at: (at[0], 0, 0)),
                      whole(stats), whole(scale), whole(proj)],
            out_specs=[total(shape)] * parts,
            scratch_shapes=[pltpu.VMEM((height + 4, width, chans), f32)],
        ),
        out_shape=[jax.ShapeDtypeStruct(shape, bf16)] * parts,
        compiler_params=params(),
        name="project",
    )(jnp.full((1,), first, jnp.int32), offsets, br, stats, scale, proj)


def norm_back_kernel(count, parts, at_ref, offsets, br, stats, scale, proj, earlier, sums_before, *refs):
    pieces = refs[:parts]
    grad_o, sums_o, projgrad_o, rows, sums = refs[parts:]
    height, width, chans = rows.shape[0] - 4, rows.shape[1], rows.shape[2]
    group, held = pieces[0].shape[0], pieces[0].shape[1]
    batch = stats.shape[0] // 2
    sums[...] = jnp.zeros(sums.shape, f32)
    projgrad = earlier[...]
    for at in range(group):
        m = at_ref[0] + at
        rows[...] = jnp.zeros(rows.shape, f32)
        for k, piece in enumerate(pieces):
            rows[pl.ds(offsets[k], held)] += piece[at].astype(f32)
        grad = rows[2:height + 2].reshape(height * width, chans).astype(bf16)
        mean, inv_std, gain, shift = norm_columns(stats, scale, m, batch, count)
        scaled = (br[at] - mean) * inv_std
        active, slope = silu_and_slope(scaled * gain + shift)
        back = lax.dot_general(proj[...], grad, (((1,), (1,)), ((), ())), preferred_element_type=f32) * slope
        grad_o[at] = back
        lane = lax.broadcasted_iota(jnp.int32, sums.shape, 1)
        products = jnp.sum(back * scaled, axis=1, keepdims=True)
        sums[...] += jnp.where(lane == m, products, jnp.where(lane == batch + m, jnp.sum(back, axis=1, keepdims=True), 0.0))
        projgrad = projgrad + jnp.dot(active.astype(bf16), grad, preferred_element_type=f32)
    projgrad_o[...] = projgrad
    sums_o[...] = sums_before[...] + sums[...].T[0:sums_o.shape[0]]


def norm_back(first, offsets, br, stats, scale, proj, earlier, sums_before, pieces, count, height, width):
    batch, chans5, pixels = br.shape
    group = pieces[0].shape[0]
    outs = [((group, chans5, pixels), f32), (stats.shape, f32), (proj.shape, f32)]
    return pl.pallas_call(
        lambda *refs: norm_back_kernel(count, len(pieces), *refs),
        grid_spec=pltpu.PrefetchScalarGridSpec(
            num_scalar_prefetch=1,
            grid=(1,),
            in_specs=[pl.BlockSpec(memory_space=pltpu.SMEM), pl.BlockSpec((pl.Element(group), pl.Element(chans5), pl.Element(pixels)), lambda i, at: (at[0], 0, 0)),
                      whole(stats), whole(scale), whole(proj), whole(earlier), whole(sums_before)] + [whole(p) for p in pieces],
            out_specs=[total(s) for s, _ in outs],
            scratch_shapes=[pltpu.VMEM((height + 4, width, proj.shape[1]), f32), pltpu.VMEM((chans5, LANE), f32)],
        ),
        out_shape=[jax.ShapeDtypeStruct(s, d) for s, d in outs],
        compiler_params=params(),
        name="norm_back",
    )(jnp.full((1,), first, jnp.int32), offsets, br, stats, scale, proj, earlier, sums_before, *pieces)


def weight_grad_kernel(taps, groups, height, width, count, cuts, stats, scale, sums, places, projgrad, x_hbm, br_hbm, *refs):
    backs = refs[:groups]
    wg_hbm, tg_hbm, pg_o, both, x, tg, wg, br, back, sems, in_sems = refs[groups:]
    batch = br.shape[0]
    owner = [(g, k) for g, part in enumerate(backs) for k in range(part.shape[0])]

    def in_copies(m):
        g, k = owner[m]
        return (pltpu.make_async_copy(br_hbm.at[m], br.at[m], in_sems.at[m]),
                pltpu.make_async_copy(backs[g].at[k], back.at[m], in_sems.at[batch + m]))

    for m in range(batch):
        for copy in in_copies(m):
            copy.start()
    own = pg_o.shape[0]
    pixels = br.shape[2]
    rows, all_pixels = tg.shape
    in_chans = x.shape[1]
    filled = (len(taps) + 1) * own
    x_copy = pltpu.make_async_copy(x_hbm, x, sems.at[0])
    x_copy.start()
    px = Pixels(places, cuts, batch, height, width)
    pool_grad = jnp.zeros((own, LANE), f32)
    lane = lax.broadcasted_iota(jnp.int32, (own, LANE), 1)
    t = sums[...].T
    for m in range(batch):
        for copy in in_copies(m):
            copy.wait()
        mean, inv_std, gain, _ = norm_columns(stats, scale, m, batch, count)
        gain_sum, shift_sum = t[:, m:m + 1], t[:, batch + m:batch + m + 1]
        scaled = (br[m] - mean) * inv_std
        grad = inv_std * gain * (back[m] - (shift_sum + scaled * gain_sum) / count)
        both[0:4 * own, m * pixels:(m + 1) * pixels] = grad[0:4 * own]
        pool = grad[4 * own:]
        band = px.band[:, m * pixels:(m + 1) * pixels]
        upper = jnp.sum(jnp.where(band, 0.0, pool), axis=1, keepdims=True).astype(bf16).astype(f32)
        lower = jnp.sum(jnp.where(band, pool, 0.0), axis=1, keepdims=True).astype(bf16).astype(f32)
        pool_grad = jnp.where(lane == IMAGES * m, upper, pool_grad)
        pool_grad = jnp.where(lane == IMAGES * m + 1, lower, pool_grad)
        many = (cuts[m] * width).astype(f32)
        spread = jnp.where(band, lower / jnp.maximum(height * width - many, 1.0), upper / jnp.maximum(many, 1.0))
        both[4 * own:, m * pixels:(m + 1) * pixels] = spread
    pg_o[...] = pool_grad[:, 0:pg_o.shape[1]].astype(bf16)

    for k, (dr, dc, b) in enumerate(taps):
        v = both[b * own:(b + 1) * own]
        shift = dr * width + dc
        if shift:
            v = pltpu.roll(v * px.valid(dr, dc), shift % all_pixels, 1)
        tg[k * own:(k + 1) * own] = v.astype(bf16)
    tg[filled - own:] = both[4 * own:].astype(bf16)
    tg_copy = pltpu.make_async_copy(tg, tg_hbm, sems.at[1])
    tg_copy.start()
    x_copy.wait()
    chans = projgrad.shape[1]
    some = projgrad.shape[0] * chans // in_chans
    step = 512 if in_chans % 512 == 0 else in_chans
    wg[filled:] = jnp.zeros((wg.shape[0] - filled, in_chans), bf16)
    for k in range(in_chans // chans):
        wg[filled:filled + some, k * chans:(k + 1) * chans] = projgrad[k * some:(k + 1) * some].astype(bf16)

    def out_copy(n):
        part = pl.ds(pl.multiple_of(n * step, step), step)
        return pltpu.make_async_copy(wg.at[:, part], wg_hbm.at[:, part], sems.at[2 + n])

    def multiply(n, _):
        part = pl.ds(pl.multiple_of(n * step, step), step)
        wg[0:filled, part] = jnp.dot(tg[...], x[:, part], preferred_element_type=f32).astype(bf16)
        out_copy(n).start()
        return 0

    lax.fori_loop(0, in_chans // step, multiply, 0)
    tg_copy.wait()
    for n in range(in_chans // step):
        out_copy(n).wait()


def aspp_weight_grads(rows, cuts, x, br, stats, scale, sums, projgrad, backs, count, height, width):
    all_pixels, in_chans = x.shape
    batch, chans5, pixels = br.shape
    own = chans5 // 5
    places = pixel_places(batch, height, width)
    groups = len(backs)
    hbm = pl.BlockSpec(memory_space=pl.ANY)
    outs = [(rows, in_chans), ((len(tap_list()) + 1) * own, all_pixels), (own, IMAGES * batch)]
    return pl.pallas_call(
        lambda *refs: weight_grad_kernel(tap_list(), groups, height, width, count, *refs),
        grid=(1,),
        in_specs=[pl.BlockSpec(memory_space=pltpu.SMEM)] + [whole(v) for v in (stats, scale, sums, places, projgrad)]
        + [hbm] * (2 + len(backs)),
        out_specs=[hbm, hbm, total(outs[2])],
        out_shape=[jax.ShapeDtypeStruct(s, bf16) for s in outs],
        scratch_shapes=[pltpu.VMEM((chans5, all_pixels), f32), pltpu.VMEM((all_pixels, in_chans), bf16),
                        pltpu.VMEM(outs[1], bf16), pltpu.VMEM(outs[0], bf16),
                        pltpu.VMEM(br.shape, f32), pltpu.VMEM(br.shape, f32),
                        pltpu.SemaphoreType.DMA((2 + in_chans // 512 + 1,)), pltpu.SemaphoreType.DMA((2 * batch,))],
        compiler_params=params(),
        name="aspp_weight_grads",
    )(cuts, stats, scale, sums, places, projgrad, x, br, *backs)


def unpack_weights(summed, wide, own, proj_shape):
    rows, in_chans = summed.shape
    block = 512 if in_chans % 512 == 0 else in_chans
    chans = proj_shape[1]
    pieces = block // chans
    some = proj_shape[0] * chans // in_chans

    def kernel(v, wide_o, pool_o, proj_o):
        wide_o[...] = v[0:wide].astype(f32)
        pool_o[...] = v[wide:wide + own].astype(f32)
        tail = v[wide + own:].astype(f32)
        for k in range(pieces):
            proj_o[k * some:(k + 1) * some] = tail[0:some, k * chans:(k + 1) * chans]

    def lanes(a):
        return pl.BlockSpec((a, block), lambda j: (0, j))

    return pl.pallas_call(
        kernel,
        grid=(in_chans // block,),
        in_specs=[lanes(rows)],
        out_specs=[lanes(wide), lanes(own), pl.BlockSpec((some * pieces, chans), lambda j: (j, 0))],
        out_shape=[jax.ShapeDtypeStruct(s, f32) for s in ((wide, in_chans), (own, in_chans), proj_shape)],
        compiler_params=params(),
        name="unpack_weights",
    )(summed)


def input_grad_kernel(batch, span, height, width, at, cuts, tg, w, pg, pw, band, o):
    i = pl.program_id(0)
    pixels = height * width
    v = lax.dot_general(tg[...], w[...], (((0,), (0,)), ((), ())), preferred_element_type=f32)
    image = lax.dot_general(pg[...], pw[...], (((0,), (0,)), ((), ())), preferred_element_type=f32)
    image = image / image_counts(cuts, batch, height, width)
    index = lax.broadcasted_iota(jnp.int32, (IMAGES * batch, 1), 0)
    row = band[...]
    for k in range(span):
        m = i * span + k
        first = jnp.sum(jnp.where(index == IMAGES * m, image, 0.0), axis=0, keepdims=True)
        second = jnp.sum(jnp.where(index == IMAGES * m + 1, image, 0.0), axis=0, keepdims=True)
        part = slice(k * pixels, (k + 1) * pixels)
        o[part] = (v[part] + jnp.where(row >= cuts[m], second, first)).astype(bf16)


def aspp_input_grad(place, cuts, tg, wt, pool_grad, pwt, parts, height, width):
    rows, in_chans = wt.shape
    all_pixels = tg.shape[1]
    own = pwt.shape[0]
    pixels = height * width
    batch = all_pixels // pixels
    block = in_chans // parts
    span = 2 if (2 * pixels) % LANE == 0 and batch % 2 == 0 else batch
    row_column = jnp.asarray(np.arange(pixels)[:, None] // width, jnp.int32)
    return pl.pallas_call(
        lambda *refs: input_grad_kernel(batch, span, height, width, *refs),
        grid_spec=pltpu.PrefetchScalarGridSpec(
            num_scalar_prefetch=2,
            grid=(batch // span,),
            in_specs=[
                pl.BlockSpec((rows, span * pixels), lambda i, at, cuts: (0, i)),
                pl.BlockSpec((rows, block), lambda i, at, cuts: (0, at[0])),
                whole(pool_grad),
                pl.BlockSpec((own, block), lambda i, at, cuts: (0, at[0])),
                whole(row_column),
            ],
            out_specs=pl.BlockSpec((span * pixels, block), lambda i, at, cuts: (i, 0)),
        ),
        out_shape=jax.ShapeDtypeStruct((all_pixels, block), bf16),
        compiler_params=params(),
        name="aspp_input_grad",
        cost_estimate=pl.CostEstimate(flops=1, bytes_accessed=1, transcendentals=1),
    )(place, cuts, tg, wt, pool_grad, pwt, row_column)


def doubled_sum(value, axis):
    size = lax.axis_size(axis)
    step = 1
    while step < size:
        value = value + lax.ppermute(value, axis, [(i, i ^ step) for i in range(size)])
        step *= 2
    return value


def exchanged(pieces, axis):
    size = lax.axis_size(axis)
    return [pieces[0]] + [lax.ppermute(pieces[k], axis, [(i, i ^ k) for i in range(size)]) for k in range(1, size)]


def added(a, b):
    return (a.astype(f32) + b.astype(f32)).astype(bf16)


def scatter_sum(value, axis, unit):
    size = lax.axis_size(axis)
    count = size // unit
    me = lax.axis_index(axis)
    rows = value.shape[0] // count
    out = None
    for k in range(count):
        piece = lax.dynamic_slice_in_dim(value, ((me // unit) ^ k) * rows, rows, 0)
        if k:
            piece = lax.ppermute(piece, axis, [(i, i ^ (k * unit)) for i in range(size)])
        out = piece.astype(f32) if out is None else out + piece.astype(f32)
    return out.astype(bf16)


def gather(value, axis, unit, beside=()):
    size = lax.axis_size(axis)
    count = size // unit
    me = lax.axis_index(axis)
    got = [value] + [lax.ppermute(value, axis, [(i, i ^ (k * unit)) for i in range(size)]) for k in range(1, count)]
    rows = value.shape[0]
    got, beside = lax.optimization_barrier((got, beside))
    if rows % 16 == 0 and rows * count >= 1024:
        places = ((me // unit) ^ jnp.arange(count, dtype=jnp.int32)) * rows

        def kernel(at, *refs):
            for k in range(count):
                refs[count][pl.ds(pl.multiple_of(at[k], 16), rows)] = refs[k][...]

        return pl.pallas_call(
            kernel,
            grid=(1,),
            in_specs=[pl.BlockSpec(memory_space=pltpu.SMEM)] + [whole(piece) for piece in got],
            out_specs=total((count * rows,) + value.shape[1:]),
            out_shape=jax.ShapeDtypeStruct((count * rows,) + value.shape[1:], value.dtype),
            compiler_params=params(),
            name="join_rows",
        )(places, *got), beside
    out = jnp.zeros((count * rows,) + value.shape[1:], value.dtype)
    for k, piece in enumerate(got):
        out = lax.dynamic_update_slice_in_dim(out, piece, ((me // unit) ^ k) * rows, 0)
    return out, beside


def tied(value, *others):
    return lax.optimization_barrier((value,) + others)[0]


def local(aspp_input, low_input, aspp_ids, low_ids, aspp_weight, pool_weight, bn_gain, bn_shift, projection_matrix,
          reduce_weight, merge1_weight, merge2_weight, class_weight, logit_grad):
    section = lax.axis_index("section")
    sections = lax.axis_size("section")
    batch, height, width, in_chans = aspp_input.shape
    taps, own = aspp_weight.shape[1], aspp_weight.shape[2]
    branches = bn_gain.shape[0]
    chans = projection_matrix.shape[2]
    red = reduce_weight.shape[1]
    classes = class_weight.shape[1]
    fine_rows, fine_cols = low_input.shape[1], low_input.shape[2]
    pixels = height * width
    count = pixels * lax.axis_size("dp")
    coarse_rows = fine_rows // 4
    groups = [(0, batch - 1), (batch - 1, 1)]

    x = aspp_input.reshape(batch * pixels, in_chans)
    wt = jnp.transpose(aspp_weight, (1, 2, 0)).reshape(taps * own, in_chans)
    pwt = pool_weight.T
    proj = projection_matrix.reshape(branches * own, chans)
    cuts = jnp.sum((aspp_ids[:, :, 0] == 0).astype(jnp.int32), axis=1)
    br, moments, pooled = aspp_forward(cuts, x, wt, pwt, batch, height, width)

    down = [(i, i + 1) for i in range(sections - 1)]
    up = [(i + 1, i) for i in range(sections - 1)]
    target = jnp.pad(logit_grad, ((0, 0), (0, 0), (0, 0), (0, LANE - classes)))

    def rim(low_rows, target_rows):
        paired = jnp.concatenate([target_rows[:, 0:1], target_rows[:, 1:2]], axis=3)
        return jnp.concatenate([low_rows, paired], axis=1)

    top = lax.ppermute(rim(low_input[:, -HALO:], target[:, -2:]), "section", down)
    end = lax.ppermute(rim(low_input[:, :HALO], target[:, :2]), "section", up)
    distance = jnp.arange(sections, dtype=jnp.int32)
    offsets = (section ^ distance) * coarse_rows

    stats = doubled_sum(moments, "dp")
    tables = row_tables(4 * cuts, low_ids.shape[1], section, fine_rows, height)
    scale = jnp.concatenate([bn_gain, bn_shift], axis=0)
    saved = blank(batch, saved_shapes(fine_rows, fine_cols, chans, red))
    parts = []
    for first, size in groups:
        at = tied(offsets, target, *tables, saved[0]) if parts else offsets
        parts.append(project(first, size, at, br, stats, scale, proj, count, coarse_rows, sections, height, width))
    projs = [exchanged(p, "section") for p in parts]
    projs[0][0] = tied(projs[0][0], *[p[0] for p in parts[1:]])
    pieces = []
    for g, (first, size) in enumerate(groups):
        pgrad, saved = decode(first, size, tables, top, low_input, end, projs[g], target, reduce_weight.T,
                              merge1_weight, merge2_weight, class_weight.T, saved)
        if g + 1 < len(groups):
            pgrad, *projs[g + 1] = lax.optimization_barrier((pgrad, *projs[g + 1]))
        pieces.append(exchanged([pgrad] * sections, "section"))
    backs = []
    projgrad, sums = jnp.zeros(proj.shape, f32), jnp.zeros(stats.shape, f32)
    for (first, size), piece in zip(groups, pieces):
        back, sums, projgrad = norm_back(first, offsets, br, stats, scale, proj, projgrad, sums, piece, count, height, width)
        backs.append(back)
    sums = doubled_sum(sums, "dp")
    filled = (taps + 1) * own
    rows = -(-(filled + projgrad.size // in_chans) // 32) * 32
    grads, tg, pool_grad = aspp_weight_grads(rows, cuts, x, br, stats, scale, sums, projgrad, backs, count, height, width)

    order = list(reversed(range(sections)))
    received = {}

    def input_of(k, tg):
        place = (section ^ k).reshape(1).astype(jnp.int32)
        return aspp_input_grad(place, cuts, tg, wt, pool_grad, pwt, sections, height, width)

    def sent(piece, k):
        return lax.ppermute(piece, "section", [(i, i ^ k) for i in range(sections)]) if k else piece

    share = lax.psum_scatter(grads, "dp", tiled=True)
    early, late = order[:len(order) // 2], order[len(order) // 2:]
    piece = input_of(early[0], tied(tg, grads))
    far = sent(piece, early[0])
    first = tied(saved[0], piece)
    packed, low_grad, logits = decode_grads(0, (first,) + saved[1:], low_input, target, reduce_weight.T, class_weight.T, None)
    swap = [(i, i ^ 1) for i in range(lax.axis_size("dp"))]
    bit = lax.axis_index("dp") % 2
    half = packed.shape[0] // 2
    mine = lax.dynamic_slice_in_dim(packed, bit * half, half, 0)
    packed = added(mine, lax.ppermute(lax.dynamic_slice_in_dim(packed, (1 - bit) * half, half, 0), "dp", swap))
    packed, far, tied_tg = lax.optimization_barrier((packed, far, tg))
    packed = scatter_sum(packed, "section", 1)
    received[early[0]] = far
    for k in early[1:]:
        received[k] = input_of(k, tied_tg)
        packed = tied(packed, received[k])
    held = tuple(received[k] for k in early)
    (share, packed), held = lax.optimization_barrier(((share, packed), held))
    received.update(zip(early, held))

    summed = lax.all_gather(share, "dp", tiled=True)
    for k in early[1:]:
        received[k] = sent(received[k], k)
    steps = [lambda v: scatter_sum(v, "dp", 2), lambda v: gather(v, "dp", 2)[0]]
    for k in late:
        packed, tied_tg = lax.optimization_barrier((packed, tg) + ((piece,) if k != late[0] else ()))[:2]
        piece = input_of(k, tied_tg)
        if steps:
            packed = steps.pop(0)(packed)
        packed, piece = lax.optimization_barrier((packed, piece))
        received[k] = sent(piece, k)
    input_grad = sum(received[k].astype(f32) for k in order).reshape(batch, height, width, in_chans // sections)
    packed, input_grad = gather(packed, "section", 1, input_grad)
    packed, summed = lax.optimization_barrier((packed, summed))
    other = lax.ppermute(packed, "dp", swap)
    merge1_grad, merge2_grad, reduce_grad, class_grad = unpack_decoder(bit.reshape(1).astype(jnp.int32), packed, other, chans, red,
                                                                       classes)

    wide, pool_weight_grad, proj_weight_grad = unpack_weights(summed, taps * own, own, proj.shape)
    sums = jnp.sum(sums.reshape(2, batch, -1), axis=1)
    return (
        jnp.transpose(logits, (0, 2, 3, 1)),
        input_grad,
        low_grad,
        jnp.transpose(wide.reshape(taps, own, in_chans), (2, 0, 1)),
        pool_weight_grad.T,
        sums[0].reshape(branches, own),
        sums[1].reshape(branches, own),
        proj_weight_grad.reshape(branches, own, chans),
        reduce_grad,
        merge1_grad,
        merge2_grad,
        class_grad,
    )


def solution(mesh):
    return jax.shard_map(
        local,
        mesh=mesh,
        in_specs=(
            P("dp", None, None, None), P("dp", "section", None, None), P("dp", None, None), P("dp", None, None),
            P(None, None, "section"), P(None, "section"), P(None, "section"), P(None, "section"), P(None, "section", None),
            P(), P(), P(), P(), P("dp", "section", None, None),
        ),
        out_specs=(
            P("dp", "section", None, None), P("dp", None, None, "section"), P("dp", "section", None, None),
            P(None, None, "section"), P(None, "section"), P(None, "section"), P(None, "section"), P(None, "section", None),
            P(), P(), P(), P(),
        ),
        check_vma=False,
    )
```
